32 devices in a mesh: dp: 8 (over z, x), tensor: 4 (over y, core).
Axes of the slice: x: 2, y: 2, z: 4, core: 2. Of those that a mesh axis runs over, the one named last changes fastest.
Arguments:
- tokens: bfloat16 [15360, 1024], P(('dp', 'tensor')), may hold values from -6 to 6
- token_kinds: int32 [24, 640], P('dp'), may hold values 0 or 1
- segment_ids: int32 [24, 640], P('dp'), may hold values from 0 to 3, never falling along the last dimension, each value on 1 to 320 neighbouring positions
- cotangent: bfloat16 [15360, 1024], P(('dp', 'tensor')), may hold values from -6 to 6
- query_weight: bfloat16 [1, 4, 1024, 1024], P(None, None, None, 'tensor'), may hold values from -0.1875 to 0.1875
- query_bias: bfloat16 [1, 4, 1024], P(None, None, 'tensor'), may hold values from -3 to 3
- key_weight: bfloat16 [1, 1024, 1024], P(None, None, 'tensor'), may hold values from -0.1875 to 0.1875
- key_bias: bfloat16 [1, 1024], P(None, 'tensor'), may hold values from -3 to 3
- value_weight: bfloat16 [1, 1024, 1024], P(None, None, 'tensor'), may hold values from -0.1875 to 0.1875
- value_bias: bfloat16 [1, 1024], P(None, 'tensor'), may hold values from -3 to 3
- output_weight: bfloat16 [1, 1024, 1024], P(None, 'tensor'), may hold values from -1.5 to 1.5
- output_bias: float32 [1, 1024], replicated, may hold values from -2 to 2
- inner_gain: float32 [1, 1024], replicated, may hold values from 0.5 to 1.5
- inner_shift: float32 [1, 1024], replicated, may hold values from -2 to 2
- expand_weight: bfloat16 [1, 1024, 4096], P(None, None, 'tensor'), may hold values from -0.1875 to 0.1875
- expand_bias: bfloat16 [1, 4096], P(None, 'tensor'), may hold values from -3 to 3
- contract_weight: bfloat16 [1, 4096, 1024], P(None, 'tensor'), may hold values from -0.09375 to 0.09375
- contract_bias: float32 [1, 1024], replicated, may hold values from -2 to 2
- outer_gain: float32 [1, 1024], replicated, may hold values from 0.5 to 1.5
- outer_shift: float32 [1, 1024], replicated, may hold values from -2 to 2
Outputs:
- result: float32 [15360, 1024], P(('dp', 'tensor'))
- tokens_gradient: float32 [15360, 1024], P(('dp', 'tensor'))
- query_weight_gradient: float32 [1, 4, 1024, 1024], P(None, None, None, 'tensor')
- query_bias_gradient: float32 [1, 4, 1024], P(None, None, 'tensor')
- key_weight_gradient: float32 [1, 1024, 1024], P(None, None, 'tensor')
- key_bias_gradient: float32 [1, 1024], P(None, 'tensor')
- value_weight_gradient: float32 [1, 1024, 1024], P(None, None, 'tensor')
- value_bias_gradient: float32 [1, 1024], P(None, 'tensor')
- output_weight_gradient: float32 [1, 1024, 1024], P(None, 'tensor')
- output_bias_gradient: float32 [1, 1024], replicated
- inner_gain_gradient: float32 [1, 1024], replicated
- inner_shift_gradient: float32 [1, 1024], replicated
- expand_weight_gradient: float32 [1, 1024, 4096], P(None, None, 'tensor')
- expand_bias_gradient: float32 [1, 4096], P(None, 'tensor')
- contract_weight_gradient: float32 [1, 4096, 1024], P(None, 'tensor')
- contract_bias_gradient: float32 [1, 1024], replicated
- outer_gain_gradient: float32 [1, 1024], replicated
- outer_shift_gradient: float32 [1, 1024], replicated
The draws below stay inside these ranges and needn't reach their ends.
Inputs may be any that keep to these rules, and one draw needn't show every extreme that they name: `segment_ids`: document numbers never fall along a sequence; each sequence holds all 4 documents.
All inputs are finite; a program needn't handle non-finite values. No bound on the sum of `token_kinds` on one device may be relied on, other than what follows from the above.
Results may differ from the reference program's by a relative error of at most 0.02.
Values may be sent and summed in bfloat16 or wider, within the bound.
No kernel may reach another device: no remote copies, remote signals or barrier semaphores. Data moves between devices by JAX's collectives and lax.ppermute only.
A program may use at most 128 MiB of HBM per device.

```python
import math
import jax
import jax.numpy as jnp
import numpy as np
from jax import lax

D = 1024
H = 16
HD = 64
FF = 4096
LAYERS = 1
LEN = 640
DOCS = 4
SEQS = 24
TOKENS = 15360


def place_ends(drawn, rng, smallest, high):
    longest = drawn.shape.index(max(drawn.shape))
    spots = []
    for shift in (0, 1):
        where = [jax.random.randint(jax.random.fold_in(rng, axis), (), 0, length) for axis, length in enumerate(drawn.shape)]
        where[longest] = (where[longest] + shift) % drawn.shape[longest]
        spots.append(tuple(where))
    return drawn.at[spots[0]].set(smallest).at[spots[1]].set(high)


def shard_levels(key, dims, shards, smallest, largest):
    factor_of = 1.0
    for axis_at, shards_of in shards:
        heights = jax.random.uniform(jax.random.fold_in(jax.random.fold_in(key, 6), axis_at), (shards_of,), jnp.float32, smallest / len(shards), largest / len(shards))
        factor_of = factor_of * jnp.repeat(jnp.exp(heights), dims[axis_at] // shards_of).reshape((-1,) + (1,) * (len(dims) - 1 - axis_at))
    return factor_of


def length_profile(number_of, total, most, skew):
    portions = [(1 << 20) // math.isqrt(standing ** skew) + 1 for standing in range(2, number_of + 1)]
    rest, holding = total - most - (number_of - 1), [1] * (number_of - 1)
    while rest > 0:
        movable = [i for i in range(number_of - 1) if holding[i] < most]
        whole, left = sum([portions[i] for i in movable]), rest
        for i in movable:
            more = min(most - holding[i], max(1, left * portions[i] // whole), rest)
            holding[i] = holding[i] + more
            rest = rest - more
    return np.array([most] + holding)


def ragged(key, amount, total, reach, lean):
    if amount == 2:
        one = jax.random.randint(key, (), max(1, total - reach), min(reach, total - 1) + 1)
        return jnp.stack([one, total - one])
    tallies = jnp.asarray(length_profile(amount, total, reach, lean), jnp.int32)
    twos = (amount - 1) // 2
    source_of, sink = tallies[1:1 + 2 * twos:2], tallies[2:2 + 2 * twos:2]
    slack = jnp.minimum(source_of - 1, reach - sink)
    moved = jax.random.randint(jax.random.fold_in(key, 1), (twos,), 0, 1 << 20) % (slack + 1)
    tallies = tallies.at[1:1 + 2 * twos:2].set(source_of - moved).at[2:2 + 2 * twos:2].set(sink + moved)
    return tallies[jax.random.permutation(jax.random.fold_in(key, 2), amount)]


def normal_values(key, dims, deviation, bound, shards=(), kind=jnp.bfloat16):
    loudness = shard_levels(key, dims, shards, -0.22, 0.18) if shards else 1.0
    drawn = jax.random.normal(key, dims, jnp.float32) * deviation * loudness
    return jnp.minimum(jnp.maximum(drawn, -bound), bound).astype(kind)


def setup_inputs(seed: int = 0) -> dict:
    arg_keys = jax.random.split(jax.random.key(seed), 21)
    return {
        "tokens": normal_values(arg_keys[0], (TOKENS, D), 1.0, 6.0, ((0, 32),)),
        "token_kinds": place_ends((jax.random.randint(arg_keys[1], (SEQS, LEN), 0, 5) < 1).astype(jnp.int32), jax.random.fold_in(arg_keys[1], 1), 0, 1),
        "segment_ids": jax.vmap(lambda own: jnp.searchsorted(jnp.cumsum(ragged(own, DOCS, LEN, LEN // 2, 0)), jnp.arange(LEN), side="right"))(jax.random.split(arg_keys[2], SEQS)).reshape((SEQS, LEN)).astype(jnp.int32),
        "cotangent": normal_values(arg_keys[3], (TOKENS, D), 1.0, 6.0, ((0, 32),)),
        "query_weight": normal_values(arg_keys[4], (LAYERS, 4, D, D), D ** -0.5, 0.1875, ((3, 4),)),
        "query_bias": normal_values(arg_keys[5], (LAYERS, 4, D), 0.5, 3.0, ((2, 4),)),
        "key_weight": normal_values(arg_keys[6], (LAYERS, D, D), D ** -0.5, 0.1875, ((2, 4),)),
        "key_bias": normal_values(arg_keys[7], (LAYERS, D), 0.5, 3.0, ((1, 4),)),
        "value_weight": normal_values(arg_keys[8], (LAYERS, D, D), D ** -0.5, 0.1875, ((2, 4),)),
        "value_bias": normal_values(arg_keys[9], (LAYERS, D), 0.5, 3.0, ((1, 4),)),
        "output_weight": normal_values(arg_keys[10], (LAYERS, D, D), (D // 64) ** -0.5, 1.5, ((1, 4),)),
        "output_bias": normal_values(arg_keys[11], (LAYERS, D), 0.3, 2.0, (), jnp.float32),
        "inner_gain": jnp.clip(1.0 + 0.1 * jax.random.normal(arg_keys[12], (LAYERS, D), jnp.float32), 0.5, 1.5),
        "inner_shift": normal_values(arg_keys[13], (LAYERS, D), 0.3, 2.0, (), jnp.float32),
        "expand_weight": normal_values(arg_keys[14], (LAYERS, D, FF), D ** -0.5, 0.1875, ((2, 4),)),
        "expand_bias": normal_values(arg_keys[15], (LAYERS, FF), 0.5, 3.0, ((1, 4),)),
        "contract_weight": normal_values(arg_keys[16], (LAYERS, FF, D), FF ** -0.5, 0.09375, ((1, 4),)),
        "contract_bias": normal_values(arg_keys[17], (LAYERS, D), 0.3, 2.0, (), jnp.float32),
        "outer_gain": jnp.clip(1.0 + 0.1 * jax.random.normal(arg_keys[18], (LAYERS, D), jnp.float32), 0.5, 1.5),
        "outer_shift": normal_values(arg_keys[19], (LAYERS, D), 0.3, 2.0, (), jnp.float32),
    }


@jax.custom_vjp
def low(v):
    return lax.optimization_barrier(v.astype(jnp.bfloat16)).astype(jnp.float32)

@jax.custom_vjp
def low_back(v):
    return v

def low_keep(v):
    return (low(v), None)

def low_pass(kept, grad):
    return (grad,)

def back_keep(v):
    return (v, None)

def back_low(kept, grad):
    return (low(grad),)
low.defvjp(low_keep, low_pass)
low_back.defvjp(back_keep, back_low)
NORM_EPS = 1e-05
MASKED = -1e+30
HIGHEST = lax.Precision.HIGHEST

def both_round(values):
    return low_back(low(values))

def dense(left_side, right_side):
    return jnp.dot(left_side, right_side, precision=HIGHEST, preferred_element_type=jnp.float32)

def norm_rows(values, norm_gain, norm_shift):
    centre = lax.optimization_barrier(jnp.mean(values, axis=-1, keepdims=True))
    offset = values - centre
    spread = lax.optimization_barrier(jnp.mean(offset * offset, axis=-1, keepdims=True))
    return offset * lax.rsqrt(spread + NORM_EPS) * norm_gain + norm_shift

def attend_one(inputs):
    query_word, query_entity, keys_seq, values_seq, kinds_row, segments_row = inputs
    length = keys_seq.shape[0]
    word_heads = query_word.reshape(length, H, HD)
    entity_heads = query_entity.reshape(length, H, HD)
    key_heads = keys_seq.reshape(length, H, HD)
    value_heads = values_seq.reshape(length, H, HD)
    to_word = jnp.einsum('qhd,khd->hqk', word_heads, key_heads, precision=HIGHEST)
    to_entity = jnp.einsum('qhd,khd->hqk', entity_heads, key_heads, precision=HIGHEST)
    key_is_word = (kinds_row == 0)[None, None, :]
    raw_scores = low_back(jnp.where(key_is_word, to_word, to_entity) * HD ** (-0.5))
    same_doc = (segments_row[:, None] == segments_row[None, :])[None]
    soft_weights = low(jax.nn.softmax(jnp.where(same_doc, raw_scores, MASKED), axis=-1))
    mixed_heads = jnp.einsum('hqk,khd->qhd', soft_weights, value_heads, precision=HIGHEST)
    return mixed_heads.reshape(length, H * HD)

def block_forward(start, token_kinds, segment_ids, query_weight, query_bias, key_weight, key_bias, value_weight, value_bias, output_weight, output_bias, inner_gain, inner_shift, expand_weight, expand_bias, contract_weight, contract_bias, outer_gain, outer_shift):
    hidden = start
    word_rows = (token_kinds.reshape(-1) == 0)[:, None]
    for layer_index in range(LAYERS):
        rounded_in = low(hidden)
        query_all = jnp.einsum('td,sde->ste', rounded_in, query_weight[layer_index], precision=HIGHEST)
        query_all = query_all + query_bias[layer_index][:, None, :]
        query_word = both_round(jnp.where(word_rows, query_all[0], query_all[2]))
        query_entity = both_round(jnp.where(word_rows, query_all[1], query_all[3]))
        keys_all = both_round(dense(rounded_in, key_weight[layer_index]) + key_bias[layer_index])
        values_all = both_round(dense(rounded_in, value_weight[layer_index]) + value_bias[layer_index])
        context = lax.map(jax.checkpoint(attend_one), (query_word.reshape(SEQS, LEN, D), query_entity.reshape(SEQS, LEN, D), keys_all.reshape(SEQS, LEN, D), values_all.reshape(SEQS, LEN, D), token_kinds, segment_ids))
        context = both_round(context.reshape(TOKENS, D))
        inner_sum = low_back(dense(context, output_weight[layer_index])) + output_bias[layer_index] + hidden
        inner_out = norm_rows(inner_sum, inner_gain[layer_index], inner_shift[layer_index])
        rounded_mid = low(inner_out)
        expanded = low_back(dense(rounded_mid, expand_weight[layer_index]) + expand_bias[layer_index])
        activated = low(jax.nn.gelu(expanded, approximate=False))
        outer_sum = low_back(dense(activated, contract_weight[layer_index])) + contract_bias[layer_index] + inner_out
        hidden = norm_rows(outer_sum, outer_gain[layer_index], outer_shift[layer_index])
    return hidden

def reference(tokens, token_kinds, segment_ids, cotangent, query_weight, query_bias, key_weight, key_bias, value_weight, value_bias, output_weight, output_bias, inner_gain, inner_shift, expand_weight, expand_bias, contract_weight, contract_bias, outer_gain, outer_shift):
    params = (query_weight, query_bias, key_weight, key_bias, value_weight, value_bias, output_weight, output_bias, inner_gain, inner_shift, expand_weight, expand_bias, contract_weight, contract_bias, outer_gain, outer_shift)
    params = tuple((item.astype(jnp.float32) for item in params))

    def wrapped(start, *weights):
        return block_forward(start, token_kinds, segment_ids, *weights)
    result, pullback = jax.vjp(wrapped, tokens.astype(jnp.float32), *params)
    grads = pullback(cotangent.astype(jnp.float32))
    return (result, grads[0], grads[1], grads[2], grads[3], grads[4], grads[5], grads[6], grads[7], grads[8], grads[9], grads[10], grads[11], grads[12], grads[13], grads[14], grads[15], grads[16])
```

```python
import functools

import jax
import jax.numpy as jnp
import numpy as np
from jax import lax
from jax.experimental import pallas as pl
from jax.experimental.pallas import tpu as pltpu
from jax.sharding import PartitionSpec as P

HD = 64
NORM_EPS = 1e-05
MASKED = -1e30
F32 = jnp.float32
BF16 = jnp.bfloat16
VMEM_LIMIT = 48 * 1024 * 1024


def nn(a, b):
    return lax.dot_general(a, b, (((1,), (0,)), ((), ())), preferred_element_type=F32)


def nt(a, b):
    return lax.dot_general(a, b, (((1,), (1,)), ((), ())), preferred_element_type=F32)


def tn(a, b):
    return lax.dot_general(a, b, (((0,), (0,)), ((), ())), preferred_element_type=F32)


def call(body, name, *, grid=(1,), prefetch=(), ins, outs, aliases=None, scratch=(), flops=0, moved=0):
    def spec(block, index_map):
        if block is None:
            return pl.BlockSpec(memory_space=pl.ANY)
        return pl.BlockSpec(block, index_map)

    in_specs = [spec(block, index_map) for _, block, index_map in ins]
    out_specs = [spec(block, index_map) for _, _, block, index_map in outs]
    shift = len(prefetch)
    return pl.pallas_call(
        body,
        grid_spec=pltpu.PrefetchScalarGridSpec(
            num_scalar_prefetch=shift,
            grid=grid,
            in_specs=in_specs,
            out_specs=out_specs,
            scratch_shapes=list(scratch),
        ),
        out_shape=[jax.ShapeDtypeStruct(shape, dtype) for shape, dtype, _, _ in outs],
        input_output_aliases={shift + k: v for k, v in (aliases or {}).items()},
        compiler_params=pltpu.CompilerParams(vmem_limit_bytes=VMEM_LIMIT),
        cost_estimate=pl.CostEstimate(flops=flops, bytes_accessed=moved, transcendentals=0),
        name=name,
    )(*prefetch, *[array for array, _, _ in ins])


def whole(array):
    zeros = (0,) * array.ndim
    return (array, array.shape, lambda *_: zeros)


def out_whole(shape, dtype):
    zeros = (0,) * len(shape)
    return (shape, dtype, shape, lambda *_: zeros)


def swap(array, axis, size, bit):
    return lax.ppermute(array, axis, [(r, r ^ bit) for r in range(size)])


def gather_blocks(own, size):
    blocks = {0: own}
    bit = 2
    while bit < size:
        for j in sorted(blocks):
            blocks[j | bit] = swap(blocks[j], "tensor", size, bit)
        bit *= 2
    for j in sorted(blocks):
        blocks[j | 1] = swap(blocks[j], "tensor", size, 1)
    return [blocks[j] for j in range(size)]


def scatter_sum(send, keeps, size):
    received = swap(send, "tensor", size, 1)
    addends = [keeps[0][None], received]
    held = {
        2 * m: (keeps[m].astype(F32) + received[m].astype(F32)).astype(BF16)
        for m in range(1, len(keeps))
    }
    bit = size // 2
    while bit >= 2:
        leaving = sorted(j for j in held if j & bit)
        arrived = swap(jnp.stack([held[j] for j in leaving]), "tensor", size, bit)
        addends.append(arrived)
        for m, j in enumerate(leaving):
            if j ^ bit:
                rest = j ^ bit
                held[rest] = (held[rest].astype(F32) + arrived[m].astype(F32)).astype(BF16)
            del held[j]
        bit //= 2
    return addends


def addend_specs(addends):
    return [(a, (1,) + a.shape[1:], lambda *_: (0, 0, 0)) for a in addends]


def place(state, shapes, piece, layout, name):
    array, places = piece
    count = places.shape[0]
    rows = array.shape[0] // count

    def body(places_ref, in_ref, *refs):
        out_refs = refs[-len(layout) :]
        for (_, _, leads, start, wide), out_ref in zip(layout, out_refs, strict=True):
            for lead in range(leads):
                at = start + lead * wide
                out_ref[lead] = in_ref[:, at : at + wide].astype(F32)

    ins = [(array, (rows, array.shape[1]), lambda m, spots: (m, 0))]
    outs, aliases = [], {}
    for number, (out, first, leads, _, wide) in enumerate(layout):
        index_map = functools.partial(lambda lead, m, spots: (lead, spots[m], 0), first // leads)
        outs.append((shapes[out], F32, (leads, rows, wide), index_map))
        if out in state:
            aliases[len(ins)] = number
            ins.append((state[out], None, None))
    got = call(
        body, name, grid=(count,), prefetch=(places,), ins=ins, outs=outs, aliases=aliases, moved=array.size * 6
    )
    return {**state, **{entry[0]: value for entry, value in zip(layout, got, strict=True)}}


def sum_over_dp(array, order, size):
    if array.shape[0] % (16 * size):
        return [(lax.psum(array, "dp"), jnp.zeros((1,), jnp.int32))]
    here = lax.axis_index("dp")
    bits = len(order)
    mine = [(here >> bit) & 1 for bit in order]
    current = array
    for bit, own in zip(order, mine, strict=True):
        half = current.shape[0] // 2
        leaving = lax.dynamic_slice_in_dim(current, (1 - own) * half, half, 0)
        staying = lax.dynamic_slice_in_dim(current, own * half, half, 0)
        arrived = swap(leaving, "dp", size, 1 << bit)
        current = (staying.astype(F32) + arrived.astype(F32)).astype(BF16)

    def where(differs):
        spot = 0
        for level in range(bits):
            spot = spot * 2 + (mine[level] ^ ((differs >> level) & 1))
        return spot

    held = [0]
    pieces = [(current, jnp.stack([where(0)]).astype(jnp.int32))]
    for level in reversed(range(bits)):
        arrived = swap(current, "dp", size, 1 << order[level])
        came = [differs | (1 << level) for differs in held]
        pieces.append((arrived, jnp.stack([where(d) for d in came]).astype(jnp.int32)))
        held = held + came
        if level:
            current = jnp.concatenate([current, arrived], axis=0)
    return pieces


def doubling_sum(array, axis, size):
    bit = 1
    while bit < size:
        array = array + swap(array, axis, size, bit)
        bit *= 2
    return array


def piece_rounds(count, size):
    left = {}
    for g in range(count * size):
        left.setdefault((g // count, g % size), []).append(g)
    rounds = []
    for _ in range(count):
        match = {}

        def augment(u, seen):
            for v in range(size):
                if left.get((u, v)) and v not in seen:
                    seen.add(v)
                    if v not in match or augment(match[v], seen):
                        match[v] = u
                        return True
            return False

        for bit in range(size):
            if all(left.get((u, u ^ bit)) for u in range(size)):
                match.update({u ^ bit: u for u in range(size)})
                break
        else:
            for u in range(size):
                augment(u, set())
        chosen = {u: (v, left[(u, v)].pop(0)) for v, u in match.items()}
        rounds.append([chosen[u] for u in range(size)])
    return rounds


def erf_parts(u):
    size = jnp.abs(u) * np.float32(0.7071067811865476)
    bell = jnp.exp(-(size * size))
    t = pl.reciprocal(1.0 + np.float32(0.3275911) * size)
    poly = np.float32(1.061405429 * 0.5)
    for c in (-1.453152027, 1.421413741, -0.284496736, 0.254829592):
        poly = poly * t + np.float32(c * 0.5)
    tail = poly * t * bell
    return jnp.where(u < 0, tail, 1.0 - tail), bell * np.float32(0.3989422804014327)


def write_rows(values, send_ref, keep_refs, size, rows):
    for j in range(size):
        block = values[j * rows : (j + 1) * rows].astype(BF16)
        if j & 1:
            send_ref[j // 2] = block
        else:
            keep_refs[j // 2][...] = block


def partial_outs(size, rows, width):
    outs = [out_whole((size // 2, rows, width), BF16)]
    return outs + [out_whole((rows, width), BF16) for _ in range(size // 2)]


def project_rows(blocks, kinds_col, weights, biases, buffers, k, count):
    size = len(blocks)
    rows, d = blocks[0].shape
    width = weights[1].shape[1]

    def body(*refs):
        x_refs = refs[:size]
        kind_ref, qw_ref, kw_ref, vw_ref, b_ref = refs[size : size + 5]
        out_ref, x_out = refs[-2:]
        x = jnp.concatenate([r[...] for r in x_refs], axis=0)
        for j in range(size):
            x_out[j] = x_refs[j][...]
        word = jnp.broadcast_to(kind_ref[0], (size * rows, width)) == 0
        bias = [b_ref[m : m + 1, :] for m in range(6)]
        for part, (first, second) in enumerate(((0, 2), (1, 3))):
            one = nn(x, qw_ref[first]) + bias[first]
            two = nn(x, qw_ref[second]) + bias[second]
            both = jnp.where(word, one, two).astype(BF16)
            for j in range(size):
                out_ref[j, :, part * width : (part + 1) * width] = both[j * rows : (j + 1) * rows]
        for part, ref, m in ((2, kw_ref, 4), (3, vw_ref, 5)):
            both = (nn(x, ref[...]) + bias[m]).astype(BF16)
            for j in range(size):
                out_ref[j, :, part * width : (part + 1) * width] = both[j * rows : (j + 1) * rows]

    ins = [whole(b) for b in blocks]
    ins.append((kinds_col, (1,) + kinds_col.shape[1:], lambda *_: (k, 0, 0)))
    ins += [whole(w) for w in weights] + [whole(biases)]
    aliases = {}
    if buffers is not None:
        for number, b in enumerate(buffers):
            aliases[len(ins)] = number
            ins.append((b, None, None))
    outs = [
        ((count * size, rows, 4 * width), BF16, (size, rows, 4 * width), lambda *_: (k, 0, 0)),
        ((count * size, rows, d), BF16, (size, rows, d), lambda *_: (k, 0, 0)),
    ]
    return call(
        body, "project_rows", ins=ins, outs=outs, aliases=aliases,
        flops=2 * size * rows * d * 6 * width, moved=size * rows * d * 6 + 12 * d * width,
    )


def head_views(piece_refs, part, pair, width):
    start = part * width + pair * 128
    return jnp.concatenate([r[0, :, start : start + 128] for r in piece_refs], axis=0)


def swap_lanes(values):
    return pltpu.roll(values.astype(F32), 64, 1)


def extended(piece_refs, pair, width, kind, left):
    qw = head_views(piece_refs, 0, pair, width)
    qe = head_views(piece_refs, 1, pair, width)
    k = head_views(piece_refs, 2, pair, width)
    v = head_views(piece_refs, 3, pair, width)
    qw32, qe32, k32 = qw.astype(F32), qe.astype(F32), k.astype(F32) * 0.125
    qw_s, qe_s, k_s = swap_lanes(qw32), swap_lanes(qe32), swap_lanes(k32)
    q_ext = (
        jnp.where(left, qw32, qe_s).astype(BF16),
        jnp.where(left, qw_s, qe32).astype(BF16),
    )
    takes = (kind + left.astype(jnp.int32)) == 1
    k_ext = (
        jnp.where(takes, jnp.where(left, k32, k_s), 0.0).astype(BF16),
        jnp.where(takes, jnp.where(left, k_s, k32), 0.0).astype(BF16),
    )
    return q_ext, k_ext, v


def query_blocks(length):
    spans, at = [], 0
    while at < length:
        step = 256 if length - at >= 256 else length - at
        spans.append((at, step))
        at += step
    return spans


def attend(pieces, table, s, seg_col, seg_row, kind_col, out_proj, size, rows):
    length = size * rows
    width, d = out_proj.shape
    pairs = width // 128

    def body(table_ref, *refs):
        piece_refs = refs[:size]
        segc_ref, segr_ref, kind_ref, wo_ref, c_ref, lse_ref, send_ref = refs[size : size + 7]
        keep_refs = refs[size + 7 :]
        left = lax.broadcasted_iota(jnp.int32, (length, 128), 1) < 64
        kind = jnp.broadcast_to(kind_ref[0], (length, 128))
        segc, segr = segc_ref[0], segr_ref[0]
        for pair in range(pairs):
            q_ext, k_ext, v = extended(piece_refs, pair, width, kind, left)
            v_t = v.astype(F32).T.astype(BF16)
            for at, step in query_blocks(length):
                same = segc == segr[:, at : at + step]
                tops = []
                for h in range(2):
                    s_t = nt(k_ext[h], q_ext[h][at : at + step])
                    s_t = jnp.where(same, s_t, MASKED)
                    top = jnp.max(s_t, axis=0, keepdims=True)
                    e = jnp.exp(s_t - top)
                    total = jnp.sum(e, axis=0, keepdims=True)
                    o_t = nn(v_t[h * 64 : h * 64 + 64], e.astype(BF16))
                    tops.append(o_t * (1.0 / total))
                    lse_ref[2 * pair + h : 2 * pair + h + 1, at : at + step] = top + jnp.log(total)
                c = jnp.concatenate(tops, axis=0).T.astype(BF16)
                c_ref[at : at + step, pair * 128 : pair * 128 + 128] = c
        write_rows(nn(c_ref[...], wo_ref[...]), send_ref, keep_refs, size, rows)

    ins = [
        (pieces, (1, rows, 4 * width), functools.partial(lambda j, _, t: (t[s * size + j], 0, 0), j))
        for j in range(size)
    ]
    ins += [
        (seg_col, (1, length, 1), lambda *_: (s, 0, 0)),
        (seg_row, (1, 1, length), lambda *_: (s, 0, 0)),
        (kind_col, (1, length, 1), lambda *_: (s, 0, 0)),
        whole(out_proj),
    ]
    outs = [out_whole((length, width), BF16), out_whole((8, length), F32)]
    outs += partial_outs(size, rows, d)
    return call(
        body, "attend", prefetch=(table,), ins=ins, outs=outs,
        flops=pairs * 2 * length * length * 1024 + 2 * length * width * d, moved=length * (5 * width + d) * 2,
    )


def attend_back(pieces, table, s, seg_col, seg_row, kind_col, out_proj, context, lse, delta_blocks, buffers, sums, count):
    size = len(delta_blocks)
    rows, d = delta_blocks[0].shape
    length = size * rows
    width = out_proj.shape[0]
    pairs = width // 128

    def body(table_ref, *refs):
        piece_refs = refs[:size]
        delta_refs = refs[size : 2 * size]
        segc_ref, segr_ref, kind_ref, wo_ref, c_ref, lse_ref = refs[2 * size : 2 * size + 6]
        n_out = 5
        tail = refs[2 * size + 6 :]
        sum_in = tail[0] if sums is not None else None
        first_out, second_out, delta_out, wo_grad, bias_out, first_all, second_all = tail[-(n_out + 2) :]
        step_at = pl.program_id(0)

        @pl.when(step_at == 0)
        def _():
            left = lax.broadcasted_iota(jnp.int32, (length, 128), 1) < 64
            kind = jnp.broadcast_to(kind_ref[0], (length, 128))
            word = kind == 0
            straight = (kind + left.astype(jnp.int32)) == 1
            segc, segr = segc_ref[0], segr_ref[0]
            delta = jnp.concatenate([r[...] for r in delta_refs], axis=0)
            c_all = c_ref[...]
            grad = nn(c_all.astype(F32).T.astype(BF16), delta)
            wo_grad[...] = grad if sum_in is None else grad + sum_in[...]
            for pair in range(pairs):
                dc = nt(delta, wo_ref[pair * 128 : pair * 128 + 128, :]).astype(BF16)
                q_ext, k_ext, v = extended(piece_refs, pair, width, kind, left)
                k_ext_t = [k.astype(F32).T.astype(BF16) for k in k_ext]
                dc32 = dc.astype(F32)
                inner = (dc32 * c_all[:, pair * 128 : pair * 128 + 128].astype(F32)).T
                dc_h = (jnp.where(left, dc32, 0.0).astype(BF16), jnp.where(left, 0.0, dc32).astype(BF16))
                dv = jnp.zeros((length, 128), F32)
                dk = [jnp.zeros((length, 128), F32)] * 2
                dq = [[], []]
                for at, step in query_blocks(length):
                    same = segc == segr[:, at : at + step]
                    for h in range(2):
                        q_b, dc_b = q_ext[h][at : at + step], dc_h[h][at : at + step]
                        row = 2 * pair + h
                        s_t = nt(k_ext[h], q_b)
                        p = jnp.where(same, jnp.exp(s_t - lse_ref[row : row + 1, at : at + step]), 0.0)
                        dp = nt(v, dc_b)
                        row_inner = jnp.sum(inner[h * 64 : h * 64 + 64, at : at + step], axis=0, keepdims=True)
                        ds = (p * (dp - row_inner)).astype(BF16)
                        dv = dv + nn(p.astype(BF16), dc_b)
                        dk[h] = dk[h] + nn(ds, q_b)
                        dq[h].append(nn(k_ext_t[h], ds).T)
                dq0, dq1 = (jnp.concatenate(parts, axis=0) for parts in dq)
                dqw = jnp.where(left, dq0, swap_lanes(dq1))
                dqe = jnp.where(left, swap_lanes(dq0), dq1)
                dk0, dk1 = dk[0] * 0.125, dk[1] * 0.125
                dk_pair = jnp.where(straight, jnp.where(left, dk0, dk1), jnp.where(left, swap_lanes(dk0), swap_lanes(dk1)))
                outs = (
                    jnp.where(word, dqw, 0.0), jnp.where(word, dqe, 0.0), jnp.where(word, 0.0, dqw),
                    jnp.where(word, 0.0, dqe), dk_pair, dv,
                )
                for number, values in enumerate(outs):
                    rounded = values.astype(BF16)
                    target = (first_all, second_all)[number // 3]
                    start = (number % 3) * width + pair * 128
                    target[:, start : start + 128] = rounded
                    bias_out[number : number + 1, pair * 128 : pair * 128 + 128] = jnp.sum(
                        rounded.astype(F32), axis=0, keepdims=True
                    )

        at_rows = pl.ds(pl.multiple_of(step_at * rows, 16), rows)
        first_out[0] = first_all[at_rows, :]
        second_out[0] = second_all[at_rows, :]
        for j in range(size):

            @pl.when(step_at == j)
            def _():
                delta_out[0] = delta_refs[j][...]

    ins = [
        (pieces, (1, rows, 4 * width), functools.partial(lambda j, _, t: (t[s * size + j], 0, 0), j))
        for j in range(size)
    ]
    ins += [whole(b) for b in delta_blocks]
    ins += [
        (seg_col, (1, length, 1), lambda *_: (s, 0, 0)),
        (seg_row, (1, 1, length), lambda *_: (s, 0, 0)),
        (kind_col, (1, length, 1), lambda *_: (s, 0, 0)),
        whole(out_proj),
        whole(context),
        whole(lse),
    ]
    if sums is not None:
        ins.append(whole(sums))
    aliases = {}
    if buffers is not None:
        for number, b in enumerate(buffers):
            aliases[len(ins)] = number
            ins.append((b, None, None))
    spot = lambda m, t: (t[s * size + m], 0, 0)
    outs = [
        ((count * size, rows, 3 * width), BF16, (1, rows, 3 * width), spot),
        ((count * size, rows, 3 * width), BF16, (1, rows, 3 * width), spot),
        ((count * size, rows, d), BF16, (1, rows, d), spot),
        out_whole((width, d), F32),
        out_whole((8, width), F32),
    ]
    return call(
        body, "attend_back", grid=(size,), prefetch=(table,), ins=ins, outs=outs, aliases=aliases,
        scratch=[pltpu.VMEM((length, 3 * width), BF16)] * 2,
        flops=pairs * 2 * length * length * 128 * 10 + 4 * length * width * d, moved=length * (11 * width + 2 * d) * 2,
    )


def add_up(refs):
    total = refs[0][0].astype(F32)
    for r in refs[1:]:
        total = total + r[0].astype(F32)
    return total


def normed(values):
    centre = jnp.mean(values, axis=-1, keepdims=True)
    offset = values - centre
    spread = jnp.mean(offset * offset, axis=-1, keepdims=True)
    rstd = lax.rsqrt(spread + NORM_EPS)
    return offset * rstd, rstd


def norm_pull(upstream, n, rstd, gain):
    scaled = upstream * gain
    inner = jnp.mean(scaled, axis=-1, keepdims=True)
    cross = jnp.mean(scaled * n, axis=-1, keepdims=True)
    return rstd * (scaled - inner - n * cross)


def column_sum(values):
    return jnp.sum(values, axis=0, keepdims=True)


def inner_norm(addends, x_pieces, table, s, bias, gain, shift, size):
    rows, d = addends[0].shape[1:]
    n_add = len(addends)

    def body(table_ref, *refs):
        x_ref, b_ref, g_ref, h_ref, y_ref, n_ref, rstd_ref = refs[n_add:]
        r = add_up(refs[:n_add]) + b_ref[...] + x_ref[0].astype(F32)
        n, rstd = normed(r)
        n_ref[...] = n
        rstd_ref[...] = jnp.broadcast_to(rstd, (rows, 128))
        y_ref[...] = (n * g_ref[...] + h_ref[...]).astype(BF16)

    ins = addend_specs(addends)
    ins.append((x_pieces, (1, rows, d), lambda _, t: (t[s * size], 0, 0)))
    ins += [whole(bias), whole(gain), whole(shift)]
    outs = [out_whole((rows, d), BF16), out_whole((rows, d), F32), out_whole((rows, 128), F32)]
    return call(body, "inner_norm", prefetch=(table,), ins=ins, outs=outs, flops=rows * d * 10, moved=rows * d * 14)


def outer_norm(addends, n1, inner_gain, inner_shift, bias, gain, shift, cotangents, spots, buffer, s, count):
    rows, d = addends[0].shape[1:]
    n_add = len(addends)

    def body(spots_ref, *refs):
        n1_ref, g1_ref, h1_ref, b_ref, g_ref, h_ref, e_ref = refs[n_add : n_add + 7]
        res_ref, dz_ref, dzb_ref, sums_ref = refs[-4:]
        z = add_up(refs[:n_add]) + b_ref[...] + (n1_ref[...] * g1_ref[...] + h1_ref[...])
        n, rstd = normed(z)
        res_ref[0] = n * g_ref[...] + h_ref[...]
        e = e_ref[0].astype(F32)
        dz = norm_pull(e, n, rstd, g_ref[...])
        dz_ref[...] = dz
        dzb_ref[...] = dz.astype(BF16)
        sums_ref[0:1] = column_sum(dz)
        sums_ref[1:2] = column_sum(e * n)
        sums_ref[2:3] = column_sum(e)

    ins = addend_specs(addends)
    ins += [whole(a) for a in (n1, inner_gain, inner_shift, bias, gain, shift)]
    ins.append((cotangents, (1, rows, d), lambda _, t: (t[s], 0, 0)))
    aliases = {}
    if buffer is not None:
        aliases[len(ins)] = 0
        ins.append((buffer, None, None))
    outs = [
        ((count, rows, d), F32, (1, rows, d), lambda *_: (s, 0, 0)),
        out_whole((rows, d), F32),
        out_whole((rows, d), BF16),
        out_whole((8, d), F32),
    ]
    return call(
        body, "outer_norm", prefetch=(spots,), ins=ins, outs=outs, aliases=aliases,
        flops=rows * d * 20, moved=rows * d * 22,
    )


def inner_norm_back(addends, dz, n1, rstd1, gain):
    rows, d = addends[0].shape[1:]
    n_add = len(addends)

    def body(*refs):
        dz_ref, n_ref, rstd_ref, g_ref, dr_ref, sums_ref = refs[n_add:]
        da = add_up(refs[:n_add]) + dz_ref[...]
        n = n_ref[...]
        dr = norm_pull(da, n, rstd_ref[:, 0:1], g_ref[...])
        dr_ref[...] = dr.astype(BF16)
        sums_ref[0:1] = column_sum(dr)
        sums_ref[1:2] = column_sum(da * n)
        sums_ref[2:3] = column_sum(da)

    ins = addend_specs(addends) + [whole(a) for a in (dz, n1, rstd1, gain)]
    outs = [out_whole((rows, d), BF16), out_whole((8, d), F32)]
    return call(body, "inner_norm_back", ins=ins, outs=outs, flops=rows * d * 20, moved=rows * d * 18)


def feed_forward(blocks, expand, expand_bias, contract, buffers, s, count):
    size = len(blocks)
    rows, d = blocks[0].shape
    hidden = expand.shape[1]
    length = size * rows
    tile = min(256, hidden)

    def body(*refs):
        y_refs = refs[:size]
        we_ref, be_ref, wc_ref = refs[size : size + 3]
        y_out, g_out, slope_out, send_ref = refs[-4 - size // 2 : -(size // 2)]
        keep_refs = refs[-(size // 2) :]
        y = jnp.concatenate([r[...] for r in y_refs], axis=0)
        y_out[0] = y
        for at in range(0, hidden, tile):
            cols = slice(at, at + tile)
            u = nn(y, we_ref[:, cols]) + be_ref[:, cols]
            phi_sum, phi = erf_parts(u)
            g_out[0, :, cols] = (u * phi_sum).astype(BF16)
            slope_out[0, :, cols] = (phi_sum + u * phi).astype(BF16)
        write_rows(nn(g_out[0], wc_ref[...]), send_ref, keep_refs, size, rows)

    ins = [whole(b) for b in blocks] + [whole(a) for a in (expand, expand_bias, contract)]
    aliases = {}
    if buffers is not None:
        for number, b in enumerate(buffers):
            aliases[len(ins)] = number
            ins.append((b, None, None))
    outs = [
        ((count, length, w), BF16, (1, length, w), lambda *_: (s, 0, 0)) for w in (d, hidden, hidden)
    ] + partial_outs(size, rows, d)
    return call(
        body, "feed_forward", ins=ins, outs=outs, aliases=aliases,
        flops=4 * length * d * hidden, moved=4 * d * hidden + length * (3 * d + 2 * hidden) * 2,
    )


def feed_back(blocks, expand, contract, slopes, buffers, s, count):
    size = len(blocks)
    rows, d = blocks[0].shape
    hidden = expand.shape[1]
    length = size * rows
    tile = min(256, hidden)

    def body(*refs):
        dz_refs = refs[:size]
        we_ref, wc_ref, slope_ref = refs[size : size + 3]
        sums_ref, dz_out, du_out, send_ref = refs[-4 - size // 2 : -(size // 2)]
        keep_refs = refs[-(size // 2) :]
        dz = jnp.concatenate([r[...] for r in dz_refs], axis=0)
        dz_out[0] = dz
        for at in range(0, hidden, tile):
            cols = slice(at, at + tile)
            du = (nt(dz, wc_ref[cols, :]) * slope_ref[0, :, cols].astype(F32)).astype(BF16)
            du_out[0, :, cols] = du
            sums_ref[:, cols] = column_sum(du.astype(F32))
        write_rows(nt(du_out[0], we_ref[...]), send_ref, keep_refs, size, rows)

    ins = [whole(b) for b in blocks] + [whole(expand), whole(contract)]
    ins.append((slopes, (1, length, hidden), lambda *_: (s, 0, 0)))
    aliases = {}
    if buffers is not None:
        for number, b in enumerate(buffers):
            aliases[len(ins)] = 1 + number
            ins.append((b, None, None))
    outs = [out_whole((1, hidden), F32)]
    outs += [((count, length, w), BF16, (1, length, w), lambda *_: (s, 0, 0)) for w in (d, hidden)]
    outs += partial_outs(size, rows, d)
    return call(
        body, "feed_back", ins=ins, outs=outs, aliases=aliases,
        flops=4 * length * d * hidden, moved=4 * d * hidden + length * (3 * d + 2 * hidden) * 2,
    )


def input_back(first, second, weights, k, size):
    rows = first.shape[1]
    d = weights[1].shape[0]
    width = weights[1].shape[1]

    def body(*refs):
        a_ref, b_ref, qw_ref, kw_ref, vw_ref, send_ref = refs[:6]
        keep_refs = refs[6:]
        a = jnp.concatenate([a_ref[j] for j in range(size)], axis=0)
        b = jnp.concatenate([b_ref[j] for j in range(size)], axis=0)
        total = nt(a[:, :width], qw_ref[0])
        for m in (1, 2):
            total = total + nt(a[:, m * width : (m + 1) * width], qw_ref[m])
        total = total + nt(b[:, :width], qw_ref[3])
        total = total + nt(b[:, width : 2 * width], kw_ref[...])
        total = total + nt(b[:, 2 * width :], vw_ref[...])
        write_rows(total, send_ref, keep_refs, size, rows)

    block = (size, rows, 3 * width)
    ins = [(first, block, lambda *_: (k, 0, 0)), (second, block, lambda *_: (k, 0, 0))]
    ins += [whole(w) for w in weights]
    return call(
        body, "input_back", ins=ins, outs=partial_outs(size, rows, d),
        flops=12 * size * rows * d * width, moved=size * rows * (6 * width + d) * 2 + 12 * d * width,
    )


def final_sum(addends, dr_pieces, buffer, k, count, size):
    rows, d = addends[0].shape[1:]
    n_add = len(addends)

    def body(*refs):
        refs[-1][0] = add_up(refs[: n_add + 1])

    ins = addend_specs(addends)
    ins.append((dr_pieces, (1, rows, d), lambda *_: (k * size, 0, 0)))
    aliases = {}
    if buffer is not None:
        aliases[len(ins)] = 0
        ins.append((buffer, None, None))
    outs = [((count, rows, d), F32, (1, rows, d), lambda *_: (k, 0, 0))]
    return call(body, "final_sum", ins=ins, outs=outs, aliases=aliases, flops=rows * d * 4, moved=rows * d * 12)[0]


def body(
    dp, tensor, tokens, token_kinds, segment_ids, cotangent, query_weight, query_bias, key_weight, key_bias,
    value_weight, value_bias, output_weight, output_bias, inner_gain, inner_shift, expand_weight, expand_bias,
    contract_weight, contract_bias, outer_gain, outer_shift,
):
    count, length = token_kinds.shape
    d = tokens.shape[1]
    rows = length // tensor
    me = lax.axis_index("tensor")
    width = key_weight.shape[2]
    hidden = expand_weight.shape[2]

    devices = np.arange(tensor)
    piece_at = np.array(
        [[[o * count + k for o in devices ^ r] for k in range(count)] for r in range(tensor)], np.int32
    )
    seq_piece = np.array(
        [[[s * tensor + b for b in devices ^ r] for s in range(count)] for r in range(tensor)], np.int32
    )
    table_of = np.array(
        [[(g % count) * tensor + ((g // count) ^ r) for g in seq_piece[r].reshape(-1)] for r in range(tensor)], np.int32
    )
    pick = lambda values: lax.dynamic_index_in_dim(jnp.asarray(values), me, 0, keepdims=False)
    table = pick(table_of)
    kinds = token_kinds.reshape(count * tensor, rows)
    segments = segment_ids.reshape(count * tensor, rows)
    kinds_by_piece = kinds[pick(piece_at).reshape(-1)].reshape(count, length, 1)
    seq_spots = pick(seq_piece).reshape(-1)
    kind_col = kinds[seq_spots].reshape(count, length, 1)
    seg_seq = segments[seq_spots]
    seg_col = seg_seq.reshape(count, length, 1)
    seg_row = seg_seq.reshape(count, 1, length)

    weights = (query_weight[0], key_weight[0], value_weight[0])
    biases = jnp.concatenate([query_bias[0], key_bias, value_bias], axis=0).astype(F32)

    pieces = None
    for k in range(count):
        blocks = gather_blocks(tokens[k * rows : (k + 1) * rows], tensor)
        pieces = project_rows(blocks, kinds_by_piece, weights, biases, pieces, k, count)
    qkv, x_pieces = pieces

    rounds = piece_rounds(count, tensor)
    arrived = []
    spots_of = np.zeros((tensor, count), np.int32)
    for number, chosen in enumerate(rounds):
        sends = pick(np.array([g % count for _, g in chosen], np.int32))
        block = lax.dynamic_slice_in_dim(cotangent, sends * rows, rows, 0)
        perm = [(u, v) for u, (v, _) in enumerate(chosen)]
        if any(u != v for u, v in perm):
            block = lax.ppermute(block, "tensor", perm)
        arrived.append(block)
        for v, g in chosen:
            spots_of[v, g // tensor] = number
    cotangents = jnp.stack(arrived)
    spots = pick(spots_of)

    contexts, totals, n1s, rstds, ys = [], [], [], [], []
    for s in range(count):
        context, lse, send, *keeps = attend(
            qkv, table, s, seg_col, seg_row, kind_col, output_weight[0], tensor, rows
        )
        addends = scatter_sum(send, keeps, tensor)
        y, n1, rstd1 = inner_norm(addends, x_pieces, table, s, output_bias, inner_gain, inner_shift, tensor)
        contexts.append(context)
        totals.append(lse)
        n1s.append(n1)
        rstds.append(rstd1)
        ys.append(y)

    expand, contract = expand_weight[0], contract_weight[0]
    expand_bias32 = expand_bias.astype(F32)
    kept, results, dzs, dzbs, outer_sums = None, None, [], [], []
    for s in range(count):
        blocks = gather_blocks(ys[s], tensor)
        *kept, send = (out := feed_forward(blocks, expand, expand_bias32, contract, kept, s, count))[:4]
        addends = scatter_sum(send, out[4:], tensor)
        results, dz, dzb, sums = outer_norm(
            addends, n1s[s], inner_gain, inner_shift, contract_bias, outer_gain, outer_shift, cotangents, spots,
            results, s, count,
        )
        dzs.append(dz)
        dzbs.append(dzb)
        outer_sums.append(sums)
    y_all, g_all, slopes = kept

    result = {}
    for number, chosen in enumerate(rounds):
        sends, lands = np.zeros(tensor, np.int32), np.zeros(tensor, np.int32)
        for u, (v, g) in enumerate(chosen):
            sends[v], lands[u] = g // tensor, g % count
        block = lax.dynamic_index_in_dim(results, pick(sends), 0, keepdims=False)
        perm = [(v, u) for u, (v, _) in enumerate(chosen)]
        if any(u != v for u, v in perm):
            block = lax.ppermute(block.astype(BF16), "tensor", perm)
        result = place(
            result, [(1, count * rows, d)], (block, pick(lands).reshape(1)), [(0, 0, 1, 0, d)], "place_result"
        )

    kept, drbs, inner_sums, expand_bias_sums = None, [], [], 0.0
    for s in range(count):
        blocks = gather_blocks(dzbs[s], tensor)
        sums, *kept, send = (out := feed_back(blocks, expand, contract, slopes, kept, s, count))[:4]
        expand_bias_sums = expand_bias_sums + sums
        addends = scatter_sum(send, out[4:], tensor)
        drb, sums = inner_norm_back(addends, dzs[s], n1s[s], rstds[s], inner_gain)
        drbs.append(drb)
        inner_sums.append(sums)
    dz_all, du_all = kept
    flat = lambda a: a.reshape(-1, a.shape[-1])
    bits = list(range(dp.bit_length() - 1))
    swapped = bits[1::-1] + bits[2:]
    contract_pieces = sum_over_dp(tn(flat(g_all), flat(dz_all)).astype(BF16), bits, dp)
    expand_pieces = sum_over_dp(tn(flat(y_all), flat(du_all)).astype(BF16), swapped, dp)

    kept, output_sum, bias_sums = None, None, 0.0
    for s in range(count):
        blocks = gather_blocks(drbs[s], tensor)
        *kept, output_sum, sums = attend_back(
            qkv, table, s, seg_col, seg_row, kind_col, output_weight[0], contexts[s], totals[s], blocks, kept,
            output_sum, count,
        )
        bias_sums = bias_sums + sums[:6]
    first, second, dr_pieces = kept
    output_pieces = sum_over_dp(output_sum.astype(BF16), bits, dp)

    x_flat = flat(x_pieces)
    first_pieces = sum_over_dp(tn(x_flat, flat(first)).astype(BF16), bits, dp)
    second_pieces = sum_over_dp(tn(x_flat, flat(second)).astype(BF16), swapped, dp)

    upstream = None
    for k in range(count):
        send, *keeps = input_back(first, second, weights, k, tensor)
        addends = scatter_sum(send, keeps, tensor)
        upstream = final_sum(addends, dr_pieces, upstream, k, count, tensor)

    norms = jnp.concatenate([sum(outer_sums)[:3], sum(inner_sums)[:3]], axis=0)
    norms = doubling_sum(norms, "tensor", tensor)
    top = jnp.concatenate([norms, jnp.pad(expand_bias_sums, ((0, 0), (0, d - hidden)))], axis=0)
    packed = jnp.concatenate([top, jnp.pad(bias_sums, ((0, 1), (0, 0)))], axis=1)
    packed = doubling_sum(packed, "dp", dp)

    shapes = [(4, d, width), (1, d, width), (1, d, width), (1, width, d), (1, d, hidden), (1, hidden, d)]
    grads = {}
    for piece in contract_pieces:
        grads = place(grads, shapes, piece, [(5, 0, 1, 0, d)], "place_contract")
    for piece in expand_pieces:
        grads = place(grads, shapes, piece, [(4, 0, 1, 0, hidden)], "place_expand")
    for piece in output_pieces:
        grads = place(grads, shapes, piece, [(3, 0, 1, 0, d)], "place_output")
    for one, two in zip(first_pieces, second_pieces, strict=True):
        grads = place(grads, shapes, one, [(0, 0, 3, 0, width)], "place_first")
        layout = [(0, 3, 1, 0, width), (1, 0, 1, width, width), (2, 0, 1, 2 * width, width)]
        grads = place(grads, shapes, two, layout, "place_second")

    return (
        result[0].reshape(-1, d),
        upstream.reshape(-1, d),
        grads[0][None],
        packed[None, 0:4, d:],
        grads[1],
        packed[4:5, d:],
        grads[2],
        packed[5:6, d:],
        grads[3],
        packed[3:4, :d],
        packed[4:5, :d],
        packed[5:6, :d],
        grads[4],
        packed[6:7, :hidden],
        grads[5],
        packed[0:1, :d],
        packed[1:2, :d],
        packed[2:3, :d],
    )


def solution(mesh):
    rows, both = P("dp", None), P(("dp", "tensor"), None)
    columns = lambda dims: P(*[None] * (dims - 1), "tensor")
    down = P(None, "tensor", None)
    weight_specs = [columns(4), columns(3), columns(3), columns(2), columns(3), columns(2), down]
    ffn_specs = [columns(3), columns(2), down]
    return jax.shard_map(
        functools.partial(body, mesh.shape["dp"], mesh.shape["tensor"]),
        mesh=mesh,
        in_specs=(both, rows, rows, both, *weight_specs, P(), P(), P(), *ffn_specs, P(), P(), P()),
        out_specs=(both, both, *weight_specs, P(), P(), P(), *ffn_specs, P(), P(), P()),
        check_vma=False,
    )
```

```python
import functools

import jax
import jax.numpy as jnp
import numpy as np
from jax import lax
from jax.experimental import pallas as pl
from jax.experimental.pallas import tpu as pltpu
from jax.sharding import PartitionSpec as P

HD = 64
NORM_EPS = 1e-05
MASKED = -1e30
F32 = jnp.float32
BF16 = jnp.bfloat16
VMEM_LIMIT = 48 * 1024 * 1024
COST = 5e8


def nn(a, b):
    return lax.dot_general(a, b, (((1,), (0,)), ((), ())), preferred_element_type=F32)


def nt(a, b):
    return lax.dot_general(a, b, (((1,), (1,)), ((), ())), preferred_element_type=F32)


def tn(a, b):
    return lax.dot_general(a, b, (((0,), (0,)), ((), ())), preferred_element_type=F32)


class Order:
    mark = None


def call(body, name, *, grid=(1,), prefetch=(), ins, outs, aliases=None, scratch=(), weight=1.0):
    def spec(block, index_map):
        if block is None:
            return pl.BlockSpec(memory_space=pl.ANY)
        return pl.BlockSpec(block, index_map)

    shift = len(prefetch)
    marks = [] if Order.mark is None else [Order.mark]
    n_in, n_out = shift + len(ins), len(outs)

    def inner(*refs):
        given, rest = refs[:n_in], refs[n_in + len(marks) :]
        body(*given, *rest[:n_out], *rest[n_out + 1 :])

    in_specs = [spec(block, index_map) for _, block, index_map in ins]
    in_specs += [pl.BlockSpec(memory_space=pl.ANY) for _ in marks]
    out_specs = [spec(block, index_map) for _, _, block, index_map in outs]
    out_specs.append(pl.BlockSpec(memory_space=pl.ANY))
    shapes = [jax.ShapeDtypeStruct(shape, dtype) for shape, dtype, _, _ in outs]
    *results, Order.mark = pl.pallas_call(
        inner,
        grid_spec=pltpu.PrefetchScalarGridSpec(
            num_scalar_prefetch=shift,
            grid=grid,
            in_specs=in_specs,
            out_specs=out_specs,
            scratch_shapes=list(scratch),
        ),
        out_shape=[*shapes, jax.ShapeDtypeStruct((8, 128), F32)],
        input_output_aliases={shift + k: v for k, v in (aliases or {}).items()},
        compiler_params=pltpu.CompilerParams(vmem_limit_bytes=VMEM_LIMIT),
        cost_estimate=pl.CostEstimate(flops=int(weight * COST), bytes_accessed=1, transcendentals=0),
        name=name,
    )(*prefetch, *[array for array, _, _ in ins], *marks)
    return results


def whole(array):
    zeros = (0,) * array.ndim
    return (array, array.shape, lambda *_: zeros)


def out_whole(shape, dtype):
    zeros = (0,) * len(shape)
    return (shape, dtype, shape, lambda *_: zeros)


def swap(array, axis, size, bit):
    return lax.ppermute(array, axis, [(r, r ^ bit) for r in range(size)])


def gather_blocks(own, size):
    blocks = {0: own}
    bit = 2
    while bit < size:
        for j in sorted(blocks):
            blocks[j | bit] = swap(blocks[j], "tensor", size, bit)
        bit *= 2
    for j in sorted(blocks):
        blocks[j | 1] = swap(blocks[j], "tensor", size, 1)
    return [blocks[j] for j in range(size)]


def combine(keep, received):
    def body(k_ref, r_ref, o_ref):
        o_ref[...] = (k_ref[...].astype(F32) + r_ref[...].astype(F32)).astype(BF16)

    return call(body, "combine", ins=[whole(keep), whole(received)], outs=[out_whole(keep.shape, BF16)])[0]


def scatter_start(sends, size):
    return [swap(block, "tensor", size, 1) for block in sends]


def scatter_rest(keeps, received, size):
    addends = [keeps[0][None], received[0][None]]
    held = {2 * m: combine(keeps[m], received[m]) for m in range(1, len(keeps))}
    bit = size // 2
    while bit >= 2:
        leaving = sorted(j for j in held if j & bit)
        arrived = [swap(held.pop(j), "tensor", size, bit) for j in leaving]
        addends.append(arrived[0][None])
        for j, block in zip(leaving[1:], arrived[1:], strict=True):
            held[j ^ bit] = combine(held[j ^ bit], block)
        bit //= 2
    return addends


def addend_specs(addends):
    return [(a, (1,) + a.shape[1:], lambda *_: (0, 0, 0)) for a in addends]


def place_outs(state, shapes, layout, rows, spot_of, ins):
    outs, aliases = [], {}
    for number, (out, first, leads, _, wide) in enumerate(layout):
        index_map = functools.partial(lambda lead, m, spots: (lead, spot_of(m, spots), 0), first // leads)
        outs.append((shapes[out], F32, (leads, rows, wide), index_map))
        if out in state:
            aliases[len(ins)] = number
            ins.append((state[out], None, None))
    return outs, aliases


def place_values(values, layout, out_refs):
    for (_, _, leads, start, wide), out_ref in zip(layout, out_refs, strict=True):
        for lead in range(leads):
            at = start + lead * wide
            out_ref[lead] = values[:, at : at + wide].astype(F32)


def place(state, shapes, array, places, layout, name):
    count = places.shape[0]
    rows = array.shape[0] // count
    n_out = len(layout)

    def body(places_ref, in_ref, *refs):
        place_values(in_ref[...], layout, refs[-n_out:])

    ins = [(array, (rows, array.shape[1]), lambda m, spots: (m, 0))]
    outs, aliases = place_outs(state, shapes, layout, rows, lambda m, spots: spots[m], ins)
    got = call(body, name, grid=(count,), prefetch=(places,), ins=ins, outs=outs, aliases=aliases)
    state.update({entry[0]: value for entry, value in zip(layout, got, strict=True)})


class DpSum:
    def __init__(self, array, order, size, state, shapes, layout, name):
        self.order, self.size, self.name = order, size, name
        self.state, self.shapes, self.layout = state, shapes, layout
        self.at = 0
        self.whole = array.shape[0] % (16 * size) != 0
        if self.whole:
            self.staying = lax.psum(array, "dp")
            return
        here = lax.axis_index("dp")
        self.mine = [(here >> bit) & 1 for bit in order]
        half = array.shape[0] // 2
        leaving = lax.dynamic_slice_in_dim(array, (1 - self.mine[0]) * half, half, 0)
        self.staying = array
        self.arrived = swap(leaving, "dp", size, 1 << order[0])
        self.held = [0]

    def where(self, differs):
        spot = 0
        for level, mine in enumerate(self.mine):
            spot = spot * 2 + (mine ^ ((differs >> level) & 1))
        return spot

    def step(self):
        if self.whole:
            if self.at == 0:
                place(self.state, self.shapes, self.staying, jnp.zeros((1,), jnp.int32), self.layout, self.name)
        elif self.at < len(self.order):
            self.halve()
        else:
            self.join()
        self.at += 1

    def halve(self):
        level, bits = self.at, len(self.order)
        rows, columns = self.arrived.shape
        last = level == bits - 1
        half = rows // 2
        scalars = [self.mine[0] if level == 0 else 0, self.where(0) if last else self.mine[level + 1]]
        n_out = len(self.layout)

        def body(scalars_ref, stay_ref, came_ref, *refs):
            if last:
                total = (stay_ref[...].astype(F32) + came_ref[...].astype(F32)).astype(BF16)
                refs[-1][...] = total
                place_values(total, self.layout, refs[-1 - n_out : -1])
                return
            for out_ref, part in ((refs[-2], 1 - scalars_ref[1]), (refs[-1], scalars_ref[1])):
                at = pl.ds(pl.multiple_of(part * half, 16), half)
                out_ref[...] = (stay_ref[at, :].astype(F32) + came_ref[at, :].astype(F32)).astype(BF16)

        ins = [(self.staying, (rows, columns), lambda m, spots: (spots[0], 0)), whole(self.arrived)]
        prefetch = (jnp.stack([jnp.asarray(v, jnp.int32) for v in scalars]),)
        if last:
            outs, aliases = place_outs(self.state, self.shapes, self.layout, rows, lambda m, spots: spots[1], ins)
            outs.append(out_whole((rows, columns), BF16))
        else:
            outs, aliases = [out_whole((half, columns), BF16)] * 2, {}
        *got, self.staying = call(
            body, self.name + "_halve", prefetch=prefetch, ins=ins, outs=outs, aliases=aliases
        )
        if last:
            self.state.update({entry[0]: value for entry, value in zip(self.layout, got, strict=True)})
            self.arrived = swap(self.staying, "dp", self.size, 1 << self.order[level])
        else:
            self.arrived = swap(got[0], "dp", self.size, 1 << self.order[level + 1])

    def join(self):
        level = 2 * len(self.order) - 1 - self.at
        count = len(self.held)
        came = [differs | (1 << level) for differs in self.held]
        spots = jnp.stack([self.where(d) for d in came]).astype(jnp.int32)
        self.held = self.held + came
        total, columns = self.arrived.shape
        rows = total // count
        n_out = len(self.layout)
        block = lambda m, spots: (m, 0)
        ins = [(self.arrived, (rows, columns), block)]
        if level:
            ins.append((self.staying, (rows, columns), block))

        def body(spots_ref, came_ref, *refs):
            values = came_ref[...]
            if level:
                refs[-1][0] = refs[0][...]
                refs[-1][1] = values
                place_values(values, self.layout, refs[-1 - n_out : -1])
            else:
                place_values(values, self.layout, refs[-n_out:])

        outs, aliases = place_outs(self.state, self.shapes, self.layout, rows, lambda m, spots: spots[m], ins)
        if level:
            outs.append(((2, total, columns), BF16, (2, rows, columns), lambda m, spots: (0, m, 0)))
        got = call(
            body, self.name + "_join", grid=(count,), prefetch=(spots,), ins=ins, outs=outs, aliases=aliases
        )
        if level:
            self.staying = got.pop().reshape(2 * total, columns)
            self.arrived = swap(self.staying, "dp", self.size, 1 << self.order[level - 1])
        self.state.update({entry[0]: value for entry, value in zip(self.layout, got, strict=True)})


def doubling_sum(array, axis, size):
    bit = 1
    while bit < size:
        array = array + swap(array, axis, size, bit)
        bit *= 2
    return array


def piece_rounds(count, size):
    left = {}
    for g in range(count * size):
        left.setdefault((g // count, g % size), []).append(g)
    rounds = []
    for _ in range(count):
        match = {}

        def augment(u, seen):
            for v in range(size):
                if left.get((u, v)) and v not in seen:
                    seen.add(v)
                    if v not in match or augment(match[v], seen):
                        match[v] = u
                        return True
            return False

        for bit in range(size):
            if all(left.get((u, u ^ bit)) for u in range(size)):
                match.update({u ^ bit: u for u in range(size)})
                break
        else:
            for u in range(size):
                augment(u, set())
        chosen = {u: (v, left[(u, v)].pop(0)) for v, u in match.items()}
        rounds.append([chosen[u] for u in range(size)])
    return rounds


def erf_parts(u):
    size = jnp.abs(u) * np.float32(0.7071067811865476)
    bell = jnp.exp(-(size * size))
    t = pl.reciprocal(1.0 + np.float32(0.3275911) * size)
    poly = np.float32(1.061405429 * 0.5)
    for c in (-1.453152027, 1.421413741, -0.284496736, 0.254829592):
        poly = poly * t + np.float32(c * 0.5)
    tail = poly * t * bell
    return jnp.where(u < 0, tail, 1.0 - tail), bell * np.float32(0.3989422804014327)


def write_rows(values, out_refs, size, rows):
    for j in range(size):
        out_refs[j][...] = values[j * rows : (j + 1) * rows].astype(BF16)


def partial_outs(size, rows, width):
    return [out_whole((rows, width), BF16) for _ in range(size)]


def column(row, wide):
    one = jnp.broadcast_to(row.astype(F32), (128, row.shape[1])).T
    return one if wide == 128 else jnp.concatenate([one] * (wide // 128), axis=1)


def project_rows(blocks, codes, weights, biases, buffers, k, count):
    size = len(blocks)
    rows, d = blocks[0].shape
    width = weights[1].shape[1]

    def body(*refs):
        x_refs = refs[:size]
        kind_ref, qw_ref, kw_ref, vw_ref, b_ref = refs[size : size + 5]
        out_ref, x_out = refs[-2:]
        x = jnp.concatenate([r[...] for r in x_refs], axis=0)
        for j in range(size):
            x_out[j] = x_refs[j][...]
        word = column(kind_ref[0] & 1, width) == 0.0
        bias = [b_ref[m : m + 1, :] for m in range(6)]
        for part, (first, second) in enumerate(((0, 2), (1, 3))):
            one = nn(x, qw_ref[first]) + bias[first]
            two = nn(x, qw_ref[second]) + bias[second]
            both = jnp.where(word, one, two).astype(BF16)
            for j in range(size):
                out_ref[j, :, part * width : (part + 1) * width] = both[j * rows : (j + 1) * rows]
        for part, ref, m in ((2, kw_ref, 4), (3, vw_ref, 5)):
            both = (nn(x, ref[...]) + bias[m]).astype(BF16)
            for j in range(size):
                out_ref[j, :, part * width : (part + 1) * width] = both[j * rows : (j + 1) * rows]

    ins = [whole(b) for b in blocks]
    ins.append((codes, (1,) + codes.shape[1:], lambda *_: (k, 0, 0)))
    ins += [whole(w) for w in weights] + [whole(biases)]
    aliases = {}
    if buffers is not None:
        for number, b in enumerate(buffers):
            aliases[len(ins)] = number
            ins.append((b, None, None))
    outs = [
        ((count * size, rows, 4 * width), BF16, (size, rows, 4 * width), lambda *_: (k, 0, 0)),
        ((count * size, rows, d), BF16, (size, rows, d), lambda *_: (k, 0, 0)),
    ]
    return call(
        body, "project_rows", weight=5, ins=ins, outs=outs, aliases=aliases,
    )


def head_views(piece_refs, part, pair, width):
    start = part * width + pair * 128
    return jnp.concatenate([r[0, :, start : start + 128] for r in piece_refs], axis=0)


def swap_lanes(values):
    return pltpu.roll(values.astype(F32), 64, 1)


def extended(piece_refs, pair, width, takes, left):
    qw = head_views(piece_refs, 0, pair, width)
    qe = head_views(piece_refs, 1, pair, width)
    k = head_views(piece_refs, 2, pair, width)
    v = head_views(piece_refs, 3, pair, width)
    qw32, qe32, k32 = qw.astype(F32), qe.astype(F32), k.astype(F32) * 0.125
    qw_s, qe_s, k_s = swap_lanes(qw32), swap_lanes(qe32), swap_lanes(k32)
    q_ext = (
        jnp.where(left, qw32, qe_s).astype(BF16),
        jnp.where(left, qw_s, qe32).astype(BF16),
    )
    k_ext = (
        jnp.where(takes, jnp.where(left, k32, k_s), 0.0).astype(BF16),
        jnp.where(takes, jnp.where(left, k_s, k32), 0.0).astype(BF16),
    )
    return q_ext, k_ext, v


def query_blocks(length):
    spans, at = [], 0
    while at < length:
        step = 256 if length - at >= 256 else length - at
        spans.append((at, step))
        at += step
    return spans


def attend(pieces, table, s, codes, out_proj, size, rows):
    length = size * rows
    width, d = out_proj.shape
    pairs = width // 128

    def body(table_ref, *refs):
        piece_refs = refs[:size]
        code_ref, wo_ref, c_ref, lse_ref = refs[size : size + 4]
        left = lax.broadcasted_iota(jnp.int32, (length, 128), 1) < 64
        code = code_ref[0]
        word = column(code & 1, 128) == 0.0
        takes = word == left
        segr = (code >> 1).astype(F32)
        segc = column(code >> 1, 256)
        for pair in range(pairs):
            q_ext, k_ext, v = extended(piece_refs, pair, width, takes, left)
            v_t = v.astype(F32).T.astype(BF16)
            for at, step in query_blocks(length):
                same = segc[:, :step] == segr[:, at : at + step]
                tops = []
                for h in range(2):
                    s_t = nt(k_ext[h], q_ext[h][at : at + step])
                    s_t = jnp.where(same, s_t, MASKED)
                    top = jnp.max(s_t, axis=0, keepdims=True)
                    e = jnp.exp(s_t - top)
                    total = jnp.sum(e, axis=0, keepdims=True)
                    o_t = nn(v_t[h * 64 : h * 64 + 64], e.astype(BF16))
                    tops.append(o_t * (1.0 / total))
                    lse_ref[2 * pair + h : 2 * pair + h + 1, at : at + step] = top + jnp.log(total)
                c = jnp.concatenate(tops, axis=0).T.astype(BF16)
                c_ref[at : at + step, pair * 128 : pair * 128 + 128] = c
        write_rows(nn(c_ref[...], wo_ref[...]), refs[-size:], size, rows)

    ins = [
        (pieces, (1, rows, 4 * width), functools.partial(lambda j, _, t: (t[s * size + j], 0, 0), j))
        for j in range(size)
    ]
    ins += [
        (codes, (1, 1, length), lambda *_: (s, 0, 0)),
        whole(out_proj),
    ]
    outs = [out_whole((length, width), BF16), out_whole((8, length), F32)]
    outs += partial_outs(size, rows, d)
    return call(
        body, "attend", weight=7, prefetch=(table,), ins=ins, outs=outs,
    )


def attend_back(pieces, table, s, codes, out_proj, context, lse, delta_blocks, buffers, sums, count):
    size = len(delta_blocks)
    rows, d = delta_blocks[0].shape
    length = size * rows
    width = out_proj.shape[0]
    pairs = width // 128

    def body(table_ref, *refs):
        piece_refs = refs[:size]
        delta_refs = refs[size : 2 * size]
        code_ref, wo_ref, c_ref, lse_ref = refs[2 * size : 2 * size + 4]
        n_out = 5
        tail = refs[2 * size + 4 :]
        sum_in = tail[0] if sums is not None else None
        first_out, second_out, delta_out, wo_grad, bias_out, first_all, second_all = tail[-(n_out + 2) :]
        step_at = pl.program_id(0)

        @pl.when(step_at == 0)
        def _():
            left = lax.broadcasted_iota(jnp.int32, (length, 128), 1) < 64
            code = code_ref[0]
            word = column(code & 1, 128) == 0.0
            takes = word == left
            segr = (code >> 1).astype(F32)
            segc = column(code >> 1, 256)
            delta = jnp.concatenate([r[...] for r in delta_refs], axis=0)
            c_all = c_ref[...]
            grad = nn(c_all.astype(F32).T.astype(BF16), delta)
            wo_grad[...] = grad if sum_in is None else grad + sum_in[...]
            for pair in range(pairs):
                dc = nt(delta, wo_ref[pair * 128 : pair * 128 + 128, :]).astype(BF16)
                q_ext, k_ext, v = extended(piece_refs, pair, width, takes, left)
                k_ext_t = [k.astype(F32).T.astype(BF16) for k in k_ext]
                dc32 = dc.astype(F32)
                dc_h = (jnp.where(left, dc32, 0.0).astype(BF16), jnp.where(left, 0.0, dc32).astype(BF16))
                dv = jnp.zeros((length, 128), F32)
                dk = [jnp.zeros((length, 128), F32)] * 2
                dq = [[], []]
                for at, step in query_blocks(length):
                    same = segc[:, :step] == segr[:, at : at + step]
                    for h in range(2):
                        q_b, dc_b = q_ext[h][at : at + step], dc_h[h][at : at + step]
                        row = 2 * pair + h
                        s_t = nt(k_ext[h], q_b)
                        p = jnp.where(same, jnp.exp(s_t - lse_ref[row : row + 1, at : at + step]), 0.0)
                        dp = nt(v, dc_b)
                        row_inner = jnp.sum(p * dp, axis=0, keepdims=True)
                        ds = (p * (dp - row_inner)).astype(BF16)
                        dv = dv + nn(p.astype(BF16), dc_b)
                        dk[h] = dk[h] + nn(ds, q_b)
                        dq[h].append(nn(k_ext_t[h], ds).T)
                dq0, dq1 = (jnp.concatenate(parts, axis=0) for parts in dq)
                dqw = jnp.where(left, dq0, swap_lanes(dq1))
                dqe = jnp.where(left, swap_lanes(dq0), dq1)
                dk0, dk1 = dk[0] * 0.125, dk[1] * 0.125
                dk_pair = jnp.where(takes, jnp.where(left, dk0, dk1), jnp.where(left, swap_lanes(dk0), swap_lanes(dk1)))
                outs = (
                    jnp.where(word, dqw, 0.0), jnp.where(word, dqe, 0.0), jnp.where(word, 0.0, dqw),
                    jnp.where(word, 0.0, dqe), dk_pair, dv,
                )
                for number, values in enumerate(outs):
                    rounded = values.astype(BF16)
                    target = (first_all, second_all)[number // 3]
                    start = (number % 3) * width + pair * 128
                    target[:, start : start + 128] = rounded
                    bias_out[number : number + 1, pair * 128 : pair * 128 + 128] = jnp.sum(
                        rounded.astype(F32), axis=0, keepdims=True
                    )

        at_rows = pl.ds(pl.multiple_of(step_at * rows, 16), rows)
        first_out[0] = first_all[at_rows, :]
        second_out[0] = second_all[at_rows, :]
        for j in range(size):

            @pl.when(step_at == j)
            def _():
                delta_out[0] = delta_refs[j][...]

    ins = [
        (pieces, (1, rows, 4 * width), functools.partial(lambda j, _, t: (t[s * size + j], 0, 0), j))
        for j in range(size)
    ]
    ins += [whole(b) for b in delta_blocks]
    ins += [
        (codes, (1, 1, length), lambda *_: (s, 0, 0)),
        whole(out_proj),
        whole(context),
        whole(lse),
    ]
    if sums is not None:
        ins.append(whole(sums))
    aliases = {}
    if buffers is not None:
        for number, b in enumerate(buffers):
            aliases[len(ins)] = number
            ins.append((b, None, None))
    spot = lambda m, t: (t[s * size + m], 0, 0)
    outs = [
        ((count * size, rows, 3 * width), BF16, (1, rows, 3 * width), spot),
        ((count * size, rows, 3 * width), BF16, (1, rows, 3 * width), spot),
        ((count * size, rows, d), BF16, (1, rows, d), spot),
        out_whole((width, d), F32),
        out_whole((8, width), F32),
    ]
    return call(
        body, "attend_back", weight=13, grid=(size,), prefetch=(table,), ins=ins, outs=outs, aliases=aliases,
        scratch=[pltpu.VMEM((length, 3 * width), BF16)] * 2,
    )


def add_up(refs):
    total = refs[0][0].astype(F32)
    for r in refs[1:]:
        total = total + r[0].astype(F32)
    return total


def normed(values):
    centre = jnp.mean(values, axis=-1, keepdims=True)
    offset = values - centre
    spread = jnp.mean(offset * offset, axis=-1, keepdims=True)
    rstd = lax.rsqrt(spread + NORM_EPS)
    return offset * rstd, rstd


def norm_pull(upstream, n, rstd, gain):
    scaled = upstream * gain
    inner = jnp.mean(scaled, axis=-1, keepdims=True)
    cross = jnp.mean(scaled * n, axis=-1, keepdims=True)
    return rstd * (scaled - inner - n * cross)


def column_sum(values):
    return jnp.sum(values, axis=0, keepdims=True)


def inner_norm(addends, x_pieces, table, s, bias, gain, shift, size):
    rows, d = addends[0].shape[1:]
    n_add = len(addends)

    def body(table_ref, *refs):
        x_ref, b_ref, g_ref, h_ref, y_ref, n_ref, rstd_ref = refs[n_add:]
        r = add_up(refs[:n_add]) + b_ref[...] + x_ref[0].astype(F32)
        n, rstd = normed(r)
        n_ref[...] = n
        rstd_ref[...] = jnp.broadcast_to(rstd, (rows, 128))
        y_ref[...] = (n * g_ref[...] + h_ref[...]).astype(BF16)

    ins = addend_specs(addends)
    ins.append((x_pieces, (1, rows, d), lambda _, t: (t[s * size], 0, 0)))
    ins += [whole(bias), whole(gain), whole(shift)]
    outs = [out_whole((rows, d), BF16), out_whole((rows, d), F32), out_whole((rows, 128), F32)]
    return call(body, "inner_norm", weight=2, prefetch=(table,), ins=ins, outs=outs)


def outer_norm(addends, n1, inner_gain, inner_shift, bias, gain, shift, cotangents, spots, buffer, s, count):
    rows, d = addends[0].shape[1:]
    n_add = len(addends)

    def body(spots_ref, *refs):
        n1_ref, g1_ref, h1_ref, b_ref, g_ref, h_ref, e_ref = refs[n_add : n_add + 7]
        res_ref, dz_ref, dzb_ref, sums_ref = refs[-4:]
        z = add_up(refs[:n_add]) + b_ref[...] + (n1_ref[...] * g1_ref[...] + h1_ref[...])
        n, rstd = normed(z)
        res_ref[0] = n * g_ref[...] + h_ref[...]
        e = e_ref[0].astype(F32)
        dz = norm_pull(e, n, rstd, g_ref[...])
        dz_ref[...] = dz
        dzb_ref[...] = dz.astype(BF16)
        sums_ref[0:1] = column_sum(dz)
        sums_ref[1:2] = column_sum(e * n)
        sums_ref[2:3] = column_sum(e)

    ins = addend_specs(addends)
    ins += [whole(a) for a in (n1, inner_gain, inner_shift, bias, gain, shift)]
    ins.append((cotangents, (1, rows, d), lambda _, t: (t[s], 0, 0)))
    aliases = {}
    if buffer is not None:
        aliases[len(ins)] = 0
        ins.append((buffer, None, None))
    outs = [
        ((count, rows, d), F32, (1, rows, d), lambda *_: (s, 0, 0)),
        out_whole((rows, d), F32),
        out_whole((rows, d), BF16),
        out_whole((8, d), F32),
    ]
    return call(
        body, "outer_norm", weight=2, prefetch=(spots,), ins=ins, outs=outs, aliases=aliases,
    )


def inner_norm_back(addends, dz, n1, rstd1, gain):
    rows, d = addends[0].shape[1:]
    n_add = len(addends)

    def body(*refs):
        dz_ref, n_ref, rstd_ref, g_ref, dr_ref, sums_ref = refs[n_add:]
        da = add_up(refs[:n_add]) + dz_ref[...]
        n = n_ref[...]
        dr = norm_pull(da, n, rstd_ref[:, 0:1], g_ref[...])
        dr_ref[...] = dr.astype(BF16)
        sums_ref[0:1] = column_sum(dr)
        sums_ref[1:2] = column_sum(da * n)
        sums_ref[2:3] = column_sum(da)

    ins = addend_specs(addends) + [whole(a) for a in (dz, n1, rstd1, gain)]
    outs = [out_whole((rows, d), BF16), out_whole((8, d), F32)]
    return call(body, "inner_norm_back", weight=2, ins=ins, outs=outs)


def feed_forward(blocks, expand, expand_bias, contract, buffers, s, count):
    size = len(blocks)
    rows, d = blocks[0].shape
    hidden = expand.shape[1]
    length = size * rows
    tile = min(256, hidden)

    def body(*refs):
        y_refs = refs[:size]
        we_ref, be_ref, wc_ref = refs[size : size + 3]
        y_out, g_out, slope_out = refs[-3 - size : -size]
        y = jnp.concatenate([r[...] for r in y_refs], axis=0)
        y_out[0] = y
        for at in range(0, hidden, tile):
            cols = slice(at, at + tile)
            u = nn(y, we_ref[:, cols]) + be_ref[:, cols]
            phi_sum, phi = erf_parts(u)
            g_out[0, :, cols] = (u * phi_sum).astype(BF16)
            slope_out[0, :, cols] = (phi_sum + u * phi).astype(BF16)
        write_rows(nn(g_out[0], wc_ref[...]), refs[-size:], size, rows)

    ins = [whole(b) for b in blocks] + [whole(a) for a in (expand, expand_bias, contract)]
    aliases = {}
    if buffers is not None:
        for number, b in enumerate(buffers):
            aliases[len(ins)] = number
            ins.append((b, None, None))
    outs = [
        ((count, length, w), BF16, (1, length, w), lambda *_: (s, 0, 0)) for w in (d, hidden, hidden)
    ] + partial_outs(size, rows, d)
    return call(
        body, "feed_forward", weight=8, ins=ins, outs=outs, aliases=aliases,
    )


def feed_back(blocks, expand, contract, slopes, buffers, s, count):
    size = len(blocks)
    rows, d = blocks[0].shape
    hidden = expand.shape[1]
    length = size * rows
    tile = min(256, hidden)

    def body(*refs):
        dz_refs = refs[:size]
        we_ref, wc_ref, slope_ref = refs[size : size + 3]
        sums_ref, dz_out, du_out = refs[-3 - size : -size]
        dz = jnp.concatenate([r[...] for r in dz_refs], axis=0)
        dz_out[0] = dz
        for at in range(0, hidden, tile):
            cols = slice(at, at + tile)
            du = (nt(dz, wc_ref[cols, :]) * slope_ref[0, :, cols].astype(F32)).astype(BF16)
            du_out[0, :, cols] = du
            sums_ref[:, cols] = column_sum(du.astype(F32))
        write_rows(nt(du_out[0], we_ref[...]), refs[-size:], size, rows)

    ins = [whole(b) for b in blocks] + [whole(expand), whole(contract)]
    ins.append((slopes, (1, length, hidden), lambda *_: (s, 0, 0)))
    aliases = {}
    if buffers is not None:
        for number, b in enumerate(buffers):
            aliases[len(ins)] = 1 + number
            ins.append((b, None, None))
    outs = [out_whole((1, hidden), F32)]
    outs += [((count, length, w), BF16, (1, length, w), lambda *_: (s, 0, 0)) for w in (d, hidden)]
    outs += partial_outs(size, rows, d)
    return call(
        body, "feed_back", weight=5, ins=ins, outs=outs, aliases=aliases,
    )


def input_back(first, second, weights, k, size):
    rows = first.shape[1]
    d = weights[1].shape[0]
    width = weights[1].shape[1]

    def body(*refs):
        a_ref, b_ref, qw_ref, kw_ref, vw_ref = refs[:5]
        a = jnp.concatenate([a_ref[j] for j in range(size)], axis=0)
        b = jnp.concatenate([b_ref[j] for j in range(size)], axis=0)
        total = nt(a[:, :width], qw_ref[0])
        for m in (1, 2):
            total = total + nt(a[:, m * width : (m + 1) * width], qw_ref[m])
        total = total + nt(b[:, :width], qw_ref[3])
        total = total + nt(b[:, width : 2 * width], kw_ref[...])
        total = total + nt(b[:, 2 * width :], vw_ref[...])
        write_rows(total, refs[-size:], size, rows)

    block = (size, rows, 3 * width)
    ins = [(first, block, lambda *_: (k, 0, 0)), (second, block, lambda *_: (k, 0, 0))]
    ins += [whole(w) for w in weights]
    return call(
        body, "input_back", weight=4, ins=ins, outs=partial_outs(size, rows, d),
    )


def collect(blocks):
    rows, d = blocks[0].shape

    def body(*refs):
        for m in range(len(blocks)):
            refs[-1][m] = refs[m][...]

    outs = [out_whole((len(blocks), rows, d), BF16)]
    return call(body, "collect", ins=[whole(b) for b in blocks], outs=outs)[0]


def final_sum(addends, dr_pieces, buffer, k, count, size):
    rows, d = addends[0].shape[1:]
    n_add = len(addends)

    def body(*refs):
        refs[-1][0] = add_up(refs[: n_add + 1])

    ins = addend_specs(addends)
    ins.append((dr_pieces, (1, rows, d), lambda *_: (k * size, 0, 0)))
    aliases = {}
    if buffer is not None:
        aliases[len(ins)] = 0
        ins.append((buffer, None, None))
    outs = [((count, rows, d), F32, (1, rows, d), lambda *_: (k, 0, 0))]
    return call(body, "final_sum", ins=ins, outs=outs, aliases=aliases)[0]


def body(
    dp, tensor, tokens, token_kinds, segment_ids, cotangent, query_weight, query_bias, key_weight, key_bias,
    value_weight, value_bias, output_weight, output_bias, inner_gain, inner_shift, expand_weight, expand_bias,
    contract_weight, contract_bias, outer_gain, outer_shift,
):
    count, length = token_kinds.shape
    d = tokens.shape[1]
    rows = length // tensor
    me = lax.axis_index("tensor")
    width = key_weight.shape[2]
    hidden = expand_weight.shape[2]

    devices = np.arange(tensor)
    piece_at = np.array(
        [[[o * count + k for o in devices ^ r] for k in range(count)] for r in range(tensor)], np.int32
    )
    seq_piece = np.array(
        [[[s * tensor + b for b in devices ^ r] for s in range(count)] for r in range(tensor)], np.int32
    )
    table_of = np.array(
        [[(g % count) * tensor + ((g // count) ^ r) for g in seq_piece[r].reshape(-1)] for r in range(tensor)], np.int32
    )
    pick = lambda values: lax.dynamic_index_in_dim(jnp.asarray(values), me, 0, keepdims=False)
    table = pick(table_of)
    codes = (segment_ids * 2 + token_kinds).reshape(count * tensor, rows)
    order = np.concatenate([piece_at.reshape(tensor, -1), seq_piece.reshape(tensor, -1)], axis=1)
    codes = codes[pick(order)].reshape(2, count, 1, length)
    piece_codes, seq_codes = codes[0], codes[1]

    weights = (query_weight[0], key_weight[0], value_weight[0])
    biases = jnp.concatenate([query_bias[0], key_bias, value_bias], axis=0).astype(F32)
    expand, contract = expand_weight[0], contract_weight[0]
    expand_bias32 = expand_bias.astype(F32)
    out_proj = output_weight[0]
    Order.mark = None

    gathered = [gather_blocks(tokens[k * rows : (k + 1) * rows], tensor) for k in range(count)]
    pieces = None
    for k in range(count):
        pieces = project_rows(gathered[k], piece_codes, weights, biases, pieces, k, count)
    qkv, x_pieces = pieces

    rounds = piece_rounds(count, tensor)
    arrived = []
    spots_of = np.zeros((tensor, count), np.int32)
    for number, chosen in enumerate(rounds):
        sends = pick(np.array([g % count for _, g in chosen], np.int32))
        block = lax.dynamic_slice_in_dim(cotangent, sends * rows, rows, 0)
        perm = [(u, v) for u, (v, _) in enumerate(chosen)]
        if any(u != v for u, v in perm):
            block = lax.ppermute(block, "tensor", perm)
        arrived.append(block)
        for v, g in chosen:
            spots_of[v, g // tensor] = number
    spots = pick(spots_of)
    hold = {"cotangents": collect(arrived)}

    def stage(run, finish, before):
        for s in range(count):
            partial = run(s)
            received = scatter_start(partial[1::2], tensor)
            if s:
                finish(s - 1)
            elif before is not None:
                before(count - 1)
            hold["addends", s] = scatter_rest(partial[0::2], received, tensor)

    def run_attend(s):
        hold["context", s], hold["lse", s], *partial = attend(qkv, table, s, seq_codes, out_proj, tensor, rows)
        return partial

    def finish_attend(s):
        y, hold["n1", s], hold["rstd1", s] = inner_norm(
            hold["addends", s], x_pieces, table, s, output_bias, inner_gain, inner_shift, tensor
        )
        hold["y", s] = gather_blocks(y, tensor)

    def run_forward(s):
        out = feed_forward(hold["y", s], expand, expand_bias32, contract, hold.get("kept"), s, count)
        hold["kept"] = out[:3]
        return out[3:]

    def finish_forward(s):
        hold["results"], hold["dz", s], dzb, hold["outer", s] = outer_norm(
            hold["addends", s], hold["n1", s], inner_gain, inner_shift, contract_bias, outer_gain, outer_shift,
            hold["cotangents"], spots, hold.get("results"), s, count,
        )
        hold["dzb", s] = gather_blocks(dzb, tensor)

    def run_back(s):
        out = feed_back(hold["dzb", s], expand, contract, hold["kept"][2], hold.get("back"), s, count)
        hold["expand_bias", s], hold["back"] = out[0], out[1:3]
        return out[3:]

    def finish_back(s):
        drb, hold["inner", s] = inner_norm_back(
            hold["addends", s], hold["dz", s], hold["n1", s], hold["rstd1", s], inner_gain
        )
        hold["drb", s] = gather_blocks(drb, tensor)

    stage(run_attend, finish_attend, None)
    stage(run_forward, finish_forward, finish_attend)
    stage(run_back, finish_back, finish_forward)
    y_all, g_all, _ = hold["kept"]
    dz_all, du_all = hold["back"]

    shapes = [(4, d, width), (1, d, width), (1, d, width), (1, width, d), (1, d, hidden), (1, hidden, d)]
    grads = {}
    flat = lambda a: a.reshape(-1, a.shape[-1])
    bits = list(range(dp.bit_length() - 1))
    swapped = bits[1::-1] + bits[2:]
    sum_of = lambda array, order, layout, name: DpSum(array, order, dp, grads, shapes, layout, name)
    steps = lambda *sums: [one.step() for one in sums]
    of_contract = sum_of(tn(flat(g_all), flat(dz_all)).astype(BF16), bits, [(5, 0, 1, 0, d)], "contract")
    of_expand = sum_of(tn(flat(y_all), flat(du_all)).astype(BF16), swapped, [(4, 0, 1, 0, hidden)], "expand")

    kept, output_sum = None, None
    for s in range(count):
        *kept, output_sum, hold["bias", s] = attend_back(
            qkv, table, s, seq_codes, out_proj, hold["context", s], hold["lse", s], hold["drb", s], kept, output_sum, count
        )
        if s == 0:
            finish_back(count - 1)
        steps(of_contract, of_expand)
    first, second, dr_pieces = kept

    x_flat = flat(x_pieces)
    of_first = sum_of(tn(x_flat, flat(first)).astype(BF16), bits, [(0, 0, 3, 0, width)], "first")
    layout = [(0, 3, 1, 0, width), (1, 0, 1, width, width), (2, 0, 1, 2 * width, width)]
    of_second = sum_of(tn(x_flat, flat(second)).astype(BF16), swapped, layout, "second")
    of_output = sum_of(output_sum.astype(BF16), bits, [(3, 0, 1, 0, d)], "output")

    for k in range(count):
        partial = input_back(first, second, weights, k, tensor)
        hold["addends", k] = scatter_rest(partial[0::2], scatter_start(partial[1::2], tensor), tensor)
    done = len(bits) * 2
    while of_first.at < done:
        for one in (of_first, of_second, of_output, of_contract, of_expand):
            if one.at < done:
                one.step()

    result = {}
    for number, chosen in enumerate(rounds):
        sends, lands = np.zeros(tensor, np.int32), np.zeros(tensor, np.int32)
        for u, (v, g) in enumerate(chosen):
            sends[v], lands[u] = g // tensor, g % count
        block = lax.dynamic_index_in_dim(hold["results"], pick(sends), 0, keepdims=False)
        perm = [(v, u) for u, (v, _) in enumerate(chosen)]
        if any(u != v for u, v in perm):
            block = lax.ppermute(block.astype(BF16), "tensor", perm)
        place(result, [(1, count * rows, d)], block, pick(lands).reshape(1), [(0, 0, 1, 0, d)], "place_result")

    upstream = None
    for k in range(count):
        upstream = final_sum(hold["addends", k], dr_pieces, upstream, k, count, tensor)

    total = lambda name: sum(hold[name, s] for s in range(count))
    norms = jnp.concatenate([total("outer")[:3], total("inner")[:3]], axis=0)
    norms = doubling_sum(norms, "tensor", tensor)
    top = jnp.concatenate([norms, jnp.pad(total("expand_bias"), ((0, 0), (0, d - hidden)))], axis=0)
    packed = jnp.concatenate([top, jnp.pad(total("bias")[:6], ((0, 1), (0, 0)))], axis=1)
    packed = doubling_sum(packed, "dp", dp)

    return (
        result[0].reshape(-1, d),
        upstream.reshape(-1, d),
        grads[0][None],
        packed[None, 0:4, d:],
        grads[1],
        packed[4:5, d:],
        grads[2],
        packed[5:6, d:],
        grads[3],
        packed[3:4, :d],
        packed[4:5, :d],
        packed[5:6, :d],
        grads[4],
        packed[6:7, :hidden],
        grads[5],
        packed[0:1, :d],
        packed[1:2, :d],
        packed[2:3, :d],
    )


def solution(mesh):
    rows, both = P("dp", None), P(("dp", "tensor"), None)
    columns = lambda dims: P(*[None] * (dims - 1), "tensor")
    down = P(None, "tensor", None)
    weight_specs = [columns(4), columns(3), columns(3), columns(2), columns(3), columns(2), down]
    ffn_specs = [columns(3), columns(2), down]
    return jax.shard_map(
        functools.partial(body, mesh.shape["dp"], mesh.shape["tensor"]),
        mesh=mesh,
        in_specs=(both, rows, rows, both, *weight_specs, P(), P(), P(), *ffn_specs, P(), P(), P()),
        out_specs=(both, both, *weight_specs, P(), P(), P(), *ffn_specs, P(), P(), P()),
        check_vma=False,
    )
```

```python
import functools

import jax
import jax.numpy as jnp
import numpy as np
from jax import lax
from jax.experimental import pallas as pl
from jax.experimental.pallas import tpu as pltpu
from jax.sharding import PartitionSpec as P

HD = 64
NORM_EPS = 1e-05
MASKED = -1e30
F32 = jnp.float32
BF16 = jnp.bfloat16
SMALL, LARGE = 6, 22
COST = 1.15e9
SWAPPED = "ea"
AFTER = (
    "Ge", "Gc:2.5", "near1:1", "norm:5", "attend:1", "attend:1", "c:0.02", "near2", "norms:0.5", "e:5", "attend:1", "c:0.02", "add:1", "e:0.02",
    "Ga", "take:1", "Gb:1", "c:0.5", "e:0.02", "in:2.5", "send:2.5", "a:1", "b:2.5", "c:2.5", "a", "e:0.02", "b:1", "a:9", "b:1", "e", "a:0.5", "sum", "b:0.02", "c:2.5", "a", "b", "e", "put", "end:0.02", "c:1", "b:2.5", "a:2.5",
)


def nn(a, b):
    return lax.dot_general(a, b, (((1,), (0,)), ((), ())), preferred_element_type=F32)


def nt(a, b):
    return lax.dot_general(a, b, (((1,), (1,)), ((), ())), preferred_element_type=F32)


def tn(a, b):
    return lax.dot_general(a, b, (((0,), (0,)), ((), ())), preferred_element_type=F32)


class Order:
    mark = None
    weight = 0.2


def call(body, name, *, grid=(1,), prefetch=(), ins, outs, aliases=None, scratch=(), weight=None, vmem=SMALL):
    def spec(block, index_map):
        if block is None:
            return pl.BlockSpec(memory_space=pl.ANY)
        return pl.BlockSpec(block, index_map, pipeline_mode=pl.Buffered(1) if grid == (1,) else None)

    shift = len(prefetch)
    marks = [] if Order.mark is None else [Order.mark]
    n_in, n_out = shift + len(ins), len(outs)

    def inner(*refs):
        given, rest = refs[:n_in], refs[n_in + len(marks) :]
        body(*given, *rest[:n_out], *rest[n_out + 1 :])

    in_specs = [spec(block, index_map) for _, block, index_map in ins]
    in_specs += [pl.BlockSpec(memory_space=pl.ANY) for _ in marks]
    out_specs = [spec(block, index_map) for _, _, block, index_map in outs]
    out_specs.append(pl.BlockSpec(memory_space=pl.ANY))
    shapes = [jax.ShapeDtypeStruct(shape, dtype) for shape, dtype, _, _ in outs]
    *results, Order.mark = pl.pallas_call(
        inner,
        grid_spec=pltpu.PrefetchScalarGridSpec(
            num_scalar_prefetch=shift,
            grid=grid,
            in_specs=in_specs,
            out_specs=out_specs,
            scratch_shapes=list(scratch),
        ),
        out_shape=[*shapes, jax.ShapeDtypeStruct((8, 128), F32)],
        input_output_aliases={shift + k: v for k, v in (aliases or {}).items()},
        compiler_params=pltpu.CompilerParams(vmem_limit_bytes=vmem * 1024 * 1024),
        cost_estimate=pl.CostEstimate(flops=int((Order.weight if weight is None else weight) * COST), bytes_accessed=1, transcendentals=0),
        name=name,
    )(*prefetch, *[array for array, _, _ in ins], *marks)
    return results


def whole(array):
    zeros = (0,) * array.ndim
    return (array, array.shape, lambda *_: zeros)


def out_whole(shape, dtype):
    zeros = (0,) * len(shape)
    return (shape, dtype, shape, lambda *_: zeros)


def swap(array, axis, size, bit):
    return lax.ppermute(array, axis, [(r, r ^ bit) for r in range(size)])


def gather_start(own, size):
    blocks = {0: own}
    bit = 2
    while bit < size:
        for j in sorted(blocks):
            blocks[j | bit] = swap(blocks[j], "tensor", size, bit)
        bit *= 2
    return blocks


def gather_end(blocks, size):
    even = relay([blocks[j] for j in range(0, size, 2)])
    odd = swap(even, "tensor", size, 1)
    return [((odd if j & 1 else even), j // 2) for j in range(size)]


def block_specs(blocks):
    return [
        (a, (1, *a.shape[1:]), functools.partial(lambda at, *_: (at, 0, 0), at)) for a, at in blocks
    ]


def combine(keep, received, m):
    rows, d = keep.shape

    def body(k_ref, r_ref, o_ref):
        o_ref[...] = (k_ref[...].astype(F32) + r_ref[0].astype(F32)).astype(BF16)

    ins = [whole(keep), (received, (1, rows, d), lambda *_: (m, 0, 0))]
    return call(body, "combine", ins=ins, outs=[out_whole((rows, d), BF16)])[0]


def scatter_rest(keeps, received, size):
    addends = [keeps[0][None], received]
    held = {2 * m: combine(keeps[m], received, m) for m in range(1, len(keeps))}
    bit = size // 2
    while bit >= 2:
        leaving = sorted(j for j in held if j & bit)
        arrived = [swap(held.pop(j), "tensor", size, bit) for j in leaving]
        addends.append(arrived[0][None])
        for j, block in zip(leaving[1:], arrived[1:], strict=True):
            held[j ^ bit] = combine(held[j ^ bit], block[None], 0)
        bit //= 2
    return addends


def addend_specs(addends):
    return [(a, (1,) + a.shape[1:], lambda *_: (0, 0, 0)) for a in addends]


def place_outs(state, shapes, layout, rows, spot_of, ins):
    outs, aliases = [], {}
    for number, (out, (lead, leads), _, wide, block) in enumerate(layout):
        index_map = functools.partial(lambda lead, block, m, spots: (lead, spot_of(m, spots), block), lead, block)
        outs.append((shapes[out], F32, (leads, rows, wide), index_map))
        if out in state:
            aliases[len(ins)] = number
            ins.append((state[out], None, None))
    return outs, aliases


def place_values(values, layout, out_refs):
    for (_, (_, leads), start, wide, _), out_ref in zip(layout, out_refs, strict=True):
        for lead in range(leads):
            at = start + lead * wide
            out_ref[lead] = values[:, at : at + wide].astype(F32)


class DpSum:
    def __init__(self, entries, size, state, shapes, name):
        self.size, self.name, self.state, self.shapes = size, name, state, shapes
        self.at = 0
        self.orders = [order for _, order, _ in entries]
        self.layouts = [layout for _, _, layout in entries]
        self.bits = len(entries[0][1])
        self.steps = 2 * self.bits
        here = lax.axis_index("dp")
        self.mine = [[(here >> bit) & 1 for bit in order] for order in self.orders]
        self.held = [0]
        self.staying = [halves[0] for halves, _, _ in entries]
        self.send([halves[1] for halves, _, _ in entries], 0)

    def scalars(self, values):
        return jnp.stack([jnp.asarray(v, jnp.int32) for v in values])

    def send(self, blocks, level):
        self.arrived = [
            swap(block, "dp", self.size, 1 << order[level]) for block, order in zip(blocks, self.orders, strict=True)
        ]

    def where(self, m, differs):
        spot = 0
        for level, mine in enumerate(self.mine[m]):
            spot = spot * 2 + (mine ^ ((differs >> level) & 1))
        return spot

    def step(self):
        if self.at < self.bits:
            self.halve()
        else:
            self.join()
        self.at += 1

    def placing(self, ins, rows, spot_of):
        outs, aliases = [], {}
        for m, layout in enumerate(self.layouts):
            index_of = functools.partial(spot_of, m)
            more, taken = place_outs(self.state, self.shapes, layout, rows[m], index_of, ins)
            aliases.update({k: v + len(outs) for k, v in taken.items()})
            outs += more
        return outs, aliases

    def keep_placed(self, got):
        names = [entry[0] for layout in self.layouts for entry in layout]
        self.state.update(dict(zip(names, got, strict=True)))

    def halve(self):
        level = self.at
        last = level == self.bits - 1
        n = len(self.staying)
        shapes = [a.shape for a in self.arrived]
        ends = np.cumsum([0] + [len(layout) for layout in self.layouts])

        def body(scalars_ref, *refs):
            outs = refs[2 * n :]
            for m in range(n):
                stay_ref, came_ref = refs[2 * m : 2 * m + 2]
                if last:
                    total = (stay_ref[...].astype(F32) + came_ref[...].astype(F32)).astype(BF16)
                    outs[len(outs) - n + m][...] = total
                    place_values(total, self.layouts[m], outs[len(outs) - n - ends[-1] :][ends[m] : ends[m + 1]])
                    continue
                half = shapes[m][0] // 2
                for out_ref, part in ((outs[2 * m], 1 - scalars_ref[m]), (outs[2 * m + 1], scalars_ref[m])):
                    at = pl.ds(pl.multiple_of(part * half, 16), half)
                    out_ref[...] = (stay_ref[at, :].astype(F32) + came_ref[at, :].astype(F32)).astype(BF16)

        ins = [whole(a) for pair in zip(self.staying, self.arrived, strict=True) for a in pair]
        if last:
            prefetch = self.scalars([self.where(m, 0) for m in range(n)])
            outs, aliases = self.placing(ins, [shape[0] for shape in shapes], lambda m, i, spots: spots[m])
            outs += [out_whole(shape, BF16) for shape in shapes]
        else:
            prefetch = self.scalars([mine[level + 1] for mine in self.mine])
            outs, aliases = [], {}
            for rows, columns in shapes:
                outs += [out_whole((rows // 2, columns), BF16)] * 2
        got = call(
            body, self.name + "_halve", prefetch=(prefetch,), ins=ins, outs=outs, aliases=aliases
        )
        if last:
            self.staying = got[len(got) - n :]
            self.keep_placed(got[: len(got) - n])
            self.send(self.staying, level)
        else:
            self.staying = got[1::2]
            self.send(got[0::2], level + 1)

    def join(self):
        level = self.steps - 1 - self.at
        count = len(self.held)
        came = [differs | (1 << level) for differs in self.held]
        self.held = self.held + came
        n = len(self.arrived)
        spots = self.scalars([self.where(m, differs) for m in range(n) for differs in came])
        rows = [a.shape[0] // count for a in self.arrived]
        ends = np.cumsum([0] + [len(layout) for layout in self.layouts])
        block = lambda i, spots: (i, 0)
        ins = [(a, (r, a.shape[1]), block) for a, r in zip(self.arrived, rows, strict=True)]
        if level:
            ins += [(a, (r, a.shape[1]), block) for a, r in zip(self.staying, rows, strict=True)]

        def body(spots_ref, *refs):
            joined = refs[len(refs) - n :] if level else ()
            placed = refs[len(refs) - len(joined) - ends[-1] : len(refs) - len(joined)]
            for m in range(n):
                values = refs[m][...]
                if level:
                    joined[m][0] = refs[n + m][...]
                    joined[m][1] = values
                place_values(values, self.layouts[m], placed[ends[m] : ends[m + 1]])

        outs, aliases = self.placing(ins, rows, lambda m, i, spots: spots[m * count + i])
        if level:
            for a, r in zip(self.arrived, rows, strict=True):
                outs.append(((2, *a.shape), BF16, (2, r, a.shape[1]), lambda i, spots: (0, i, 0)))
        got = call(
            body, self.name + "_join", grid=(count,), prefetch=(spots,), ins=ins, outs=outs, aliases=aliases
        )
        if level:
            self.staying = [a.reshape(-1, a.shape[2]) for a in got[len(got) - n :]]
            got = got[: len(got) - n]
            self.send(self.staying, level - 1)
        self.keep_placed(got)


def weight_grad(left_side, right_side, bit, name, more=None):
    tokens, total = left_side.shape
    columns = right_side.shape[1]
    half = total // 2

    def body(mine_ref, a_ref, b_ref, *refs):
        stay_ref, leave_ref = refs[-2:]
        product = tn(a_ref[...], b_ref[...]).astype(BF16)
        if more is not None:
            product = jnp.concatenate([product, refs[0][...]], axis=1)
        mine = pl.program_id(0) == mine_ref[0]

        @pl.when(mine)
        def _():
            stay_ref[...] = product

        @pl.when(jnp.logical_not(mine))
        def _():
            leave_ref[...] = product

    ins = [(left_side, (tokens, half), lambda i, mine: (0, i)), whole(right_side)]
    if more is not None:
        ins.append((more, (half, more.shape[1]), lambda i, mine: (i, 0)))
        columns += more.shape[1]
    outs = [out_whole((half, columns), BF16)] * 2
    mine = ((lax.axis_index("dp") >> bit) & 1).reshape(1).astype(jnp.int32)
    return call(body, name, vmem=LARGE, grid=(2,), prefetch=(mine,), ins=ins, outs=outs)


def add(one, two):
    def body(one_ref, two_ref, out_ref):
        out_ref[...] = one_ref[...] + two_ref[...]

    return call(body, "add", ins=[whole(one), whole(two)], outs=[out_whole(one.shape, F32)])[0]


def norm_sums(outer, inner):
    n, shape = len(outer), outer[0].shape

    def body(*refs):
        for at, group in ((0, refs[:n]), (3, refs[n : 2 * n])):
            total = group[0][0:3]
            for r in group[1:]:
                total = total + r[0:3]
            refs[-1][at : at + 3] = total
        refs[-1][6:8] = jnp.zeros((2, shape[1]), F32)

    ins = [whole(a) for a in (*outer, *inner)]
    return call(body, "norm_sums", ins=ins, outs=[out_whole(shape, F32)])[0]


def pack(output_sum, norms, came, expand_bias, bias):
    width, d = output_sum.shape
    hidden = expand_bias[0].shape[1]
    n = len(bias)

    def body(o_ref, norm_ref, came_ref, *refs):
        out_ref, rows_ref = refs[-2:]
        rows_ref[...] = jnp.zeros((128, d), F32)
        rows_ref[0:6] = norm_ref[0:6] + came_ref[0:6]
        total = refs[0][...]
        for r in refs[1:n]:
            total = total + r[...]
        rows_ref[6:7, :hidden] = total
        total = refs[n][0:6]
        for r in refs[n + 1 : 2 * n]:
            total = total + r[0:6]
        rows_ref[7:13, :width] = total
        out_ref[:, :width] = o_ref[...].T.astype(BF16)
        out_ref[:, width:] = rows_ref[...].T.astype(BF16)

    ins = [whole(a) for a in (output_sum, norms, came, *expand_bias, *bias)]
    outs = [out_whole((d, width + 128), BF16)]
    return call(body, "pack", ins=ins, outs=outs, scratch=[pltpu.VMEM((128, d), F32)])[0]


def piece_rounds(count, size):
    left = {}
    for g in range(count * size):
        left.setdefault((g // count, g % size), []).append(g)
    rounds = []
    for _ in range(count):
        match = {}

        def augment(u, seen):
            for v in range(size):
                if left.get((u, v)) and v not in seen:
                    seen.add(v)
                    if v not in match or augment(match[v], seen):
                        match[v] = u
                        return True
            return False

        for bit in range(size):
            if all(left.get((u, u ^ bit)) for u in range(size)):
                match.update({u ^ bit: u for u in range(size)})
                break
        else:
            for u in range(size):
                augment(u, set())
        chosen = {u: (v, left[(u, v)].pop(0)) for v, u in match.items()}
        rounds.append([chosen[u] for u in range(size)])
    return rounds


def erf_parts(u):
    size = jnp.abs(u) * np.float32(0.7071067811865476)
    bell = jnp.exp(-(size * size))
    t = pl.reciprocal(1.0 + np.float32(0.3275911) * size)
    poly = np.float32(1.061405429 * 0.5)
    for c in (-1.453152027, 1.421413741, -0.284496736, 0.254829592):
        poly = poly * t + np.float32(c * 0.5)
    tail = poly * t * bell
    return jnp.where(u < 0, tail, 1.0 - tail), bell * np.float32(0.3989422804014327)


def write_rows(values, out_refs, size, rows):
    for j in range(size):
        block = values[j * rows : (j + 1) * rows].astype(BF16)
        if j & 1:
            out_refs[0][j // 2] = block
        else:
            out_refs[1 + j // 2][...] = block


def partial_outs(size, rows, width):
    return [out_whole((size // 2, rows, width), BF16)] + [out_whole((rows, width), BF16)] * (size // 2)


def column(row, wide):
    one = jnp.broadcast_to(row.astype(F32), (128, row.shape[1])).T
    return one if wide == 128 else jnp.concatenate([one] * (wide // 128), axis=1)


def project_rows(blocks, codes, weights, biases, count):
    size = len(blocks)
    rows = blocks[0].shape[0] // count
    d = blocks[0].shape[1]
    width = weights[1].shape[1]
    total = 2 * count * rows

    def body(*refs):
        code_ref, qw_ref, kw_ref, vw_ref, b_ref, out_ref, x_out = refs[size:]
        bias = [b_ref[m : m + 1, :] for m in range(6)]
        for at in range(0, size, 2):
            x = jnp.concatenate([refs[at][...], refs[at + 1][...]], axis=0)
            spots = [(m, at + i) for i in range(2) for m in range(count)]
            for number, (m, i) in enumerate(spots):
                x_out[m, i] = x[number * rows : (number + 1) * rows]
            word = column(code_ref[at // 2] & 1, width)[:total] == 0.0

            def write(part, values):
                for number, (m, i) in enumerate(spots):
                    out_ref[m, i, :, part * width : (part + 1) * width] = values[number * rows : (number + 1) * rows]

            for part, (first, second) in enumerate(((0, 2), (1, 3))):
                one = nn(x, qw_ref[first]) + bias[first]
                two = nn(x, qw_ref[second]) + bias[second]
                write(part, jnp.where(word, one, two).astype(BF16))
            for part, ref, m in ((2, kw_ref, 4), (3, vw_ref, 5)):
                write(part, (nn(x, ref[...]) + bias[m]).astype(BF16))

    ins = [whole(b) for b in blocks] + [whole(codes)]
    ins += [whole(w) for w in weights] + [whole(biases)]
    outs = [out_whole((count, size, rows, wide), BF16) for wide in (4 * width, d)]
    return call(body, "project_rows", vmem=LARGE, weight=10, ins=ins, outs=outs)


def relay(blocks):
    rows, d = blocks[0].shape
    n = len(blocks)

    def body(*refs):
        for m in range(n):
            refs[-1][m] = refs[m][...]

    return call(body, "relay", ins=[whole(b) for b in blocks], outs=[out_whole((n, rows, d), BF16)])[0]


def again(array):
    def body(in_ref, out_ref):
        out_ref[...] = in_ref[...]

    return call(body, "again", ins=[whole(array)], outs=[out_whole(array.shape, array.dtype)])[0]


def head_views(piece_refs, part, pair, width):
    start = part * width + pair * 128
    return jnp.concatenate([r[0, :, start : start + 128] for r in piece_refs], axis=0)


def swap_lanes(values):
    return pltpu.roll(values.astype(F32), 64, 1)


def extended(piece_refs, pair, width, takes, left):
    qw = head_views(piece_refs, 0, pair, width)
    qe = head_views(piece_refs, 1, pair, width)
    k = head_views(piece_refs, 2, pair, width)
    v = head_views(piece_refs, 3, pair, width)
    qw32, qe32, k32 = qw.astype(F32), qe.astype(F32), k.astype(F32) * 0.125
    qw_s, qe_s, k_s = swap_lanes(qw32), swap_lanes(qe32), swap_lanes(k32)
    q_ext = (
        jnp.where(left, qw32, qe_s).astype(BF16),
        jnp.where(left, qw_s, qe32).astype(BF16),
    )
    k_ext = (
        jnp.where(takes, jnp.where(left, k32, k_s), 0.0).astype(BF16),
        jnp.where(takes, jnp.where(left, k_s, k32), 0.0).astype(BF16),
    )
    return q_ext, k_ext, v


def query_blocks(length):
    spans, at = [], 0
    while at < length:
        step = 256 if length - at >= 256 else length - at
        spans.append((at, step))
        at += step
    return spans


def attend(pieces, table, s, codes, out_proj, size, rows):
    length = size * rows
    width, d = out_proj.shape
    pairs = width // 128

    def body(table_ref, *refs):
        piece_refs = refs[:size]
        code_ref, wo_ref, c_ref, lse_ref = refs[size : size + 4]
        left = lax.broadcasted_iota(jnp.int32, (length, 128), 1) < 64
        code = code_ref[0]
        word = column(code & 1, 128) == 0.0
        takes = word == left
        segr = (code >> 1).astype(F32)
        segc = column(code >> 1, 256)
        for pair in range(pairs):
            q_ext, k_ext, v = extended(piece_refs, pair, width, takes, left)
            v_t = v.astype(F32).T.astype(BF16)
            for at, step in query_blocks(length):
                same = segc[:, :step] == segr[:, at : at + step]
                tops = []
                for h in range(2):
                    s_t = nt(k_ext[h], q_ext[h][at : at + step])
                    s_t = jnp.where(same, s_t, MASKED)
                    top = jnp.max(s_t, axis=0, keepdims=True)
                    e = jnp.exp(s_t - top)
                    total = jnp.sum(e, axis=0, keepdims=True)
                    o_t = nn(v_t[h * 64 : h * 64 + 64], e.astype(BF16))
                    tops.append(o_t * (1.0 / total))
                    lse_ref[2 * pair + h : 2 * pair + h + 1, at : at + step] = top + jnp.log(total)
                c = jnp.concatenate(tops, axis=0).T.astype(BF16)
                c_ref[at : at + step, pair * 128 : pair * 128 + 128] = c
        write_rows(nn(c_ref[...], wo_ref[...]), refs[-1 - size // 2 :], size, rows)

    ins = [
        (pieces, (1, rows, 4 * width), functools.partial(lambda j, _, t: (t[s * size + j], 0, 0), j))
        for j in range(size)
    ]
    ins += [
        (codes, (1, 1, length), lambda *_: (s, 0, 0)),
        whole(out_proj),
    ]
    outs = [out_whole((length, width), BF16), out_whole((8, length), F32)]
    outs += partial_outs(size, rows, d)
    return call(
        body, "attend", vmem=LARGE, weight=7, prefetch=(table,), ins=ins, outs=outs,
    )


def attend_back(pieces, table, s, codes, out_proj, context, lse, delta_blocks, buffers, sums, count):
    size = len(delta_blocks)
    rows, d = delta_blocks[0][0].shape[1:]
    length = size * rows
    width = out_proj.shape[0]
    pairs = width // 128

    def body(table_ref, *refs):
        piece_refs = refs[:size]
        delta_refs = refs[size : 2 * size]
        code_ref, wo_ref, c_ref, lse_ref = refs[2 * size : 2 * size + 4]
        n_out = 5
        tail = refs[2 * size + 4 :]
        sum_in = tail[0] if sums is not None else None
        first_out, second_out, delta_out, wo_grad, bias_out, first_all, second_all = tail[-(n_out + 2) :]
        step_at = pl.program_id(0)

        @pl.when(step_at == 0)
        def _():
            left = lax.broadcasted_iota(jnp.int32, (length, 128), 1) < 64
            code = code_ref[0]
            word = column(code & 1, 128) == 0.0
            takes = word == left
            segr = (code >> 1).astype(F32)
            segc = column(code >> 1, 256)
            delta = jnp.concatenate([r[0] for r in delta_refs], axis=0)
            c_all = c_ref[...]
            grad = nn(c_all.astype(F32).T.astype(BF16), delta)
            wo_grad[...] = grad if sum_in is None else grad + sum_in[...]
            for pair in range(pairs):
                dc = nt(delta, wo_ref[pair * 128 : pair * 128 + 128, :]).astype(BF16)
                q_ext, k_ext, v = extended(piece_refs, pair, width, takes, left)
                k_ext_t = [k.astype(F32).T.astype(BF16) for k in k_ext]
                dc32 = dc.astype(F32)
                dc_h = (jnp.where(left, dc32, 0.0).astype(BF16), jnp.where(left, 0.0, dc32).astype(BF16))
                dv = jnp.zeros((length, 128), F32)
                dk = [jnp.zeros((length, 128), F32)] * 2
                dq = [[], []]
                for at, step in query_blocks(length):
                    same = segc[:, :step] == segr[:, at : at + step]
                    for h in range(2):
                        q_b, dc_b = q_ext[h][at : at + step], dc_h[h][at : at + step]
                        row = 2 * pair + h
                        s_t = nt(k_ext[h], q_b)
                        p = jnp.where(same, jnp.exp(s_t - lse_ref[row : row + 1, at : at + step]), 0.0)
                        dp = nt(v, dc_b)
                        row_inner = jnp.sum(p * dp, axis=0, keepdims=True)
                        ds = (p * (dp - row_inner)).astype(BF16)
                        dv = dv + nn(p.astype(BF16), dc_b)
                        dk[h] = dk[h] + nn(ds, q_b)
                        dq[h].append(nn(k_ext_t[h], ds).T)
                dq0, dq1 = (jnp.concatenate(parts, axis=0) for parts in dq)
                dqw = jnp.where(left, dq0, swap_lanes(dq1))
                dqe = jnp.where(left, swap_lanes(dq0), dq1)
                dk0, dk1 = dk[0] * 0.125, dk[1] * 0.125
                dk_pair = jnp.where(takes, jnp.where(left, dk0, dk1), jnp.where(left, swap_lanes(dk0), swap_lanes(dk1)))
                outs = (
                    jnp.where(word, dqw, 0.0), jnp.where(word, dqe, 0.0), jnp.where(word, 0.0, dqw),
                    jnp.where(word, 0.0, dqe), dk_pair, dv,
                )
                for number, values in enumerate(outs):
                    rounded = values.astype(BF16)
                    target = (first_all, second_all)[number // 4]
                    start = (number % 4) * width + pair * 128
                    target[:, start : start + 128] = rounded
                    bias_out[number : number + 1, pair * 128 : pair * 128 + 128] = jnp.sum(
                        rounded.astype(F32), axis=0, keepdims=True
                    )

        at_rows = pl.ds(pl.multiple_of(step_at * rows, 16), rows)
        first_out[0] = first_all[at_rows, :]
        second_out[0] = second_all[at_rows, :]
        for j in range(size):

            @pl.when(step_at == j)
            def _():
                delta_out[0] = delta_refs[j][0]

    ins = [
        (pieces, (1, rows, 4 * width), functools.partial(lambda j, _, t: (t[s * size + j], 0, 0), j))
        for j in range(size)
    ]
    ins += block_specs(delta_blocks)
    ins += [
        (codes, (1, 1, length), lambda *_: (s, 0, 0)),
        whole(out_proj),
        whole(context),
        whole(lse),
    ]
    if sums is not None:
        ins.append(whole(sums))
    aliases = {}
    if buffers is not None:
        for number, b in enumerate(buffers):
            aliases[len(ins)] = number
            ins.append((b, None, None))
    spot = lambda m, t: (t[s * size + m], 0, 0)
    outs = [
        ((count * size, rows, 4 * width), BF16, (1, rows, 4 * width), spot),
        ((count * size, rows, 2 * width), BF16, (1, rows, 2 * width), spot),
        ((count * size, rows, d), BF16, (1, rows, d), spot),
        out_whole((width, d), F32),
        out_whole((8, width), F32),
    ]
    return call(
        body, "attend_back", vmem=LARGE, grid=(size,), prefetch=(table,), ins=ins, outs=outs, aliases=aliases,
        scratch=[pltpu.VMEM((length, 4 * width), BF16), pltpu.VMEM((length, 2 * width), BF16)],
    )


def add_up(refs):
    total = refs[0][0].astype(F32)
    for r in refs[1:]:
        total = total + r[0].astype(F32)
    return total


def normed(values):
    centre = jnp.mean(values, axis=-1, keepdims=True)
    offset = values - centre
    spread = jnp.mean(offset * offset, axis=-1, keepdims=True)
    rstd = lax.rsqrt(spread + NORM_EPS)
    return offset * rstd, rstd


def norm_pull(upstream, n, rstd, gain):
    scaled = upstream * gain
    inner = jnp.mean(scaled, axis=-1, keepdims=True)
    cross = jnp.mean(scaled * n, axis=-1, keepdims=True)
    return rstd * (scaled - inner - n * cross)


def column_sum(values):
    return jnp.sum(values, axis=0, keepdims=True)


def inner_norm(addends, x_pieces, table, s, bias, gain, shift, size):
    rows, d = addends[0].shape[1:]
    n_add = len(addends)

    def body(table_ref, *refs):
        x_ref, b_ref, g_ref, h_ref, y_ref, n_ref, rstd_ref = refs[n_add:]
        r = add_up(refs[:n_add]) + b_ref[...] + x_ref[0].astype(F32)
        n, rstd = normed(r)
        n_ref[...] = n
        rstd_ref[...] = jnp.broadcast_to(rstd, (rows, 128))
        y_ref[...] = (n * g_ref[...] + h_ref[...]).astype(BF16)

    ins = addend_specs(addends)
    ins.append((x_pieces, (1, rows, d), lambda _, t: (t[s * size], 0, 0)))
    ins += [whole(bias), whole(gain), whole(shift)]
    outs = [out_whole((rows, d), BF16), out_whole((rows, d), F32), out_whole((rows, 128), F32)]
    return call(body, "inner_norm", weight=5, prefetch=(table,), ins=ins, outs=outs)


def outer_norm(addends, n1, inner_gain, inner_shift, bias, gain, shift, cotangents, spots, buffer, s, count):
    rows, d = addends[0].shape[1:]
    n_add = len(addends)

    def body(spots_ref, *refs):
        n1_ref, g1_ref, h1_ref, b_ref, g_ref, h_ref, e_ref = refs[n_add : n_add + 7]
        res_ref, dz_ref, dzb_ref, sums_ref = refs[-4:]
        z = add_up(refs[:n_add]) + b_ref[...] + (n1_ref[...] * g1_ref[...] + h1_ref[...])
        n, rstd = normed(z)
        res_ref[0] = n * g_ref[...] + h_ref[...]
        e = e_ref[0].astype(F32)
        dz = norm_pull(e, n, rstd, g_ref[...])
        dz_ref[...] = dz
        dzb_ref[...] = dz.astype(BF16)
        sums_ref[0:1] = column_sum(dz)
        sums_ref[1:2] = column_sum(e * n)
        sums_ref[2:3] = column_sum(e)

    ins = addend_specs(addends)
    ins += [whole(a) for a in (n1, inner_gain, inner_shift, bias, gain, shift)]
    ins.append((cotangents, (1, rows, d), lambda _, t: (t[s], 0, 0)))
    aliases = {}
    if buffer is not None:
        aliases[len(ins)] = 0
        ins.append((buffer, None, None))
    outs = [
        ((count, rows, d), F32, (1, rows, d), lambda *_: (s, 0, 0)),
        out_whole((rows, d), F32),
        out_whole((rows, d), BF16),
        out_whole((8, d), F32),
    ]
    return call(
        body, "outer_norm", weight=5, prefetch=(spots,), ins=ins, outs=outs, aliases=aliases,
    )


def inner_norm_back(addends, dz, n1, rstd1, gain):
    rows, d = addends[0].shape[1:]
    n_add = len(addends)

    def body(*refs):
        dz_ref, n_ref, rstd_ref, g_ref, dr_ref, sums_ref = refs[n_add:]
        da = add_up(refs[:n_add]) + dz_ref[...]
        n = n_ref[...]
        dr = norm_pull(da, n, rstd_ref[:, 0:1], g_ref[...])
        dr_ref[...] = dr.astype(BF16)
        sums_ref[0:1] = column_sum(dr)
        sums_ref[1:2] = column_sum(da * n)
        sums_ref[2:3] = column_sum(da)

    ins = addend_specs(addends) + [whole(a) for a in (dz, n1, rstd1, gain)]
    outs = [out_whole((rows, d), BF16), out_whole((8, d), F32)]
    return call(body, "inner_norm_back", weight=5, ins=ins, outs=outs)


def feed_forward(blocks, expand, expand_bias, contract, buffers, s, count):
    size = len(blocks)
    rows, d = blocks[0][0].shape[1:]
    hidden = expand.shape[1]
    length = size * rows
    tile = min(256, hidden)

    def body(*refs):
        y_refs = refs[:size]
        we_ref, be_ref, wc_ref = refs[size : size + 3]
        n_partial = 1 + size // 2
        y_out, g_out, slope_out = refs[-3 - n_partial : -n_partial]
        y = jnp.concatenate([r[0] for r in y_refs], axis=0)
        y_out[0] = y
        for at in range(0, hidden, tile):
            cols = slice(at, at + tile)
            u = nn(y, we_ref[:, cols]) + be_ref[:, cols]
            phi_sum, phi = erf_parts(u)
            g_out[0, :, cols] = (u * phi_sum).astype(BF16)
            slope_out[0, :, cols] = (phi_sum + u * phi).astype(BF16)
        write_rows(nn(g_out[0], wc_ref[...]), refs[-n_partial:], size, rows)

    ins = block_specs(blocks) + [whole(a) for a in (expand, expand_bias, contract)]
    aliases = {}
    if buffers is not None:
        for number, b in enumerate(buffers):
            aliases[len(ins)] = number
            ins.append((b, None, None))
    outs = [
        ((count, length, w), BF16, (1, length, w), lambda *_: (s, 0, 0)) for w in (d, hidden, hidden)
    ] + partial_outs(size, rows, d)
    return call(
        body, "feed_forward", vmem=LARGE, weight=7, ins=ins, outs=outs, aliases=aliases,
    )


def feed_back(blocks, expand, contract, slopes, buffers, s, count):
    size = len(blocks)
    rows, d = blocks[0][0].shape[1:]
    hidden = expand.shape[1]
    length = size * rows
    tile = min(256, hidden)

    def body(*refs):
        dz_refs = refs[:size]
        we_ref, wc_ref, slope_ref = refs[size : size + 3]
        n_partial = 1 + size // 2
        sums_ref, dz_out, du_out = refs[-3 - n_partial : -n_partial]
        dz = jnp.concatenate([r[0] for r in dz_refs], axis=0)
        dz_out[0] = dz
        for at in range(0, hidden, tile):
            cols = slice(at, at + tile)
            du = (nt(dz, wc_ref[cols, :]) * slope_ref[0, :, cols].astype(F32)).astype(BF16)
            du_out[0, :, cols] = du
            sums_ref[:, cols] = column_sum(du.astype(F32))
        write_rows(nt(du_out[0], we_ref[...]), refs[-n_partial:], size, rows)

    ins = block_specs(blocks) + [whole(expand), whole(contract)]
    ins.append((slopes, (1, length, hidden), lambda *_: (s, 0, 0)))
    aliases = {}
    if buffers is not None:
        for number, b in enumerate(buffers):
            aliases[len(ins)] = 1 + number
            ins.append((b, None, None))
    outs = [out_whole((1, hidden), F32)]
    outs += [((count, length, w), BF16, (1, length, w), lambda *_: (s, 0, 0)) for w in (d, hidden)]
    outs += partial_outs(size, rows, d)
    return call(
        body, "feed_back", vmem=LARGE, weight=6, ins=ins, outs=outs, aliases=aliases,
    )


def input_back(first, second, weights, size, count):
    rows = first.shape[1]
    d = weights[1].shape[0]
    width = weights[1].shape[1]

    def body(*refs):
        a_ref, b_ref, qw_ref, kw_ref, vw_ref = refs[:5]
        a = jnp.concatenate([a_ref[j] for j in range(size)], axis=0)
        b = jnp.concatenate([b_ref[j] for j in range(size)], axis=0)
        total = nt(a[:, :width], qw_ref[0])
        for m in (1, 2, 3):
            total = total + nt(a[:, m * width : (m + 1) * width], qw_ref[m])
        total = total + nt(b[:, :width], kw_ref[...])
        total = total + nt(b[:, width:], vw_ref[...])
        write_rows(total, refs[5:], size, rows)

    ins = [(a, (size, rows, a.shape[2]), lambda k: (k, 0, 0)) for a in (first, second)]
    ins += [whole(w) for w in weights]
    outs = [((size // 2, count * rows, d), BF16, (size // 2, rows, d), lambda k: (0, k, 0))]
    outs += [((count * rows, d), BF16, (rows, d), lambda k: (k, 0)) for _ in range(size // 2)]
    return call(body, "input_back", vmem=LARGE, grid=(count,), ins=ins, outs=outs)


def take(array, spots, dtypes):
    rows, d = array.shape[1:]

    def body(spots_ref, in_ref, *out_refs):
        for m, out_ref in enumerate(out_refs):
            out_ref[...] = in_ref[spots_ref[m]].astype(out_ref.dtype)

    outs = [out_whole((rows, d), dtype) for dtype in dtypes]
    return call(body, "take", prefetch=(spots,), ins=[whole(array)], outs=outs)


def put(blocks, spots):
    rows, d = blocks[0].shape
    n = len(blocks)

    def body(spots_ref, *refs):
        for m in range(n):
            refs[-1][pl.ds(pl.multiple_of(spots_ref[m] * rows, 16), rows), :] = refs[m][...].astype(F32)

    ins = [whole(b) for b in blocks]
    return call(body, "put", prefetch=(spots,), ins=ins, outs=[out_whole((n * rows, d), F32)])[0]


def collect(blocks):
    rows, d = blocks[0].shape

    def body(*refs):
        for m in range(len(blocks)):
            refs[-1][m] = refs[m][...]

    outs = [out_whole((len(blocks), rows, d), BF16)]
    return call(body, "collect", ins=[whole(b) for b in blocks], outs=outs)[0]


def final_sum(addends, dr_pieces, size, count):
    rows, d = dr_pieces.shape[1:]

    def body(*refs):
        refs[-1][...] = add_up(refs[:-1])

    ins = [(a, (1, rows, d), lambda k: (0, k, 0)) for a in addends]
    ins.append((dr_pieces, (1, rows, d), lambda k: (k * size, 0, 0)))
    outs = [((count * rows, d), F32, (rows, d), lambda k: (k, 0))]
    return call(body, "final_sum", grid=(count,), ins=ins, outs=outs)[0]


def across(array, rows):
    d, n = array.shape[1:]

    def body(in_ref, one_ref, two_ref):
        turned = in_ref[0].T
        one_ref[0] = turned[:rows]
        two_ref[...] = turned[rows:]

    outs = [out_whole((1, rows, d), F32), out_whole((n - rows, d), F32)]
    return call(body, "across", ins=[whole(array)], outs=outs)


def body(
    dp, tensor, tokens, token_kinds, segment_ids, cotangent, query_weight, query_bias, key_weight, key_bias,
    value_weight, value_bias, output_weight, output_bias, inner_gain, inner_shift, expand_weight, expand_bias,
    contract_weight, contract_bias, outer_gain, outer_shift,
):
    count, length = token_kinds.shape
    d = tokens.shape[1]
    rows = length // tensor
    me = lax.axis_index("tensor")
    width = key_weight.shape[2]
    hidden = expand_weight.shape[2]

    devices = np.arange(tensor)
    piece_at = np.array(
        [[[o * count + k for o in devices ^ r] for k in range(count)] for r in range(tensor)], np.int32
    )
    seq_piece = np.array(
        [[[s * tensor + b for b in devices ^ r] for s in range(count)] for r in range(tensor)], np.int32
    )
    table_of = np.array(
        [[(g % count) * tensor + ((g // count) ^ r) for g in seq_piece[r].reshape(-1)] for r in range(tensor)], np.int32
    )
    pick = lambda values: lax.dynamic_index_in_dim(jnp.asarray(values), me, 0, keepdims=False)
    table = pick(table_of)
    codes = (segment_ids * 2 + token_kinds).reshape(count * tensor, rows)
    lie = piece_at.transpose(0, 2, 1).reshape(tensor, -1)
    codes = codes[pick(np.concatenate([lie, seq_piece.reshape(tensor, -1)], axis=1))]
    lie_codes = codes[: count * tensor].reshape(tensor // 2, 1, -1)
    lie_codes = jnp.pad(lie_codes, ((0, 0), (0, 0), (0, -lie_codes.shape[2] % 128)))
    seq_codes = codes[count * tensor :].reshape(count, 1, length)

    weights = (query_weight[0], key_weight[0], value_weight[0])
    biases = jnp.concatenate([query_bias[0], key_bias, value_bias], axis=0).astype(F32)
    expand, contract = expand_weight[0], contract_weight[0]
    expand_bias32 = expand_bias.astype(F32)
    out_proj = output_weight[0]
    Order.mark, Order.weight = None, 0.2

    rounds = piece_rounds(count, tensor)
    perms = [[(u, v) for u, (v, _) in enumerate(chosen)] for chosen in rounds]
    stays = [all(u == v for u, v in perm) for perm in perms]
    sends = np.array([[chosen[u][1] % count for chosen in rounds] for u in range(tensor)], np.int32)
    spots_of = np.zeros((tensor, count), np.int32)
    for number, chosen in enumerate(rounds):
        for v, g in chosen:
            spots_of[v, g // tensor] = number
    spots = pick(spots_of)
    arrived = [
        block if stay else lax.ppermute(block, "tensor", perm)
        for block, stay, perm in zip(
            take(cotangent.reshape(count, rows, d), pick(sends), [BF16] * count), stays, perms, strict=True
        )
    ]
    held = {0: tokens}
    for bit in range(1, tensor.bit_length() - 1):
        for j in sorted(held):
            held[j | 1 << bit] = swap(held[j], "tensor", tensor, 1 << bit)
    for j in range(0, tensor, 2):
        held[j | 1] = swap(held[j], "tensor", tensor, 1)
    pieces = project_rows([held[j] for j in range(tensor)], lie_codes, weights, biases, count)
    qkv, x_pieces = (a.reshape(count * tensor, rows, -1) for a in pieces)

    hold = {"cotangents": collect(arrived)}

    def run_attend(s):
        hold["context", s], hold["lse", s], *partial = attend(qkv, table, s, seq_codes, out_proj, tensor, rows)
        return partial

    def finish_attend(s):
        y, hold["n1", s], hold["rstd1", s] = inner_norm(
            hold["addends", s], x_pieces, table, s, output_bias, inner_gain, inner_shift, tensor
        )
        hold["y", s] = gather_start(y, tensor)

    def run_forward(s):
        out = feed_forward(hold["y", s], expand, expand_bias32, contract, hold.get("kept"), s, count)
        hold["kept"] = out[:3]
        return out[3:]

    def finish_forward(s):
        hold["results"], hold["dz", s], dzb, hold["outer", s] = outer_norm(
            hold["addends", s], hold["n1", s], inner_gain, inner_shift, contract_bias, outer_gain, outer_shift,
            hold["cotangents"], spots, hold.get("results"), s, count,
        )
        hold["dzb", s] = gather_start(dzb, tensor)

    def run_back(s):
        out = feed_back(hold["dzb", s], expand, contract, hold["kept"][2], hold.get("back"), s, count)
        hold["expand_bias", s], hold["back"] = out[0], out[1:3]
        return out[3:]

    def finish_back(s):
        drb, hold["inner", s] = inner_norm_back(
            hold["addends", s], hold["dz", s], hold["n1", s], hold["rstd1", s], inner_gain
        )
        hold["drb", s] = gather_start(drb, tensor)

    shapes = [(4, d, width), (1, d, width), (1, d, width), (1, d, width + 128), (1, d, hidden), (1, hidden, d)]
    grads = {}
    flat = lambda a: a.reshape(-1, a.shape[-1])
    bits = list(range(dp.bit_length() - 1))
    swapped = bits[1::-1] + bits[2:]
    orders = {name: swapped if name in SWAPPED else bits for name in "ceab"}

    def sum_over_dp(name, halves, order, layout):
        sums[name] = DpSum([(halves, order, layout)], dp, grads, shapes, name)

    sums = {}

    stages = [(run_attend, finish_attend, "y"), (run_forward, finish_forward, "dzb"), (run_back, finish_back, "drb")]
    runs = [(*one, s) for one in stages for s in range(count)]
    finished, complete = set(), set()

    def finish(i):
        if i not in finished:
            finished.add(i)
            runs[i][1](runs[i][3])

    def bring(i):
        if i not in complete:
            finish(i)
            complete.add(i)
            key = runs[i][2], runs[i][3]
            hold[key] = gather_end(hold[key], tensor)

    for i, (run, _, _, s) in enumerate(runs):
        if i >= count:
            bring(i - count)
        send, *keeps = run(s)
        received = swap(send, "tensor", tensor, 1)
        if i >= 2:
            bring(i - 2)
        if i >= 1:
            finish(i - 1)
        hold["addends", s] = scatter_rest(keeps, received, tensor)
    y_all, du_all = hold["kept"][0], hold["back"][1]

    def steps(names):
        for name in names:
            one = sums[{"c": "contract", "e": "expand", "a": "first", "b": "second"}[name]]
            if one.at < one.steps:
                one.step()

    returns, lands = np.zeros((tensor, count), np.int32), np.zeros((tensor, count), np.int32)
    for number, chosen in enumerate(rounds):
        for u, (v, g) in enumerate(chosen):
            returns[v, number], lands[u, number] = g // tensor, g % count

    kept, output_sum = None, None
    x_flat = flat(x_pieces)
    runs_back = list(range(count))
    for token in AFTER:
        name, _, weight = token.partition(":")
        Order.weight = float(weight or 0.2)
        if name == "attend":
            s = runs_back.pop(0)
            bring(2 * count + s)
            *kept, output_sum, hold["bias", s] = attend_back(
                qkv, table, s, seq_codes, out_proj, hold["context", s], hold["lse", s], hold["drb", s], kept,
                output_sum, count,
            )
            first, second, dr_pieces = kept
        elif name in ("near1", "near2"):
            bring(2 * count + int(name[-1]))
        elif name == "norm":
            finish(3 * count - 1)
        elif name == "norms":
            norms = norm_sums([hold["outer", s] for s in range(count)], [hold["inner", s] for s in range(count)])
            came = swap(norms, "tensor", tensor, 1)
        elif name == "add":
            for bit in range(1, tensor.bit_length() - 1):
                norms = add(norms, came)
                came = swap(norms, "tensor", tensor, 1 << bit)
        elif name == "Gc":
            halves = weight_grad(flat(hold["kept"][1]), flat(hold["back"][0]), orders["c"][0], "contract_grad")
            sum_over_dp("contract", halves, orders["c"], [(5, (0, 1), 0, d, 0)])
        elif name == "Ge":
            halves = weight_grad(flat(y_all), flat(du_all), orders["e"][0], "expand_grad")
            sum_over_dp("expand", halves, orders["e"], [(4, (0, 1), 0, hidden, 0)])
        elif name == "Ga":
            halves = weight_grad(x_flat, flat(first), orders["a"][0], "first_grad")
            sum_over_dp("first", halves, orders["a"], [(0, (0, 4), 0, width, 0)])
        elif name == "Gb":
            sums_of = lambda key: [hold[key, s] for s in range(count)]
            more = pack(output_sum, norms, came, sums_of("expand_bias"), sums_of("bias"))
            halves = weight_grad(x_flat, flat(second), orders["b"][0], "second_grad", more)
            layout = [(1, (0, 1), 0, width, 0), (2, (0, 1), width, width, 0), (3, (0, 1), 2 * width, width + 128, 0)]
            sum_over_dp("second", halves, orders["b"], layout)
        elif name == "in":
            send, *keeps = input_back(first, second, weights, tensor, count)
        elif name == "send":
            received = swap(again(send), "tensor", tensor, 1)
        elif name == "sum":
            addends = scatter_rest(keeps, received, tensor)
        elif name == "end":
            upstream = final_sum(addends, dr_pieces, tensor, count)
        elif name == "take":
            blocks = take(hold["results"], pick(returns), [F32 if stay else BF16 for stay in stays])
            blocks = [
                block if stay else lax.ppermute(block, "tensor", [(v, u) for u, v in perm])
                for block, stay, perm in zip(blocks, stays, perms, strict=True)
            ]
        elif name == "put":
            hold["result"] = put(blocks, pick(lands))
        else:
            steps(name)
    Order.weight = 0.2
    for one in sums.values():
        while one.at < one.steps:
            one.step()

    output_grad, small = across(grads[3], width)
    return (
        hold["result"],
        upstream,
        grads[0][None],
        small[None, 7:11, :width],
        grads[1],
        small[11:12, :width],
        grads[2],
        small[12:13, :width],
        output_grad,
        small[3:4],
        small[4:5],
        small[5:6],
        grads[4],
        small[6:7, :hidden],
        grads[5],
        small[0:1],
        small[1:2],
        small[2:3],
    )


def solution(mesh):
    rows, both = P("dp", None), P(("dp", "tensor"), None)
    columns = lambda dims: P(*[None] * (dims - 1), "tensor")
    down = P(None, "tensor", None)
    weight_specs = [columns(4), columns(3), columns(3), columns(2), columns(3), columns(2), down]
    ffn_specs = [columns(3), columns(2), down]
    return jax.shard_map(
        functools.partial(body, mesh.shape["dp"], mesh.shape["tensor"]),
        mesh=mesh,
        in_specs=(both, rows, rows, both, *weight_specs, P(), P(), P(), *ffn_specs, P(), P(), P()),
        out_specs=(both, both, *weight_specs, P(), P(), P(), *ffn_specs, P(), P(), P()),
        check_vma=False,
    )
```

```python
import functools

import jax
import jax.numpy as jnp
import numpy as np
from jax import lax
from jax.experimental import pallas as pl
from jax.experimental.pallas import tpu as pltpu
from jax.sharding import PartitionSpec as P

HD = 64
NORM_EPS = 1e-05
MASKED = -1e30
F32 = jnp.float32
BF16 = jnp.bfloat16
SMALL, LARGE = 6, 22
COST = 1.15e9
SWAPPED = "ea"
AFTER = (
    "Ge:2.5", "Gc:0.02", "near1", "attend:1", "norm:5", "norms:1", "attend:1", "c:0.02", "e:0.02", "near2:5", "take:2.5", "attend:1", "add:2.5", "Ga",
    "c:0.02", "e:2.5", "Gb", "in:1", "e:0.02", "c:2.5", "a:2.5", "b", "e:2.5", "a:0.02", "send:0.5", "c:2.5", "b:0.5", "put:0.02", "a:1", "b:1", "e:0.5", "c:0.02", "a:9", "b:0.02", "sum:1", "a:0.5", "e:1", "c:0.5", "b:0.5", "a:1", "end:0.5", "b:9",
)


def nn(a, b):
    return lax.dot_general(a, b, (((1,), (0,)), ((), ())), preferred_element_type=F32)


def nt(a, b):
    return lax.dot_general(a, b, (((1,), (1,)), ((), ())), preferred_element_type=F32)


def tn(a, b):
    return lax.dot_general(a, b, (((0,), (0,)), ((), ())), preferred_element_type=F32)


class Order:
    mark = None
    weight = 0.2


def call(body, name, *, grid=(1,), prefetch=(), ins, outs, aliases=None, scratch=(), weight=None, vmem=SMALL):
    def spec(block, index_map):
        if block is None:
            return pl.BlockSpec(memory_space=pl.ANY)
        return pl.BlockSpec(block, index_map, pipeline_mode=pl.Buffered(1) if grid == (1,) else None)

    shift = len(prefetch)
    marks = [] if Order.mark is None else [Order.mark]
    n_in, n_out = shift + len(ins), len(outs)

    def inner(*refs):
        given, rest = refs[:n_in], refs[n_in + len(marks) :]
        body(*given, *rest[:n_out], *rest[n_out + 1 :])

    in_specs = [spec(block, index_map) for _, block, index_map in ins]
    in_specs += [pl.BlockSpec(memory_space=pl.ANY) for _ in marks]
    out_specs = [spec(block, index_map) for _, _, block, index_map in outs]
    out_specs.append(pl.BlockSpec(memory_space=pl.ANY))
    shapes = [jax.ShapeDtypeStruct(shape, dtype) for shape, dtype, _, _ in outs]
    *results, Order.mark = pl.pallas_call(
        inner,
        grid_spec=pltpu.PrefetchScalarGridSpec(
            num_scalar_prefetch=shift,
            grid=grid,
            in_specs=in_specs,
            out_specs=out_specs,
            scratch_shapes=list(scratch),
        ),
        out_shape=[*shapes, jax.ShapeDtypeStruct((8, 128), F32)],
        input_output_aliases={shift + k: v for k, v in (aliases or {}).items()},
        compiler_params=pltpu.CompilerParams(vmem_limit_bytes=vmem * 1024 * 1024),
        cost_estimate=pl.CostEstimate(flops=int((Order.weight if weight is None else weight) * COST), bytes_accessed=1, transcendentals=0),
        name=name,
    )(*prefetch, *[array for array, _, _ in ins], *marks)
    return results


def whole(array):
    zeros = (0,) * array.ndim
    return (array, array.shape, lambda *_: zeros)


def out_whole(shape, dtype):
    zeros = (0,) * len(shape)
    return (shape, dtype, shape, lambda *_: zeros)


def swap(array, axis, size, bit):
    return lax.ppermute(array, axis, [(r, r ^ bit) for r in range(size)])


def gather_start(own, size):
    blocks = {0: own}
    bit = 2
    while bit < size:
        for j in sorted(blocks):
            blocks[j | bit] = swap(blocks[j], "tensor", size, bit)
        bit *= 2
    return blocks


def gather_end(blocks, size):
    even = relay([blocks[j] for j in range(0, size, 2)])
    odd = swap(even, "tensor", size, 1)
    return [((odd if j & 1 else even), j // 2) for j in range(size)]


def block_specs(blocks):
    return [
        (a, (1, *a.shape[1:]), functools.partial(lambda at, *_: (at, 0, 0), at)) for a, at in blocks
    ]


def combine(keep, received, m):
    rows, d = keep.shape

    def body(k_ref, r_ref, o_ref):
        o_ref[...] = (k_ref[...].astype(F32) + r_ref[0].astype(F32)).astype(BF16)

    ins = [whole(keep), (received, (1, rows, d), lambda *_: (m, 0, 0))]
    return call(body, "combine", ins=ins, outs=[out_whole((rows, d), BF16)])[0]


def scatter_rest(keeps, received, size):
    addends = [keeps[0][None], received]
    held = {2 * m: combine(keeps[m], received, m) for m in range(1, len(keeps))}
    bit = size // 2
    while bit >= 2:
        leaving = sorted(j for j in held if j & bit)
        arrived = [swap(held.pop(j), "tensor", size, bit) for j in leaving]
        addends.append(arrived[0][None])
        for j, block in zip(leaving[1:], arrived[1:], strict=True):
            held[j ^ bit] = combine(held[j ^ bit], block[None], 0)
        bit //= 2
    return addends


def addend_specs(addends):
    return [(a, (1,) + a.shape[1:], lambda *_: (0, 0, 0)) for a in addends]


def place_outs(state, shapes, layout, rows, spot_of, ins):
    outs, aliases = [], {}
    for number, (out, (lead, leads), _, wide, block) in enumerate(layout):
        index_map = functools.partial(lambda lead, block, m, spots: (lead, spot_of(m, spots), block), lead, block)
        outs.append((shapes[out], F32, (leads, rows, wide), index_map))
        if out in state:
            aliases[len(ins)] = number
            ins.append((state[out], None, None))
    return outs, aliases


def place_values(values, layout, out_refs):
    for (_, (_, leads), start, wide, _), out_ref in zip(layout, out_refs, strict=True):
        for lead in range(leads):
            at = start + lead * wide
            out_ref[lead] = values[:, at : at + wide].astype(F32)


class DpSum:
    def __init__(self, entries, size, state, shapes, name):
        self.size, self.name, self.state, self.shapes = size, name, state, shapes
        self.at = 0
        self.orders = [order for _, order, _ in entries]
        self.layouts = [layout for _, _, layout in entries]
        self.bits = len(entries[0][1])
        self.steps = 2 * self.bits
        here = lax.axis_index("dp")
        self.mine = [[(here >> bit) & 1 for bit in order] for order in self.orders]
        self.held = [0]
        self.staying = [halves[0] for halves, _, _ in entries]
        self.send([halves[1] for halves, _, _ in entries], 0)

    def scalars(self, values):
        return jnp.stack([jnp.asarray(v, jnp.int32) for v in values])

    def send(self, blocks, level):
        self.arrived = [
            swap(block, "dp", self.size, 1 << order[level]) for block, order in zip(blocks, self.orders, strict=True)
        ]

    def where(self, m, differs):
        spot = 0
        for level, mine in enumerate(self.mine[m]):
            spot = spot * 2 + (mine ^ ((differs >> level) & 1))
        return spot

    def step(self):
        if self.at < self.bits:
            self.halve()
        else:
            self.join()
        self.at += 1

    def placing(self, ins, rows, spot_of):
        outs, aliases = [], {}
        for m, layout in enumerate(self.layouts):
            index_of = functools.partial(spot_of, m)
            more, taken = place_outs(self.state, self.shapes, layout, rows[m], index_of, ins)
            aliases.update({k: v + len(outs) for k, v in taken.items()})
            outs += more
        return outs, aliases

    def keep_placed(self, got):
        names = [entry[0] for layout in self.layouts for entry in layout]
        self.state.update(dict(zip(names, got, strict=True)))

    def halve(self):
        level = self.at
        last = level == self.bits - 1
        n = len(self.staying)
        shapes = [a.shape for a in self.arrived]
        ends = np.cumsum([0] + [len(layout) for layout in self.layouts])

        def body(scalars_ref, *refs):
            outs = refs[2 * n :]
            for m in range(n):
                stay_ref, came_ref = refs[2 * m : 2 * m + 2]
                if last:
                    total = (stay_ref[...].astype(F32) + came_ref[...].astype(F32)).astype(BF16)
                    outs[len(outs) - n + m][...] = total
                    place_values(total, self.layouts[m], outs[len(outs) - n - ends[-1] :][ends[m] : ends[m + 1]])
                    continue
                half = shapes[m][0] // 2
                for out_ref, part in ((outs[2 * m], 1 - scalars_ref[m]), (outs[2 * m + 1], scalars_ref[m])):
                    at = pl.ds(pl.multiple_of(part * half, 16), half)
                    out_ref[...] = (stay_ref[at, :].astype(F32) + came_ref[at, :].astype(F32)).astype(BF16)

        ins = [whole(a) for pair in zip(self.staying, self.arrived, strict=True) for a in pair]
        if last:
            prefetch = self.scalars([self.where(m, 0) for m in range(n)])
            outs, aliases = self.placing(ins, [shape[0] for shape in shapes], lambda m, i, spots: spots[m])
            outs += [out_whole(shape, BF16) for shape in shapes]
        else:
            prefetch = self.scalars([mine[level + 1] for mine in self.mine])
            outs, aliases = [], {}
            for rows, columns in shapes:
                outs += [out_whole((rows // 2, columns), BF16)] * 2
        got = call(
            body, self.name + "_halve", prefetch=(prefetch,), ins=ins, outs=outs, aliases=aliases
        )
        if last:
            self.staying = got[len(got) - n :]
            self.keep_placed(got[: len(got) - n])
            self.send(self.staying, level)
        else:
            self.staying = got[1::2]
            self.send(got[0::2], level + 1)

    def join(self):
        level = self.steps - 1 - self.at
        count = len(self.held)
        came = [differs | (1 << level) for differs in self.held]
        self.held = self.held + came
        n = len(self.arrived)
        spots = self.scalars([self.where(m, differs) for m in range(n) for differs in came])
        rows = [a.shape[0] // count for a in self.arrived]
        ends = np.cumsum([0] + [len(layout) for layout in self.layouts])
        block = lambda i, spots: (i, 0)
        ins = [(a, (r, a.shape[1]), block) for a, r in zip(self.arrived, rows, strict=True)]
        if level:
            ins += [(a, (r, a.shape[1]), block) for a, r in zip(self.staying, rows, strict=True)]

        def body(spots_ref, *refs):
            joined = refs[len(refs) - n :] if level else ()
            placed = refs[len(refs) - len(joined) - ends[-1] : len(refs) - len(joined)]
            for m in range(n):
                values = refs[m][...]
                if level:
                    joined[m][0] = refs[n + m][...]
                    joined[m][1] = values
                place_values(values, self.layouts[m], placed[ends[m] : ends[m + 1]])

        outs, aliases = self.placing(ins, rows, lambda m, i, spots: spots[m * count + i])
        if level:
            for a, r in zip(self.arrived, rows, strict=True):
                outs.append(((2, *a.shape), BF16, (2, r, a.shape[1]), lambda i, spots: (0, i, 0)))
        got = call(
            body, self.name + "_join", grid=(count,), prefetch=(spots,), ins=ins, outs=outs, aliases=aliases
        )
        if level:
            self.staying = [a.reshape(-1, a.shape[2]) for a in got[len(got) - n :]]
            got = got[: len(got) - n]
            self.send(self.staying, level - 1)
        self.keep_placed(got)


def weight_grad(left_side, right_side, bit, name, more=None):
    tokens, total = left_side.shape
    columns = right_side.shape[1]
    half = total // 2

    def body(mine_ref, a_ref, b_ref, *refs):
        stay_ref, leave_ref = refs[-2:]
        product = tn(a_ref[...], b_ref[...]).astype(BF16)
        if more is not None:
            product = jnp.concatenate([product, refs[0][...]], axis=1)
        mine = pl.program_id(0) == mine_ref[0]

        @pl.when(mine)
        def _():
            stay_ref[...] = product

        @pl.when(jnp.logical_not(mine))
        def _():
            leave_ref[...] = product

    ins = [(left_side, (tokens, half), lambda i, mine: (0, i)), whole(right_side)]
    if more is not None:
        ins.append((more, (half, more.shape[1]), lambda i, mine: (i, 0)))
        columns += more.shape[1]
    outs = [out_whole((half, columns), BF16)] * 2
    mine = ((lax.axis_index("dp") >> bit) & 1).reshape(1).astype(jnp.int32)
    return call(body, name, vmem=LARGE, grid=(2,), prefetch=(mine,), ins=ins, outs=outs)


def add(one, two):
    def body(one_ref, two_ref, out_ref):
        out_ref[...] = one_ref[...] + two_ref[...]

    return call(body, "add", ins=[whole(one), whole(two)], outs=[out_whole(one.shape, F32)])[0]


def norm_sums(outer, inner):
    n, shape = len(outer), outer[0].shape

    def body(*refs):
        for at, group in ((0, refs[:n]), (3, refs[n : 2 * n])):
            total = group[0][0:3]
            for r in group[1:]:
                total = total + r[0:3]
            refs[-1][at : at + 3] = total
        refs[-1][6:8] = jnp.zeros((2, shape[1]), F32)

    ins = [whole(a) for a in (*outer, *inner)]
    return call(body, "norm_sums", ins=ins, outs=[out_whole(shape, F32)])[0]


def pack(output_sum, norms, came, expand_bias, bias):
    width, d = output_sum.shape
    hidden = expand_bias[0].shape[1]
    n = len(bias)

    def body(o_ref, norm_ref, came_ref, *refs):
        out_ref, rows_ref = refs[-2:]
        rows_ref[...] = jnp.zeros((128, d), F32)
        rows_ref[0:6] = norm_ref[0:6] + came_ref[0:6]
        total = refs[0][...]
        for r in refs[1:n]:
            total = total + r[...]
        rows_ref[6:7, :hidden] = total
        total = refs[n][0:6]
        for r in refs[n + 1 : 2 * n]:
            total = total + r[0:6]
        rows_ref[7:13, :width] = total
        out_ref[:, :width] = o_ref[...].T.astype(BF16)
        out_ref[:, width:] = rows_ref[...].T.astype(BF16)

    ins = [whole(a) for a in (output_sum, norms, came, *expand_bias, *bias)]
    outs = [out_whole((d, width + 128), BF16)]
    return call(body, "pack", ins=ins, outs=outs, scratch=[pltpu.VMEM((128, d), F32)])[0]


def piece_rounds(count, size):
    left = {}
    for g in range(count * size):
        left.setdefault((g // count, g % size), []).append(g)
    rounds = []
    for _ in range(count):
        match = {}

        def augment(u, seen):
            for v in range(size):
                if left.get((u, v)) and v not in seen:
                    seen.add(v)
                    if v not in match or augment(match[v], seen):
                        match[v] = u
                        return True
            return False

        for bit in range(size):
            if all(left.get((u, u ^ bit)) for u in range(size)):
                match.update({u ^ bit: u for u in range(size)})
                break
        else:
            for u in range(size):
                augment(u, set())
        chosen = {u: (v, left[(u, v)].pop(0)) for v, u in match.items()}
        rounds.append([chosen[u] for u in range(size)])
    return rounds


def erf_parts(u):
    size = jnp.abs(u) * np.float32(0.7071067811865476)
    bell = jnp.exp(-(size * size))
    t = pl.reciprocal(1.0 + np.float32(0.3275911) * size)
    poly = np.float32(1.061405429 * 0.5)
    for c in (-1.453152027, 1.421413741, -0.284496736, 0.254829592):
        poly = poly * t + np.float32(c * 0.5)
    tail = poly * t * bell
    return jnp.where(u < 0, tail, 1.0 - tail), bell * np.float32(0.3989422804014327)


def write_rows(values, out_refs, size, rows):
    for j in range(size):
        block = values[j * rows : (j + 1) * rows].astype(BF16)
        if j & 1:
            out_refs[0][j // 2] = block
        else:
            out_refs[1 + j // 2][...] = block


def partial_outs(size, rows, width):
    return [out_whole((size // 2, rows, width), BF16)] + [out_whole((rows, width), BF16)] * (size // 2)


def column(row, wide):
    one = jnp.broadcast_to(row.astype(F32), (128, row.shape[1])).T
    return one if wide == 128 else jnp.concatenate([one] * (wide // 128), axis=1)


def project_rows(blocks, codes, weights, biases, count, near=()):
    size = len(blocks)
    skip = near[0].shape[1] if near else 0
    rows = blocks[0].shape[0] // count
    d = blocks[0].shape[1]
    width = weights[1].shape[1]
    total = 2 * count * rows

    def body(*refs):
        code_ref, qw_ref, kw_ref, vw_ref, b_ref, *near_refs, out_ref, x_out = refs[size:]
        for near_ref, to in zip(near_refs, (out_ref, x_out)):
            to[:, :skip] = near_ref[...]
        bias = [b_ref[m : m + 1, :] for m in range(6)]
        for at in range(0, size, 2):
            x = jnp.concatenate([refs[at][...], refs[at + 1][...]], axis=0)
            spots = [(m, skip + at + i) for i in range(2) for m in range(count)]
            for number, (m, i) in enumerate(spots):
                x_out[m, i] = x[number * rows : (number + 1) * rows]
            word = column(code_ref[(skip + at) // 2] & 1, width)[:total] == 0.0

            def write(part, values):
                for number, (m, i) in enumerate(spots):
                    out_ref[m, i, :, part * width : (part + 1) * width] = values[number * rows : (number + 1) * rows]

            for part, (first, second) in enumerate(((0, 2), (1, 3))):
                one = nn(x, qw_ref[first]) + bias[first]
                two = nn(x, qw_ref[second]) + bias[second]
                write(part, jnp.where(word, one, two).astype(BF16))
            for part, ref, m in ((2, kw_ref, 4), (3, vw_ref, 5)):
                write(part, (nn(x, ref[...]) + bias[m]).astype(BF16))

    ins = [whole(b) for b in blocks] + [whole(codes)]
    ins += [whole(w) for w in weights] + [whole(biases)] + [whole(a) for a in near]
    outs = [out_whole((count, skip + size, rows, wide), BF16) for wide in (4 * width, d)]
    return call(body, "project_rows", vmem=LARGE, weight=5, ins=ins, outs=outs)


def relay(blocks):
    rows, d = blocks[0].shape
    n = len(blocks)

    def body(*refs):
        for m in range(n):
            refs[-1][m] = refs[m][...]

    return call(body, "relay", ins=[whole(b) for b in blocks], outs=[out_whole((n, rows, d), BF16)])[0]


def again(array):
    def body(in_ref, out_ref):
        out_ref[...] = in_ref[...]

    return call(body, "again", ins=[whole(array)], outs=[out_whole(array.shape, array.dtype)])[0]


def head_views(piece_refs, part, pair, width):
    start = part * width + pair * 128
    return jnp.concatenate([r[0, :, start : start + 128] for r in piece_refs], axis=0)


def swap_lanes(values):
    return pltpu.roll(values.astype(F32), 64, 1)


def extended(piece_refs, pair, width, takes, left):
    qw = head_views(piece_refs, 0, pair, width)
    qe = head_views(piece_refs, 1, pair, width)
    k = head_views(piece_refs, 2, pair, width)
    v = head_views(piece_refs, 3, pair, width)
    qw32, qe32, k32 = qw.astype(F32), qe.astype(F32), k.astype(F32) * 0.125
    qw_s, qe_s, k_s = swap_lanes(qw32), swap_lanes(qe32), swap_lanes(k32)
    q_ext = (
        jnp.where(left, qw32, qe_s).astype(BF16),
        jnp.where(left, qw_s, qe32).astype(BF16),
    )
    k_ext = (
        jnp.where(takes, jnp.where(left, k32, k_s), 0.0).astype(BF16),
        jnp.where(takes, jnp.where(left, k_s, k32), 0.0).astype(BF16),
    )
    return q_ext, k_ext, v


def query_blocks(length):
    spans, at = [], 0
    while at < length:
        step = 256 if length - at >= 256 else length - at
        spans.append((at, step))
        at += step
    return spans


def attend(pieces, table, s, codes, out_proj, size, rows):
    length = size * rows
    width, d = out_proj.shape
    pairs = width // 128

    def body(table_ref, *refs):
        piece_refs = refs[:size]
        code_ref, wo_ref, c_ref, lse_ref = refs[size : size + 4]
        left = lax.broadcasted_iota(jnp.int32, (length, 128), 1) < 64
        code = code_ref[0]
        word = column(code & 1, 128) == 0.0
        takes = word == left
        segr = (code >> 1).astype(F32)
        segc = column(code >> 1, 256)
        for pair in range(pairs):
            q_ext, k_ext, v = extended(piece_refs, pair, width, takes, left)
            v_t = v.astype(F32).T.astype(BF16)
            for at, step in query_blocks(length):
                same = segc[:, :step] == segr[:, at : at + step]
                tops = []
                for h in range(2):
                    s_t = nt(k_ext[h], q_ext[h][at : at + step])
                    s_t = jnp.where(same, s_t, MASKED)
                    top = jnp.max(s_t, axis=0, keepdims=True)
                    e = jnp.exp(s_t - top)
                    total = jnp.sum(e, axis=0, keepdims=True)
                    o_t = nn(v_t[h * 64 : h * 64 + 64], e.astype(BF16))
                    tops.append(o_t * (1.0 / total))
                    lse_ref[2 * pair + h : 2 * pair + h + 1, at : at + step] = top + jnp.log(total)
                c = jnp.concatenate(tops, axis=0).T.astype(BF16)
                c_ref[at : at + step, pair * 128 : pair * 128 + 128] = c
        write_rows(nn(c_ref[...], wo_ref[...]), refs[-1 - size // 2 :], size, rows)

    ins = [
        (pieces, (1, rows, 4 * width), functools.partial(lambda j, _, t: (t[s * size + j], 0, 0), j))
        for j in range(size)
    ]
    ins += [
        (codes, (1, 1, length), lambda *_: (s, 0, 0)),
        whole(out_proj),
    ]
    outs = [out_whole((length, width), BF16), out_whole((8, length), F32)]
    outs += partial_outs(size, rows, d)
    return call(
        body, "attend", vmem=LARGE, weight=7, prefetch=(table,), ins=ins, outs=outs,
    )


def attend_back(pieces, table, s, codes, out_proj, context, lse, delta_blocks, buffers, sums, count):
    size = len(delta_blocks)
    rows, d = delta_blocks[0][0].shape[1:]
    length = size * rows
    width = out_proj.shape[0]
    pairs = width // 128

    def body(table_ref, *refs):
        piece_refs = refs[:size]
        delta_refs = refs[size : 2 * size]
        code_ref, wo_ref, c_ref, lse_ref = refs[2 * size : 2 * size + 4]
        n_out = 5
        tail = refs[2 * size + 4 :]
        sum_in = tail[0] if sums is not None else None
        first_out, second_out, delta_out, wo_grad, bias_out, first_all, second_all = tail[-(n_out + 2) :]
        step_at = pl.program_id(0)

        @pl.when(step_at == 0)
        def _():
            left = lax.broadcasted_iota(jnp.int32, (length, 128), 1) < 64
            code = code_ref[0]
            word = column(code & 1, 128) == 0.0
            takes = word == left
            segr = (code >> 1).astype(F32)
            segc = column(code >> 1, 256)
            delta = jnp.concatenate([r[0] for r in delta_refs], axis=0)
            c_all = c_ref[...]
            grad = nn(c_all.astype(F32).T.astype(BF16), delta)
            wo_grad[...] = grad if sum_in is None else grad + sum_in[...]
            for pair in range(pairs):
                dc = nt(delta, wo_ref[pair * 128 : pair * 128 + 128, :]).astype(BF16)
                q_ext, k_ext, v = extended(piece_refs, pair, width, takes, left)
                k_ext_t = [k.astype(F32).T.astype(BF16) for k in k_ext]
                dc32 = dc.astype(F32)
                dc_h = (jnp.where(left, dc32, 0.0).astype(BF16), jnp.where(left, 0.0, dc32).astype(BF16))
                dv = jnp.zeros((length, 128), F32)
                dk = [jnp.zeros((length, 128), F32)] * 2
                dq = [[], []]
                for at, step in query_blocks(length):
                    same = segc[:, :step] == segr[:, at : at + step]
                    for h in range(2):
                        q_b, dc_b = q_ext[h][at : at + step], dc_h[h][at : at + step]
                        row = 2 * pair + h
                        s_t = nt(k_ext[h], q_b)
                        p = jnp.where(same, jnp.exp(s_t - lse_ref[row : row + 1, at : at + step]), 0.0)
                        dp = nt(v, dc_b)
                        row_inner = jnp.sum(p * dp, axis=0, keepdims=True)
                        ds = (p * (dp - row_inner)).astype(BF16)
                        dv = dv + nn(p.astype(BF16), dc_b)
                        dk[h] = dk[h] + nn(ds, q_b)
                        dq[h].append(nn(k_ext_t[h], ds).T)
                dq0, dq1 = (jnp.concatenate(parts, axis=0) for parts in dq)
                dqw = jnp.where(left, dq0, swap_lanes(dq1))
                dqe = jnp.where(left, swap_lanes(dq0), dq1)
                dk0, dk1 = dk[0] * 0.125, dk[1] * 0.125
                dk_pair = jnp.where(takes, jnp.where(left, dk0, dk1), jnp.where(left, swap_lanes(dk0), swap_lanes(dk1)))
                outs = (
                    jnp.where(word, dqw, 0.0), jnp.where(word, dqe, 0.0), jnp.where(word, 0.0, dqw),
                    jnp.where(word, 0.0, dqe), dk_pair, dv,
                )
                for number, values in enumerate(outs):
                    rounded = values.astype(BF16)
                    target = (first_all, second_all)[number // 4]
                    start = (number % 4) * width + pair * 128
                    target[:, start : start + 128] = rounded
                    bias_out[number : number + 1, pair * 128 : pair * 128 + 128] = jnp.sum(
                        rounded.astype(F32), axis=0, keepdims=True
                    )

        at_rows = pl.ds(pl.multiple_of(step_at * rows, 16), rows)
        first_out[0] = first_all[at_rows, :]
        second_out[0] = second_all[at_rows, :]
        for j in range(size):

            @pl.when(step_at == j)
            def _():
                delta_out[0] = delta_refs[j][0]

    ins = [
        (pieces, (1, rows, 4 * width), functools.partial(lambda j, _, t: (t[s * size + j], 0, 0), j))
        for j in range(size)
    ]
    ins += block_specs(delta_blocks)
    ins += [
        (codes, (1, 1, length), lambda *_: (s, 0, 0)),
        whole(out_proj),
        whole(context),
        whole(lse),
    ]
    if sums is not None:
        ins.append(whole(sums))
    aliases = {}
    if buffers is not None:
        for number, b in enumerate(buffers):
            aliases[len(ins)] = number
            ins.append((b, None, None))
    spot = lambda m, t: (t[s * size + m], 0, 0)
    outs = [
        ((count * size, rows, 4 * width), BF16, (1, rows, 4 * width), spot),
        ((count * size, rows, 2 * width), BF16, (1, rows, 2 * width), spot),
        ((count * size, rows, d), BF16, (1, rows, d), spot),
        out_whole((width, d), F32),
        out_whole((8, width), F32),
    ]
    return call(
        body, "attend_back", vmem=LARGE, grid=(size,), prefetch=(table,), ins=ins, outs=outs, aliases=aliases,
        scratch=[pltpu.VMEM((length, 4 * width), BF16), pltpu.VMEM((length, 2 * width), BF16)],
    )


def add_up(refs):
    total = refs[0][0].astype(F32)
    for r in refs[1:]:
        total = total + r[0].astype(F32)
    return total


def normed(values):
    centre = jnp.mean(values, axis=-1, keepdims=True)
    offset = values - centre
    spread = jnp.mean(offset * offset, axis=-1, keepdims=True)
    rstd = lax.rsqrt(spread + NORM_EPS)
    return offset * rstd, rstd


def norm_pull(upstream, n, rstd, gain):
    scaled = upstream * gain
    inner = jnp.mean(scaled, axis=-1, keepdims=True)
    cross = jnp.mean(scaled * n, axis=-1, keepdims=True)
    return rstd * (scaled - inner - n * cross)


def column_sum(values):
    return jnp.sum(values, axis=0, keepdims=True)


def inner_norm(addends, x_pieces, table, s, bias, gain, shift, size):
    rows, d = addends[0].shape[1:]
    n_add = len(addends)

    def body(table_ref, *refs):
        x_ref, b_ref, g_ref, h_ref, y_ref, n_ref, rstd_ref = refs[n_add:]
        r = add_up(refs[:n_add]) + b_ref[...] + x_ref[0].astype(F32)
        n, rstd = normed(r)
        n_ref[...] = n
        rstd_ref[...] = jnp.broadcast_to(rstd, (rows, 128))
        y_ref[...] = (n * g_ref[...] + h_ref[...]).astype(BF16)

    ins = addend_specs(addends)
    ins.append((x_pieces, (1, rows, d), lambda _, t: (t[s * size], 0, 0)))
    ins += [whole(bias), whole(gain), whole(shift)]
    outs = [out_whole((rows, d), BF16), out_whole((rows, d), F32), out_whole((rows, 128), F32)]
    return call(body, "inner_norm", weight=5, prefetch=(table,), ins=ins, outs=outs)


def outer_norm(addends, n1, inner_gain, inner_shift, bias, gain, shift, cotangents, spots, buffer, s, count):
    rows, d = addends[0].shape[1:]
    n_add = len(addends)

    def body(spots_ref, *refs):
        n1_ref, g1_ref, h1_ref, b_ref, g_ref, h_ref, e_ref = refs[n_add : n_add + 7]
        res_ref, dz_ref, dzb_ref, sums_ref = refs[-4:]
        z = add_up(refs[:n_add]) + b_ref[...] + (n1_ref[...] * g1_ref[...] + h1_ref[...])
        n, rstd = normed(z)
        res_ref[0] = n * g_ref[...] + h_ref[...]
        e = e_ref[0].astype(F32)
        dz = norm_pull(e, n, rstd, g_ref[...])
        dz_ref[...] = dz
        dzb_ref[...] = dz.astype(BF16)
        sums_ref[0:1] = column_sum(dz)
        sums_ref[1:2] = column_sum(e * n)
        sums_ref[2:3] = column_sum(e)

    ins = addend_specs(addends)
    ins += [whole(a) for a in (n1, inner_gain, inner_shift, bias, gain, shift)]
    ins.append((cotangents, (1, rows, d), lambda _, t: (t[s], 0, 0)))
    aliases = {}
    if buffer is not None:
        aliases[len(ins)] = 0
        ins.append((buffer, None, None))
    outs = [
        ((count, rows, d), F32, (1, rows, d), lambda *_: (s, 0, 0)),
        out_whole((rows, d), F32),
        out_whole((rows, d), BF16),
        out_whole((8, d), F32),
    ]
    return call(
        body, "outer_norm", weight=5, prefetch=(spots,), ins=ins, outs=outs, aliases=aliases,
    )


def inner_norm_back(addends, dz, n1, rstd1, gain):
    rows, d = addends[0].shape[1:]
    n_add = len(addends)

    def body(*refs):
        dz_ref, n_ref, rstd_ref, g_ref, dr_ref, sums_ref = refs[n_add:]
        da = add_up(refs[:n_add]) + dz_ref[...]
        n = n_ref[...]
        dr = norm_pull(da, n, rstd_ref[:, 0:1], g_ref[...])
        dr_ref[...] = dr.astype(BF16)
        sums_ref[0:1] = column_sum(dr)
        sums_ref[1:2] = column_sum(da * n)
        sums_ref[2:3] = column_sum(da)

    ins = addend_specs(addends) + [whole(a) for a in (dz, n1, rstd1, gain)]
    outs = [out_whole((rows, d), BF16), out_whole((8, d), F32)]
    return call(body, "inner_norm_back", weight=5, ins=ins, outs=outs)


def feed_forward(blocks, expand, expand_bias, contract, buffers, s, count):
    size = len(blocks)
    rows, d = blocks[0][0].shape[1:]
    hidden = expand.shape[1]
    length = size * rows
    tile = min(256, hidden)

    def body(*refs):
        y_refs = refs[:size]
        we_ref, be_ref, wc_ref = refs[size : size + 3]
        n_partial = 1 + size // 2
        y_out, g_out, slope_out = refs[-3 - n_partial : -n_partial]
        y = jnp.concatenate([r[0] for r in y_refs], axis=0)
        y_out[0] = y
        for at in range(0, hidden, tile):
            cols = slice(at, at + tile)
            u = nn(y, we_ref[:, cols]) + be_ref[:, cols]
            phi_sum, phi = erf_parts(u)
            g_out[0, :, cols] = (u * phi_sum).astype(BF16)
            slope_out[0, :, cols] = (phi_sum + u * phi).astype(BF16)
        write_rows(nn(g_out[0], wc_ref[...]), refs[-n_partial:], size, rows)

    ins = block_specs(blocks) + [whole(a) for a in (expand, expand_bias, contract)]
    aliases = {}
    if buffers is not None:
        for number, b in enumerate(buffers):
            aliases[len(ins)] = number
            ins.append((b, None, None))
    outs = [
        ((count, length, w), BF16, (1, length, w), lambda *_: (s, 0, 0)) for w in (d, hidden, hidden)
    ] + partial_outs(size, rows, d)
    return call(
        body, "feed_forward", vmem=LARGE, weight=7, ins=ins, outs=outs, aliases=aliases,
    )


def feed_back(blocks, expand, contract, slopes, buffers, s, count):
    size = len(blocks)
    rows, d = blocks[0][0].shape[1:]
    hidden = expand.shape[1]
    length = size * rows
    tile = min(256, hidden)

    def body(*refs):
        dz_refs = refs[:size]
        we_ref, wc_ref, slope_ref = refs[size : size + 3]
        n_partial = 1 + size // 2
        sums_ref, dz_out, du_out = refs[-3 - n_partial : -n_partial]
        dz = jnp.concatenate([r[0] for r in dz_refs], axis=0)
        dz_out[0] = dz
        for at in range(0, hidden, tile):
            cols = slice(at, at + tile)
            du = (nt(dz, wc_ref[cols, :]) * slope_ref[0, :, cols].astype(F32)).astype(BF16)
            du_out[0, :, cols] = du
            sums_ref[:, cols] = column_sum(du.astype(F32))
        write_rows(nt(du_out[0], we_ref[...]), refs[-n_partial:], size, rows)

    ins = block_specs(blocks) + [whole(expand), whole(contract)]
    ins.append((slopes, (1, length, hidden), lambda *_: (s, 0, 0)))
    aliases = {}
    if buffers is not None:
        for number, b in enumerate(buffers):
            aliases[len(ins)] = 1 + number
            ins.append((b, None, None))
    outs = [out_whole((1, hidden), F32)]
    outs += [((count, length, w), BF16, (1, length, w), lambda *_: (s, 0, 0)) for w in (d, hidden)]
    outs += partial_outs(size, rows, d)
    return call(
        body, "feed_back", vmem=LARGE, weight=6, ins=ins, outs=outs, aliases=aliases,
    )


def input_back(first, second, weights, size, count):
    rows = first.shape[1]
    d = weights[1].shape[0]
    width = weights[1].shape[1]

    def body(*refs):
        a_ref, b_ref, qw_ref, kw_ref, vw_ref = refs[:5]
        a = jnp.concatenate([a_ref[j] for j in range(size)], axis=0)
        b = jnp.concatenate([b_ref[j] for j in range(size)], axis=0)
        total = nt(a[:, :width], qw_ref[0])
        for m in (1, 2, 3):
            total = total + nt(a[:, m * width : (m + 1) * width], qw_ref[m])
        total = total + nt(b[:, :width], kw_ref[...])
        total = total + nt(b[:, width:], vw_ref[...])
        write_rows(total, refs[5:], size, rows)

    ins = [(a, (size, rows, a.shape[2]), lambda k: (k, 0, 0)) for a in (first, second)]
    ins += [whole(w) for w in weights]
    outs = [((size // 2, count * rows, d), BF16, (size // 2, rows, d), lambda k: (0, k, 0))]
    outs += [((count * rows, d), BF16, (rows, d), lambda k: (k, 0)) for _ in range(size // 2)]
    return call(body, "input_back", vmem=LARGE, grid=(count,), ins=ins, outs=outs)


def take(array, spots, dtypes, ready=()):
    rows, d = array.shape[1:]

    def body(spots_ref, in_ref, *out_refs):
        for m, out_ref in enumerate(out_refs[len(ready) :]):
            out_ref[...] = in_ref[spots_ref[m]].astype(out_ref.dtype)

    ins = [whole(array)] + [(a, None, None) for a in ready]
    outs = [out_whole((rows, d), dtype) for dtype in dtypes]
    return call(body, "take", prefetch=(spots,), ins=ins, outs=outs)


def put(blocks, spots):
    rows, d = blocks[0].shape
    n = len(blocks)

    def body(spots_ref, *refs):
        for m in range(n):
            refs[-1][pl.ds(pl.multiple_of(spots_ref[m] * rows, 16), rows), :] = refs[m][...].astype(F32)

    ins = [whole(b) for b in blocks]
    return call(body, "put", prefetch=(spots,), ins=ins, outs=[out_whole((n * rows, d), F32)])[0]


def collect(blocks):
    rows, d = blocks[0].shape

    def body(*refs):
        for m in range(len(blocks)):
            refs[-1][m] = refs[m][...]

    outs = [out_whole((len(blocks), rows, d), BF16)]
    return call(body, "collect", ins=[whole(b) for b in blocks], outs=outs)[0]


def final_sum(addends, dr_pieces, size, count):
    rows, d = dr_pieces.shape[1:]

    def body(*refs):
        refs[-1][...] = add_up(refs[:-1])

    ins = [(a, (1, rows, d), lambda k: (0, k, 0)) for a in addends]
    ins.append((dr_pieces, (1, rows, d), lambda k: (k * size, 0, 0)))
    outs = [((count * rows, d), F32, (rows, d), lambda k: (k, 0))]
    return call(body, "final_sum", grid=(count,), ins=ins, outs=outs)[0]


def across(array, rows):
    d, n = array.shape[1:]

    def body(in_ref, one_ref, two_ref):
        turned = in_ref[0].T
        one_ref[0] = turned[:rows]
        two_ref[...] = turned[rows:]

    outs = [out_whole((1, rows, d), F32), out_whole((n - rows, d), F32)]
    return call(body, "across", ins=[whole(array)], outs=outs)


def body(
    dp, tensor, tokens, token_kinds, segment_ids, cotangent, query_weight, query_bias, key_weight, key_bias,
    value_weight, value_bias, output_weight, output_bias, inner_gain, inner_shift, expand_weight, expand_bias,
    contract_weight, contract_bias, outer_gain, outer_shift,
):
    count, length = token_kinds.shape
    d = tokens.shape[1]
    rows = length // tensor
    me = lax.axis_index("tensor")
    width = key_weight.shape[2]
    hidden = expand_weight.shape[2]

    devices = np.arange(tensor)
    piece_at = np.array(
        [[[o * count + k for o in devices ^ r] for k in range(count)] for r in range(tensor)], np.int32
    )
    seq_piece = np.array(
        [[[s * tensor + b for b in devices ^ r] for s in range(count)] for r in range(tensor)], np.int32
    )
    table_of = np.array(
        [[(g % count) * tensor + ((g // count) ^ r) for g in seq_piece[r].reshape(-1)] for r in range(tensor)], np.int32
    )
    pick = lambda values: lax.dynamic_index_in_dim(jnp.asarray(values), me, 0, keepdims=False)
    table = pick(table_of)
    codes = (segment_ids * 2 + token_kinds).reshape(count * tensor, rows)
    lie = piece_at.transpose(0, 2, 1).reshape(tensor, -1)
    codes = codes[pick(np.concatenate([lie, seq_piece.reshape(tensor, -1)], axis=1))]
    lie_codes = codes[: count * tensor].reshape(tensor // 2, 1, -1)
    lie_codes = jnp.pad(lie_codes, ((0, 0), (0, 0), (0, -lie_codes.shape[2] % 128)))
    seq_codes = codes[count * tensor :].reshape(count, 1, length)

    weights = (query_weight[0], key_weight[0], value_weight[0])
    biases = jnp.concatenate([query_bias[0], key_bias, value_bias], axis=0).astype(F32)
    expand, contract = expand_weight[0], contract_weight[0]
    expand_bias32 = expand_bias.astype(F32)
    out_proj = output_weight[0]
    Order.mark, Order.weight = None, 0.2

    rounds = piece_rounds(count, tensor)
    perms = [[(u, v) for u, (v, _) in enumerate(chosen)] for chosen in rounds]
    stays = [all(u == v for u, v in perm) for perm in perms]
    sends = np.array([[chosen[u][1] % count for chosen in rounds] for u in range(tensor)], np.int32)
    spots_of = np.zeros((tensor, count), np.int32)
    for number, chosen in enumerate(rounds):
        for v, g in chosen:
            spots_of[v, g // tensor] = number
    spots = pick(spots_of)
    arrived = [
        block if stay else lax.ppermute(block, "tensor", perm)
        for block, stay, perm in zip(
            take(cotangent.reshape(count, rows, d), pick(sends), [BF16] * count, (lie_codes, seq_codes, biases)),
            stays, perms, strict=True,
        )
    ]
    held = {0: tokens}
    for bit in range(1, tensor.bit_length() - 1):
        for j in sorted(held):
            held[j | 1 << bit] = swap(held[j], "tensor", tensor, 1 << bit)
    near = project_rows([tokens, swap(tokens, "tensor", tensor, 1)], lie_codes, weights, biases, count)
    for j in range(2, tensor, 2):
        held[j] = relay([held[j]])[0]
        held[j | 1] = swap(held[j], "tensor", tensor, 1)
    pieces = project_rows([held[j] for j in range(2, tensor)], lie_codes, weights, biases, count, near)
    qkv, x_pieces = (a.reshape(count * tensor, rows, -1) for a in pieces)

    hold = {"cotangents": collect(arrived)}

    def run_attend(s):
        hold["context", s], hold["lse", s], *partial = attend(qkv, table, s, seq_codes, out_proj, tensor, rows)
        return partial

    def finish_attend(s):
        y, hold["n1", s], hold["rstd1", s] = inner_norm(
            hold["addends", s], x_pieces, table, s, output_bias, inner_gain, inner_shift, tensor
        )
        hold["y", s] = gather_start(y, tensor)

    def run_forward(s):
        out = feed_forward(hold["y", s], expand, expand_bias32, contract, hold.get("kept"), s, count)
        hold["kept"] = out[:3]
        return out[3:]

    def finish_forward(s):
        hold["results"], hold["dz", s], dzb, hold["outer", s] = outer_norm(
            hold["addends", s], hold["n1", s], inner_gain, inner_shift, contract_bias, outer_gain, outer_shift,
            hold["cotangents"], spots, hold.get("results"), s, count,
        )
        hold["dzb", s] = gather_start(dzb, tensor)

    def run_back(s):
        out = feed_back(hold["dzb", s], expand, contract, hold["kept"][2], hold.get("back"), s, count)
        hold["expand_bias", s], hold["back"] = out[0], out[1:3]
        return out[3:]

    def finish_back(s):
        drb, hold["inner", s] = inner_norm_back(
            hold["addends", s], hold["dz", s], hold["n1", s], hold["rstd1", s], inner_gain
        )
        hold["drb", s] = gather_start(drb, tensor)

    shapes = [(4, d, width), (1, d, width), (1, d, width), (1, d, width + 128), (1, d, hidden), (1, hidden, d)]
    grads = {}
    flat = lambda a: a.reshape(-1, a.shape[-1])
    bits = list(range(dp.bit_length() - 1))
    swapped = bits[1::-1] + bits[2:]
    orders = {name: swapped if name in SWAPPED else bits for name in "ceab"}

    def sum_over_dp(name, halves, order, layout):
        sums[name] = DpSum([(halves, order, layout)], dp, grads, shapes, name)

    sums = {}

    stages = [(run_attend, finish_attend, "y"), (run_forward, finish_forward, "dzb"), (run_back, finish_back, "drb")]
    runs = [(*one, s) for one in stages for s in range(count)]
    finished, complete = set(), set()

    def finish(i):
        if i not in finished:
            finished.add(i)
            runs[i][1](runs[i][3])

    def bring(i):
        if i not in complete:
            finish(i)
            complete.add(i)
            key = runs[i][2], runs[i][3]
            hold[key] = gather_end(hold[key], tensor)

    for i, (run, _, _, s) in enumerate(runs):
        if i >= count:
            bring(i - count)
        send, *keeps = run(s)
        received = swap(send, "tensor", tensor, 1)
        if i >= 2:
            bring(i - 2)
        if i >= 1:
            finish(i - 1)
        hold["addends", s] = scatter_rest(keeps, received, tensor)
    y_all, du_all = hold["kept"][0], hold["back"][1]

    def steps(names):
        for name in names:
            one = sums[{"c": "contract", "e": "expand", "a": "first", "b": "second"}[name]]
            if one.at < one.steps:
                one.step()

    returns, lands = np.zeros((tensor, count), np.int32), np.zeros((tensor, count), np.int32)
    for number, chosen in enumerate(rounds):
        for u, (v, g) in enumerate(chosen):
            returns[v, number], lands[u, number] = g // tensor, g % count

    kept, output_sum = None, None
    x_flat = flat(x_pieces)
    runs_back = list(range(count))
    for token in AFTER:
        name, _, weight = token.partition(":")
        Order.weight = float(weight or 0.2)
        if name == "attend":
            s = runs_back.pop(0)
            bring(2 * count + s)
            *kept, output_sum, hold["bias", s] = attend_back(
                qkv, table, s, seq_codes, out_proj, hold["context", s], hold["lse", s], hold["drb", s], kept,
                output_sum, count,
            )
            first, second, dr_pieces = kept
        elif name in ("near1", "near2"):
            bring(2 * count + int(name[-1]))
        elif name == "norm":
            finish(3 * count - 1)
        elif name == "norms":
            norms = norm_sums([hold["outer", s] for s in range(count)], [hold["inner", s] for s in range(count)])
            came = swap(norms, "tensor", tensor, 1)
        elif name == "add":
            for bit in range(1, tensor.bit_length() - 1):
                norms = add(norms, came)
                came = swap(norms, "tensor", tensor, 1 << bit)
        elif name == "Gc":
            halves = weight_grad(flat(hold["kept"][1]), flat(hold["back"][0]), orders["c"][0], "contract_grad")
            sum_over_dp("contract", halves, orders["c"], [(5, (0, 1), 0, d, 0)])
        elif name == "Ge":
            halves = weight_grad(flat(y_all), flat(du_all), orders["e"][0], "expand_grad")
            sum_over_dp("expand", halves, orders["e"], [(4, (0, 1), 0, hidden, 0)])
        elif name == "Ga":
            halves = weight_grad(x_flat, flat(first), orders["a"][0], "first_grad")
            sum_over_dp("first", halves, orders["a"], [(0, (0, 4), 0, width, 0)])
        elif name == "Gb":
            sums_of = lambda key: [hold[key, s] for s in range(count)]
            more = pack(output_sum, norms, came, sums_of("expand_bias"), sums_of("bias"))
            halves = weight_grad(x_flat, flat(second), orders["b"][0], "second_grad", more)
            layout = [(1, (0, 1), 0, width, 0), (2, (0, 1), width, width, 0), (3, (0, 1), 2 * width, width + 128, 0)]
            sum_over_dp("second", halves, orders["b"], layout)
        elif name == "in":
            send, *keeps = input_back(first, second, weights, tensor, count)
        elif name == "send":
            received = swap(again(send), "tensor", tensor, 1)
        elif name == "sum":
            addends = scatter_rest(keeps, received, tensor)
        elif name == "end":
            upstream = final_sum(addends, dr_pieces, tensor, count)
        elif name == "take":
            blocks = take(hold["results"], pick(returns), [F32 if stay else BF16 for stay in stays])
            blocks = [
                block if stay else lax.ppermute(block, "tensor", [(v, u) for u, v in perm])
                for block, stay, perm in zip(blocks, stays, perms, strict=True)
            ]
        elif name == "put":
            hold["result"] = put(blocks, pick(lands))
        else:
            steps(name)
    Order.weight = 0.2
    for one in sums.values():
        while one.at < one.steps:
            one.step()

    output_grad, small = across(grads[3], width)
    return (
        hold["result"],
        upstream,
        grads[0][None],
        small[None, 7:11, :width],
        grads[1],
        small[11:12, :width],
        grads[2],
        small[12:13, :width],
        output_grad,
        small[3:4],
        small[4:5],
        small[5:6],
        grads[4],
        small[6:7, :hidden],
        grads[5],
        small[0:1],
        small[1:2],
        small[2:3],
    )


def solution(mesh):
    rows, both = P("dp", None), P(("dp", "tensor"), None)
    columns = lambda dims: P(*[None] * (dims - 1), "tensor")
    down = P(None, "tensor", None)
    weight_specs = [columns(4), columns(3), columns(3), columns(2), columns(3), columns(2), down]
    ffn_specs = [columns(3), columns(2), down]
    return jax.shard_map(
        functools.partial(body, mesh.shape["dp"], mesh.shape["tensor"]),
        mesh=mesh,
        in_specs=(both, rows, rows, both, *weight_specs, P(), P(), P(), *ffn_specs, P(), P(), P()),
        out_specs=(both, both, *weight_specs, P(), P(), P(), *ffn_specs, P(), P(), P()),
        check_vma=False,
    )
```

```python
import functools

import jax
import jax.numpy as jnp
import numpy as np
from jax import lax
from jax.experimental import pallas as pl
from jax.experimental.pallas import tpu as pltpu
from jax.sharding import PartitionSpec as P

HD = 64
NORM_EPS = 1e-05
MASKED = -1e30
F32 = jnp.float32
BF16 = jnp.bfloat16
SMALL, LARGE = 6, 22
COST = 1.15e9
SWAPPED = "ea"
AFTER = (
    "Ge:2.5", "Gc:0.02", "near1", "attend:1", "norm:5", "norms:1", "attend:1", "c:0.02", "e:0.02", "near2:5", "take:2.5", "attend:1", "add:2.5", "Ga",
    "c:0.02", "e:2.5", "Gb", "in:1", "e:0.02", "c:2.5", "a:2.5", "b", "e:2.5", "a:0.02", "send:0.5", "c:2.5", "b:0.5", "put:0.02", "a:1", "b:1", "e:0.5", "c:0.02", "a:9", "b:0.02", "sum:1", "a:0.5", "e:1", "c:0.5", "b:0.5", "a:1", "end:0.5", "b:9",
)


def nn(a, b):
    return lax.dot_general(a, b, (((1,), (0,)), ((), ())), preferred_element_type=F32)


def nt(a, b):
    return lax.dot_general(a, b, (((1,), (1,)), ((), ())), preferred_element_type=F32)


def tn(a, b):
    return lax.dot_general(a, b, (((0,), (0,)), ((), ())), preferred_element_type=F32)


class Order:
    mark = None
    weight = 0.2


def call(body, name, *, grid=(1,), prefetch=(), ins, outs, aliases=None, scratch=(), weight=None, vmem=SMALL):
    def spec(block, index_map):
        if block is None:
            return pl.BlockSpec(memory_space=pl.ANY)
        return pl.BlockSpec(block, index_map, pipeline_mode=pl.Buffered(1) if grid == (1,) else None)

    shift = len(prefetch)
    marks = [] if Order.mark is None else [Order.mark]
    n_in, n_out = shift + len(ins), len(outs)

    def inner(*refs):
        given, rest = refs[:n_in], refs[n_in + len(marks) :]
        body(*given, *rest[:n_out], *rest[n_out + 1 :])

    in_specs = [spec(block, index_map) for _, block, index_map in ins]
    in_specs += [pl.BlockSpec(memory_space=pl.ANY) for _ in marks]
    out_specs = [spec(block, index_map) for _, _, block, index_map in outs]
    out_specs.append(pl.BlockSpec(memory_space=pl.ANY))
    shapes = [jax.ShapeDtypeStruct(shape, dtype) for shape, dtype, _, _ in outs]
    *results, Order.mark = pl.pallas_call(
        inner,
        grid_spec=pltpu.PrefetchScalarGridSpec(
            num_scalar_prefetch=shift,
            grid=grid,
            in_specs=in_specs,
            out_specs=out_specs,
            scratch_shapes=list(scratch),
        ),
        out_shape=[*shapes, jax.ShapeDtypeStruct((8, 128), F32)],
        input_output_aliases={shift + k: v for k, v in (aliases or {}).items()},
        compiler_params=pltpu.CompilerParams(vmem_limit_bytes=vmem * 1024 * 1024),
        cost_estimate=pl.CostEstimate(flops=int((Order.weight if weight is None else weight) * COST), bytes_accessed=1, transcendentals=0),
        name=name,
    )(*prefetch, *[array for array, _, _ in ins], *marks)
    return results


def whole(array):
    zeros = (0,) * array.ndim
    return (array, array.shape, lambda *_: zeros)


def out_whole(shape, dtype):
    zeros = (0,) * len(shape)
    return (shape, dtype, shape, lambda *_: zeros)


def swap(array, axis, size, bit):
    return lax.ppermute(array, axis, [(r, r ^ bit) for r in range(size)])


def gather_start(own, size):
    blocks = {0: own}
    bit = 2
    while bit < size:
        for j in sorted(blocks):
            blocks[j | bit] = swap(blocks[j], "tensor", size, bit)
        bit *= 2
    return blocks


def gather_end(blocks, size):
    even = relay([blocks[j] for j in range(0, size, 2)])
    odd = swap(even, "tensor", size, 1)
    return [((odd if j & 1 else even), j // 2) for j in range(size)]


def block_specs(blocks):
    return [
        (a, (1, *a.shape[1:]), functools.partial(lambda at, *_: (at, 0, 0), at)) for a, at in blocks
    ]


def combine(keep, received, m):
    rows, d = keep.shape

    def body(k_ref, r_ref, o_ref):
        o_ref[...] = (k_ref[...].astype(F32) + r_ref[0].astype(F32)).astype(BF16)

    ins = [whole(keep), (received, (1, rows, d), lambda *_: (m, 0, 0))]
    return call(body, "combine", ins=ins, outs=[out_whole((rows, d), BF16)])[0]


def scatter_rest(keeps, received, size):
    addends = [keeps[0][None], received]
    held = {2 * m: combine(keeps[m], received, m) for m in range(1, len(keeps))}
    bit = size // 2
    while bit >= 2:
        leaving = sorted(j for j in held if j & bit)
        arrived = [swap(held.pop(j), "tensor", size, bit) for j in leaving]
        addends.append(arrived[0][None])
        for j, block in zip(leaving[1:], arrived[1:], strict=True):
            held[j ^ bit] = combine(held[j ^ bit], block[None], 0)
        bit //= 2
    return addends


def addend_specs(addends):
    return [(a, (1,) + a.shape[1:], lambda *_: (0, 0, 0)) for a in addends]


def place_outs(state, shapes, layout, rows, spot_of, ins):
    outs, aliases = [], {}
    for number, (out, (lead, leads), _, wide, block) in enumerate(layout):
        index_map = functools.partial(lambda lead, block, m, spots: (lead, spot_of(m, spots), block), lead, block)
        outs.append((shapes[out], F32, (leads, rows, wide), index_map))
        if out in state:
            aliases[len(ins)] = number
            ins.append((state[out], None, None))
    return outs, aliases


def place_values(values, layout, out_refs):
    for (_, (_, leads), start, wide, _), out_ref in zip(layout, out_refs, strict=True):
        for lead in range(leads):
            at = start + lead * wide
            out_ref[lead] = values[:, at : at + wide].astype(F32)


class DpSum:
    def __init__(self, entries, size, state, shapes, name):
        self.size, self.name, self.state, self.shapes = size, name, state, shapes
        self.at = 0
        self.orders = [order for _, order, _ in entries]
        self.layouts = [layout for _, _, layout in entries]
        self.bits = len(entries[0][1])
        self.steps = 2 * self.bits
        here = lax.axis_index("dp")
        self.mine = [[(here >> bit) & 1 for bit in order] for order in self.orders]
        self.held = [0]
        self.staying = [halves[0] for halves, _, _ in entries]
        self.send([halves[1] for halves, _, _ in entries], 0)

    def scalars(self, values):
        return jnp.stack([jnp.asarray(v, jnp.int32) for v in values])

    def send(self, blocks, level):
        self.arrived = [
            swap(block, "dp", self.size, 1 << order[level]) for block, order in zip(blocks, self.orders, strict=True)
        ]

    def where(self, m, differs):
        spot = 0
        for level, mine in enumerate(self.mine[m]):
            spot = spot * 2 + (mine ^ ((differs >> level) & 1))
        return spot

    def step(self):
        if self.at < self.bits:
            self.halve()
        else:
            self.join()
        self.at += 1

    def placing(self, ins, rows, spot_of):
        outs, aliases = [], {}
        for m, layout in enumerate(self.layouts):
            index_of = functools.partial(spot_of, m)
            more, taken = place_outs(self.state, self.shapes, layout, rows[m], index_of, ins)
            aliases.update({k: v + len(outs) for k, v in taken.items()})
            outs += more
        return outs, aliases

    def keep_placed(self, got):
        names = [entry[0] for layout in self.layouts for entry in layout]
        self.state.update(dict(zip(names, got, strict=True)))

    def halve(self):
        level = self.at
        last = level == self.bits - 1
        n = len(self.staying)
        shapes = [a.shape for a in self.arrived]
        ends = np.cumsum([0] + [len(layout) for layout in self.layouts])

        def body(scalars_ref, *refs):
            outs = refs[2 * n :]
            for m in range(n):
                stay_ref, came_ref = refs[2 * m : 2 * m + 2]
                if last:
                    total = (stay_ref[...].astype(F32) + came_ref[...].astype(F32)).astype(BF16)
                    outs[len(outs) - n + m][...] = total
                    place_values(total, self.layouts[m], outs[len(outs) - n - ends[-1] :][ends[m] : ends[m + 1]])
                    continue
                half = shapes[m][0] // 2
                for out_ref, part in ((outs[2 * m], 1 - scalars_ref[m]), (outs[2 * m + 1], scalars_ref[m])):
                    at = pl.ds(pl.multiple_of(part * half, 16), half)
                    out_ref[...] = (stay_ref[at, :].astype(F32) + came_ref[at, :].astype(F32)).astype(BF16)

        ins = [whole(a) for pair in zip(self.staying, self.arrived, strict=True) for a in pair]
        if last:
            prefetch = self.scalars([self.where(m, 0) for m in range(n)])
            outs, aliases = self.placing(ins, [shape[0] for shape in shapes], lambda m, i, spots: spots[m])
            outs += [out_whole(shape, BF16) for shape in shapes]
        else:
            prefetch = self.scalars([mine[level + 1] for mine in self.mine])
            outs, aliases = [], {}
            for rows, columns in shapes:
                outs += [out_whole((rows // 2, columns), BF16)] * 2
        got = call(
            body, self.name + "_halve", prefetch=(prefetch,), ins=ins, outs=outs, aliases=aliases
        )
        if last:
            self.staying = got[len(got) - n :]
            self.keep_placed(got[: len(got) - n])
            self.send(self.staying, level)
        else:
            self.staying = got[1::2]
            self.send(got[0::2], level + 1)

    def join(self):
        level = self.steps - 1 - self.at
        count = len(self.held)
        came = [differs | (1 << level) for differs in self.held]
        self.held = self.held + came
        n = len(self.arrived)
        spots = self.scalars([self.where(m, differs) for m in range(n) for differs in came])
        rows = [a.shape[0] // count for a in self.arrived]
        ends = np.cumsum([0] + [len(layout) for layout in self.layouts])
        block = lambda i, spots: (i, 0)
        ins = [(a, (r, a.shape[1]), block) for a, r in zip(self.arrived, rows, strict=True)]
        if level:
            ins += [(a, (r, a.shape[1]), block) for a, r in zip(self.staying, rows, strict=True)]

        def body(spots_ref, *refs):
            joined = refs[len(refs) - n :] if level else ()
            placed = refs[len(refs) - len(joined) - ends[-1] : len(refs) - len(joined)]
            for m in range(n):
                values = refs[m][...]
                if level:
                    joined[m][0] = refs[n + m][...]
                    joined[m][1] = values
                place_values(values, self.layouts[m], placed[ends[m] : ends[m + 1]])

        outs, aliases = self.placing(ins, rows, lambda m, i, spots: spots[m * count + i])
        if level:
            for a, r in zip(self.arrived, rows, strict=True):
                outs.append(((2, *a.shape), BF16, (2, r, a.shape[1]), lambda i, spots: (0, i, 0)))
        got = call(
            body, self.name + "_join", grid=(count,), prefetch=(spots,), ins=ins, outs=outs, aliases=aliases
        )
        if level:
            self.staying = [a.reshape(-1, a.shape[2]) for a in got[len(got) - n :]]
            got = got[: len(got) - n]
            self.send(self.staying, level - 1)
        self.keep_placed(got)


def weight_grad(left_side, right_side, bit, name, more=None):
    tokens, total = left_side.shape
    columns = right_side.shape[1]
    half = total // 2

    def body(mine_ref, a_ref, b_ref, *refs):
        stay_ref, leave_ref = refs[-2:]
        product = tn(a_ref[...], b_ref[...]).astype(BF16)
        if more is not None:
            product = jnp.concatenate([product, refs[0][...]], axis=1)
        mine = pl.program_id(0) == mine_ref[0]

        @pl.when(mine)
        def _():
            stay_ref[...] = product

        @pl.when(jnp.logical_not(mine))
        def _():
            leave_ref[...] = product

    ins = [(left_side, (tokens, half), lambda i, mine: (0, i)), whole(right_side)]
    if more is not None:
        ins.append((more, (half, more.shape[1]), lambda i, mine: (i, 0)))
        columns += more.shape[1]
    outs = [out_whole((half, columns), BF16)] * 2
    mine = ((lax.axis_index("dp") >> bit) & 1).reshape(1).astype(jnp.int32)
    return call(body, name, vmem=LARGE, grid=(2,), prefetch=(mine,), ins=ins, outs=outs)


def add(one, two):
    def body(one_ref, two_ref, out_ref):
        out_ref[...] = one_ref[...] + two_ref[...]

    return call(body, "add", ins=[whole(one), whole(two)], outs=[out_whole(one.shape, F32)])[0]


def norm_sums(outer, inner):
    n, shape = len(outer), outer[0].shape

    def body(*refs):
        for at, group in ((0, refs[:n]), (3, refs[n : 2 * n])):
            total = group[0][0:3]
            for r in group[1:]:
                total = total + r[0:3]
            refs[-1][at : at + 3] = total
        refs[-1][6:8] = jnp.zeros((2, shape[1]), F32)

    ins = [whole(a) for a in (*outer, *inner)]
    return call(body, "norm_sums", ins=ins, outs=[out_whole(shape, F32)])[0]


def pack(output_sum, norms, came, expand_bias, bias):
    width, d = output_sum.shape
    hidden = expand_bias[0].shape[1]
    n = len(bias)

    def body(o_ref, norm_ref, came_ref, *refs):
        out_ref, rows_ref = refs[-2:]
        rows_ref[...] = jnp.zeros((128, d), F32)
        rows_ref[0:6] = norm_ref[0:6] + came_ref[0:6]
        total = refs[0][...]
        for r in refs[1:n]:
            total = total + r[...]
        rows_ref[6:7, :hidden] = total
        total = refs[n][0:6]
        for r in refs[n + 1 : 2 * n]:
            total = total + r[0:6]
        rows_ref[7:13, :width] = total
        out_ref[:, :width] = o_ref[...].T.astype(BF16)
        out_ref[:, width:] = rows_ref[...].T.astype(BF16)

    ins = [whole(a) for a in (output_sum, norms, came, *expand_bias, *bias)]
    outs = [out_whole((d, width + 128), BF16)]
    return call(body, "pack", ins=ins, outs=outs, scratch=[pltpu.VMEM((128, d), F32)])[0]


def piece_rounds(count, size):
    left = {}
    for g in range(count * size):
        left.setdefault((g // count, g % size), []).append(g)
    rounds = []
    for _ in range(count):
        match = {}

        def augment(u, seen):
            for v in range(size):
                if left.get((u, v)) and v not in seen:
                    seen.add(v)
                    if v not in match or augment(match[v], seen):
                        match[v] = u
                        return True
            return False

        for bit in range(size):
            if all(left.get((u, u ^ bit)) for u in range(size)):
                match.update({u ^ bit: u for u in range(size)})
                break
        else:
            for u in range(size):
                augment(u, set())
        chosen = {u: (v, left[(u, v)].pop(0)) for v, u in match.items()}
        rounds.append([chosen[u] for u in range(size)])
    return rounds


def erf_parts(u):
    size = jnp.abs(u) * np.float32(0.7071067811865476)
    bell = jnp.exp(-(size * size))
    t = pl.reciprocal(1.0 + np.float32(0.3275911) * size)
    poly = np.float32(1.061405429 * 0.5)
    for c in (-1.453152027, 1.421413741, -0.284496736, 0.254829592):
        poly = poly * t + np.float32(c * 0.5)
    tail = poly * t * bell
    return jnp.where(u < 0, tail, 1.0 - tail), bell * np.float32(0.3989422804014327)


def write_rows(values, out_refs, size, rows):
    for j in range(size):
        block = values[j * rows : (j + 1) * rows].astype(BF16)
        if j & 1:
            out_refs[0][j // 2] = block
        else:
            out_refs[1 + j // 2][...] = block


def partial_outs(size, rows, width):
    return [out_whole((size // 2, rows, width), BF16)] + [out_whole((rows, width), BF16)] * (size // 2)


def column(row, wide):
    one = jnp.broadcast_to(row.astype(F32), (128, row.shape[1])).T
    return one if wide == 128 else jnp.concatenate([one] * (wide // 128), axis=1)


def project_rows(blocks, codes, weights, biases, count, near=()):
    size = len(blocks)
    skip = near[0].shape[1] if near else 0
    rows = blocks[0].shape[0] // count
    d = blocks[0].shape[1]
    width = weights[1].shape[1]
    total = 2 * count * rows

    def body(*refs):
        code_ref, qw_ref, kw_ref, vw_ref, b_ref, *near_refs, out_ref, x_out = refs[size:]
        for near_ref, to in zip(near_refs, (out_ref, x_out)):
            to[:, :skip] = near_ref[...]
        bias = [b_ref[m : m + 1, :] for m in range(6)]
        for at in range(0, size, 2):
            x = jnp.concatenate([refs[at][...], refs[at + 1][...]], axis=0)
            spots = [(m, skip + at + i) for i in range(2) for m in range(count)]
            for number, (m, i) in enumerate(spots):
                x_out[m, i] = x[number * rows : (number + 1) * rows]
            word = column(code_ref[(skip + at) // 2] & 1, width)[:total] == 0.0

            def write(part, values):
                for number, (m, i) in enumerate(spots):
                    out_ref[m, i, :, part * width : (part + 1) * width] = values[number * rows : (number + 1) * rows]

            for part, (first, second) in enumerate(((0, 2), (1, 3))):
                one = nn(x, qw_ref[first]) + bias[first]
                two = nn(x, qw_ref[second]) + bias[second]
                write(part, jnp.where(word, one, two).astype(BF16))
            for part, ref, m in ((2, kw_ref, 4), (3, vw_ref, 5)):
                write(part, (nn(x, ref[...]) + bias[m]).astype(BF16))

    ins = [whole(b) for b in blocks] + [whole(codes)]
    ins += [whole(w) for w in weights] + [whole(biases)] + [whole(a) for a in near]
    outs = [out_whole((count, skip + size, rows, wide), BF16) for wide in (4 * width, d)]
    return call(body, "project_rows", vmem=LARGE, weight=5, ins=ins, outs=outs)


def relay(blocks):
    rows, d = blocks[0].shape
    n = len(blocks)

    def body(*refs):
        for m in range(n):
            refs[-1][m] = refs[m][...]

    return call(body, "relay", ins=[whole(b) for b in blocks], outs=[out_whole((n, rows, d), BF16)])[0]


def again(array):
    def body(in_ref, out_ref):
        out_ref[...] = in_ref[...]

    return call(body, "again", ins=[whole(array)], outs=[out_whole(array.shape, array.dtype)])[0]


def head_views(piece_refs, part, pair, width):
    start = part * width + pair * 128
    return jnp.concatenate([r[0, :, start : start + 128] for r in piece_refs], axis=0)


def swap_lanes(values):
    return pltpu.roll(values.astype(F32), 64, 1)


def extended(piece_refs, pair, width, takes, left):
    qw = head_views(piece_refs, 0, pair, width)
    qe = head_views(piece_refs, 1, pair, width)
    k = head_views(piece_refs, 2, pair, width)
    v = head_views(piece_refs, 3, pair, width)
    qw32, qe32, k32 = qw.astype(F32), qe.astype(F32), k.astype(F32) * 0.125
    qw_s, qe_s, k_s = swap_lanes(qw32), swap_lanes(qe32), swap_lanes(k32)
    q_ext = (
        jnp.where(left, qw32, qe_s).astype(BF16),
        jnp.where(left, qw_s, qe32).astype(BF16),
    )
    k_ext = (
        jnp.where(takes, jnp.where(left, k32, k_s), 0.0).astype(BF16),
        jnp.where(takes, jnp.where(left, k_s, k32), 0.0).astype(BF16),
    )
    return q_ext, k_ext, v


def query_blocks(length):
    spans, at = [], 0
    while at < length:
        step = length
        spans.append((at, step))
        at += step
    return spans


def attend(pieces, table, s, codes, out_proj, size, rows):
    length = size * rows
    width, d = out_proj.shape
    pairs = width // 128

    def body(table_ref, *refs):
        piece_refs = refs[:size]
        code_ref, wo_ref, c_ref, lse_ref = refs[size : size + 4]
        left = lax.broadcasted_iota(jnp.int32, (length, 128), 1) < 64
        code = code_ref[0]
        word = column(code & 1, 128) == 0.0
        takes = word == left
        segr = (code >> 1).astype(F32)
        segc = column(code >> 1, length)
        for pair in range(pairs):
            q_ext, k_ext, v = extended(piece_refs, pair, width, takes, left)
            v_t = v.astype(F32).T.astype(BF16)
            for at, step in query_blocks(length):
                same = segc[:, :step] == segr[:, at : at + step]
                tops = []
                for h in range(2):
                    s_t = nt(k_ext[h], q_ext[h][at : at + step])
                    s_t = jnp.where(same, s_t, MASKED)
                    top = jnp.max(s_t, axis=0, keepdims=True)
                    e = jnp.exp(s_t - top)
                    total = jnp.sum(e, axis=0, keepdims=True)
                    o_t = nn(v_t[h * 64 : h * 64 + 64], e.astype(BF16))
                    tops.append(o_t * (1.0 / total))
                    lse_ref[2 * pair + h : 2 * pair + h + 1, at : at + step] = top + jnp.log(total)
                c = jnp.concatenate(tops, axis=0).T.astype(BF16)
                c_ref[at : at + step, pair * 128 : pair * 128 + 128] = c
        write_rows(nn(c_ref[...], wo_ref[...]), refs[-1 - size // 2 :], size, rows)

    ins = [
        (pieces, (1, rows, 4 * width), functools.partial(lambda j, _, t: (t[s * size + j], 0, 0), j))
        for j in range(size)
    ]
    ins += [
        (codes, (1, 1, length), lambda *_: (s, 0, 0)),
        whole(out_proj),
    ]
    outs = [out_whole((length, width), BF16), out_whole((8, length), F32)]
    outs += partial_outs(size, rows, d)
    return call(
        body, "attend", vmem=LARGE, weight=7, prefetch=(table,), ins=ins, outs=outs,
    )


def attend_back(pieces, table, s, codes, out_proj, context, lse, delta_blocks, buffers, sums, count):
    size = len(delta_blocks)
    rows, d = delta_blocks[0][0].shape[1:]
    length = size * rows
    width = out_proj.shape[0]
    pairs = width // 128

    def body(table_ref, *refs):
        piece_refs = refs[:size]
        delta_refs = refs[size : 2 * size]
        code_ref, wo_ref, c_ref, lse_ref = refs[2 * size : 2 * size + 4]
        n_out = 5
        tail = refs[2 * size + 4 :]
        sum_in = tail[0] if sums is not None else None
        first_out, second_out, delta_out, wo_grad, bias_out, first_all, second_all = tail[-(n_out + 2) :]
        step_at = pl.program_id(0)

        @pl.when(step_at == 0)
        def _():
            left = lax.broadcasted_iota(jnp.int32, (length, 128), 1) < 64
            code = code_ref[0]
            word = column(code & 1, 128) == 0.0
            takes = word == left
            segr = (code >> 1).astype(F32)
            segc = column(code >> 1, length)
            delta = jnp.concatenate([r[0] for r in delta_refs], axis=0)
            c_all = c_ref[...]
            grad = nn(c_all.astype(F32).T.astype(BF16), delta)
            wo_grad[...] = grad if sum_in is None else grad + sum_in[...]
            for pair in range(pairs):
                dc = nt(delta, wo_ref[pair * 128 : pair * 128 + 128, :]).astype(BF16)
                q_ext, k_ext, v = extended(piece_refs, pair, width, takes, left)
                k_ext_t = [k.astype(F32).T.astype(BF16) for k in k_ext]
                dc32 = dc.astype(F32)
                dc_h = (jnp.where(left, dc32, 0.0).astype(BF16), jnp.where(left, 0.0, dc32).astype(BF16))
                dv = jnp.zeros((length, 128), F32)
                dk = [jnp.zeros((length, 128), F32)] * 2
                dq = [[], []]
                for at, step in query_blocks(length):
                    same = segc[:, :step] == segr[:, at : at + step]
                    for h in range(2):
                        q_b, dc_b = q_ext[h][at : at + step], dc_h[h][at : at + step]
                        row = 2 * pair + h
                        s_t = nt(k_ext[h], q_b)
                        p = jnp.where(same, jnp.exp(s_t - lse_ref[row : row + 1, at : at + step]), 0.0)
                        dp = nt(v, dc_b)
                        row_inner = jnp.sum(p * dp, axis=0, keepdims=True)
                        ds = (p * (dp - row_inner)).astype(BF16)
                        dv = dv + nn(p.astype(BF16), dc_b)
                        dk[h] = dk[h] + nn(ds, q_b)
                        dq[h].append(nn(k_ext_t[h], ds).T)
                dq0, dq1 = (jnp.concatenate(parts, axis=0) for parts in dq)
                dqw = jnp.where(left, dq0, swap_lanes(dq1))
                dqe = jnp.where(left, swap_lanes(dq0), dq1)
                dk0, dk1 = dk[0] * 0.125, dk[1] * 0.125
                dk_pair = jnp.where(takes, jnp.where(left, dk0, dk1), jnp.where(left, swap_lanes(dk0), swap_lanes(dk1)))
                outs = (
                    jnp.where(word, dqw, 0.0), jnp.where(word, dqe, 0.0), jnp.where(word, 0.0, dqw),
                    jnp.where(word, 0.0, dqe), dk_pair, dv,
                )
                for number, values in enumerate(outs):
                    rounded = values.astype(BF16)
                    target = (first_all, second_all)[number // 4]
                    start = (number % 4) * width + pair * 128
                    target[:, start : start + 128] = rounded
                    bias_out[number : number + 1, pair * 128 : pair * 128 + 128] = jnp.sum(
                        rounded.astype(F32), axis=0, keepdims=True
                    )

        at_rows = pl.ds(pl.multiple_of(step_at * rows, 16), rows)
        first_out[0] = first_all[at_rows, :]
        second_out[0] = second_all[at_rows, :]
        for j in range(size):

            @pl.when(step_at == j)
            def _():
                delta_out[0] = delta_refs[j][0]

    ins = [
        (pieces, (1, rows, 4 * width), functools.partial(lambda j, _, t: (t[s * size + j], 0, 0), j))
        for j in range(size)
    ]
    ins += block_specs(delta_blocks)
    ins += [
        (codes, (1, 1, length), lambda *_: (s, 0, 0)),
        whole(out_proj),
        whole(context),
        whole(lse),
    ]
    if sums is not None:
        ins.append(whole(sums))
    aliases = {}
    if buffers is not None:
        for number, b in enumerate(buffers):
            aliases[len(ins)] = number
            ins.append((b, None, None))
    spot = lambda m, t: (t[s * size + m], 0, 0)
    outs = [
        ((count * size, rows, 4 * width), BF16, (1, rows, 4 * width), spot),
        ((count * size, rows, 2 * width), BF16, (1, rows, 2 * width), spot),
        ((count * size, rows, d), BF16, (1, rows, d), spot),
        out_whole((width, d), F32),
        out_whole((8, width), F32),
    ]
    return call(
        body, "attend_back", vmem=LARGE, grid=(size,), prefetch=(table,), ins=ins, outs=outs, aliases=aliases,
        scratch=[pltpu.VMEM((length, 4 * width), BF16), pltpu.VMEM((length, 2 * width), BF16)],
    )


def add_up(refs):
    total = refs[0][0].astype(F32)
    for r in refs[1:]:
        total = total + r[0].astype(F32)
    return total


def normed(values):
    centre = jnp.mean(values, axis=-1, keepdims=True)
    offset = values - centre
    spread = jnp.mean(offset * offset, axis=-1, keepdims=True)
    rstd = lax.rsqrt(spread + NORM_EPS)
    return offset * rstd, rstd


def norm_pull(upstream, n, rstd, gain):
    scaled = upstream * gain
    inner = jnp.mean(scaled, axis=-1, keepdims=True)
    cross = jnp.mean(scaled * n, axis=-1, keepdims=True)
    return rstd * (scaled - inner - n * cross)


def column_sum(values):
    return jnp.sum(values, axis=0, keepdims=True)


def inner_norm(addends, x_pieces, table, s, bias, gain, shift, size):
    rows, d = addends[0].shape[1:]
    n_add = len(addends)

    def body(table_ref, *refs):
        x_ref, b_ref, g_ref, h_ref, y_ref, n_ref, rstd_ref = refs[n_add:]
        r = add_up(refs[:n_add]) + b_ref[...] + x_ref[0].astype(F32)
        n, rstd = normed(r)
        n_ref[...] = n
        rstd_ref[...] = jnp.broadcast_to(rstd, (rows, 128))
        y_ref[...] = (n * g_ref[...] + h_ref[...]).astype(BF16)

    ins = addend_specs(addends)
    ins.append((x_pieces, (1, rows, d), lambda _, t: (t[s * size], 0, 0)))
    ins += [whole(bias), whole(gain), whole(shift)]
    outs = [out_whole((rows, d), BF16), out_whole((rows, d), F32), out_whole((rows, 128), F32)]
    return call(body, "inner_norm", weight=5, prefetch=(table,), ins=ins, outs=outs)


def outer_norm(addends, n1, inner_gain, inner_shift, bias, gain, shift, cotangents, spots, buffer, s, count):
    rows, d = addends[0].shape[1:]
    n_add = len(addends)

    def body(spots_ref, *refs):
        n1_ref, g1_ref, h1_ref, b_ref, g_ref, h_ref, e_ref = refs[n_add : n_add + 7]
        res_ref, dz_ref, dzb_ref, sums_ref = refs[-4:]
        z = add_up(refs[:n_add]) + b_ref[...] + (n1_ref[...] * g1_ref[...] + h1_ref[...])
        n, rstd = normed(z)
        res_ref[0] = n * g_ref[...] + h_ref[...]
        e = e_ref[0].astype(F32)
        dz = norm_pull(e, n, rstd, g_ref[...])
        dz_ref[...] = dz
        dzb_ref[...] = dz.astype(BF16)
        sums_ref[0:1] = column_sum(dz)
        sums_ref[1:2] = column_sum(e * n)
        sums_ref[2:3] = column_sum(e)

    ins = addend_specs(addends)
    ins += [whole(a) for a in (n1, inner_gain, inner_shift, bias, gain, shift)]
    ins.append((cotangents, (1, rows, d), lambda _, t: (t[s], 0, 0)))
    aliases = {}
    if buffer is not None:
        aliases[len(ins)] = 0
        ins.append((buffer, None, None))
    outs = [
        ((count, rows, d), F32, (1, rows, d), lambda *_: (s, 0, 0)),
        out_whole((rows, d), F32),
        out_whole((rows, d), BF16),
        out_whole((8, d), F32),
    ]
    return call(
        body, "outer_norm", weight=5, prefetch=(spots,), ins=ins, outs=outs, aliases=aliases,
    )


def inner_norm_back(addends, dz, n1, rstd1, gain):
    rows, d = addends[0].shape[1:]
    n_add = len(addends)

    def body(*refs):
        dz_ref, n_ref, rstd_ref, g_ref, dr_ref, sums_ref = refs[n_add:]
        da = add_up(refs[:n_add]) + dz_ref[...]
        n = n_ref[...]
        dr = norm_pull(da, n, rstd_ref[:, 0:1], g_ref[...])
        dr_ref[...] = dr.astype(BF16)
        sums_ref[0:1] = column_sum(dr)
        sums_ref[1:2] = column_sum(da * n)
        sums_ref[2:3] = column_sum(da)

    ins = addend_specs(addends) + [whole(a) for a in (dz, n1, rstd1, gain)]
    outs = [out_whole((rows, d), BF16), out_whole((8, d), F32)]
    return call(body, "inner_norm_back", weight=5, ins=ins, outs=outs)


def feed_forward(blocks, expand, expand_bias, contract, buffers, s, count):
    size = len(blocks)
    rows, d = blocks[0][0].shape[1:]
    hidden = expand.shape[1]
    length = size * rows
    tile = min(256, hidden)

    def body(*refs):
        y_refs = refs[:size]
        we_ref, be_ref, wc_ref = refs[size : size + 3]
        n_partial = 1 + size // 2
        y_out, g_out, slope_out = refs[-3 - n_partial : -n_partial]
        y = jnp.concatenate([r[0] for r in y_refs], axis=0)
        y_out[0] = y
        for at in range(0, hidden, tile):
            cols = slice(at, at + tile)
            u = nn(y, we_ref[:, cols]) + be_ref[:, cols]
            phi_sum, phi = erf_parts(u)
            g_out[0, :, cols] = (u * phi_sum).astype(BF16)
            slope_out[0, :, cols] = (phi_sum + u * phi).astype(BF16)
        write_rows(nn(g_out[0], wc_ref[...]), refs[-n_partial:], size, rows)

    ins = block_specs(blocks) + [whole(a) for a in (expand, expand_bias, contract)]
    aliases = {}
    if buffers is not None:
        for number, b in enumerate(buffers):
            aliases[len(ins)] = number
            ins.append((b, None, None))
    outs = [
        ((count, length, w), BF16, (1, length, w), lambda *_: (s, 0, 0)) for w in (d, hidden, hidden)
    ] + partial_outs(size, rows, d)
    return call(
        body, "feed_forward", vmem=LARGE, weight=7, ins=ins, outs=outs, aliases=aliases,
    )


def feed_back(blocks, expand, contract, slopes, buffers, s, count):
    size = len(blocks)
    rows, d = blocks[0][0].shape[1:]
    hidden = expand.shape[1]
    length = size * rows
    tile = min(256, hidden)

    def body(*refs):
        dz_refs = refs[:size]
        we_ref, wc_ref, slope_ref = refs[size : size + 3]
        n_partial = 1 + size // 2
        sums_ref, dz_out, du_out = refs[-3 - n_partial : -n_partial]
        dz = jnp.concatenate([r[0] for r in dz_refs], axis=0)
        dz_out[0] = dz
        for at in range(0, hidden, tile):
            cols = slice(at, at + tile)
            du = (nt(dz, wc_ref[cols, :]) * slope_ref[0, :, cols].astype(F32)).astype(BF16)
            du_out[0, :, cols] = du
            sums_ref[:, cols] = column_sum(du.astype(F32))
        write_rows(nt(du_out[0], we_ref[...]), refs[-n_partial:], size, rows)

    ins = block_specs(blocks) + [whole(expand), whole(contract)]
    ins.append((slopes, (1, length, hidden), lambda *_: (s, 0, 0)))
    aliases = {}
    if buffers is not None:
        for number, b in enumerate(buffers):
            aliases[len(ins)] = 1 + number
            ins.append((b, None, None))
    outs = [out_whole((1, hidden), F32)]
    outs += [((count, length, w), BF16, (1, length, w), lambda *_: (s, 0, 0)) for w in (d, hidden)]
    outs += partial_outs(size, rows, d)
    return call(
        body, "feed_back", vmem=LARGE, weight=6, ins=ins, outs=outs, aliases=aliases,
    )


def input_back(first, second, weights, size, count):
    rows = first.shape[1]
    d = weights[1].shape[0]
    width = weights[1].shape[1]

    def body(*refs):
        a_ref, b_ref, qw_ref, kw_ref, vw_ref = refs[:5]
        a = jnp.concatenate([a_ref[j] for j in range(size)], axis=0)
        b = jnp.concatenate([b_ref[j] for j in range(size)], axis=0)
        total = nt(a[:, :width], qw_ref[0])
        for m in (1, 2, 3):
            total = total + nt(a[:, m * width : (m + 1) * width], qw_ref[m])
        total = total + nt(b[:, :width], kw_ref[...])
        total = total + nt(b[:, width:], vw_ref[...])
        write_rows(total, refs[5:], size, rows)

    ins = [(a, (size, rows, a.shape[2]), lambda k: (k, 0, 0)) for a in (first, second)]
    ins += [whole(w) for w in weights]
    outs = [((size // 2, count * rows, d), BF16, (size // 2, rows, d), lambda k: (0, k, 0))]
    outs += [((count * rows, d), BF16, (rows, d), lambda k: (k, 0)) for _ in range(size // 2)]
    return call(body, "input_back", vmem=LARGE, grid=(count,), ins=ins, outs=outs)


def take(array, spots, dtypes, ready=()):
    rows, d = array.shape[1:]

    def body(spots_ref, in_ref, *out_refs):
        for m, out_ref in enumerate(out_refs[len(ready) :]):
            out_ref[...] = in_ref[spots_ref[m]].astype(out_ref.dtype)

    ins = [whole(array)] + [(a, None, None) for a in ready]
    outs = [out_whole((rows, d), dtype) for dtype in dtypes]
    return call(body, "take", prefetch=(spots,), ins=ins, outs=outs)


def put(blocks, spots):
    rows, d = blocks[0].shape
    n = len(blocks)

    def body(spots_ref, *refs):
        for m in range(n):
            refs[-1][pl.ds(pl.multiple_of(spots_ref[m] * rows, 16), rows), :] = refs[m][...].astype(F32)

    ins = [whole(b) for b in blocks]
    return call(body, "put", prefetch=(spots,), ins=ins, outs=[out_whole((n * rows, d), F32)])[0]


def collect(blocks):
    rows, d = blocks[0].shape

    def body(*refs):
        for m in range(len(blocks)):
            refs[-1][m] = refs[m][...]

    outs = [out_whole((len(blocks), rows, d), BF16)]
    return call(body, "collect", ins=[whole(b) for b in blocks], outs=outs)[0]


def final_sum(addends, dr_pieces, size, count):
    rows, d = dr_pieces.shape[1:]

    def body(*refs):
        refs[-1][...] = add_up(refs[:-1])

    ins = [(a, (1, rows, d), lambda k: (0, k, 0)) for a in addends]
    ins.append((dr_pieces, (1, rows, d), lambda k: (k * size, 0, 0)))
    outs = [((count * rows, d), F32, (rows, d), lambda k: (k, 0))]
    return call(body, "final_sum", grid=(count,), ins=ins, outs=outs)[0]


def across(array, rows):
    d, n = array.shape[1:]

    def body(in_ref, one_ref, two_ref):
        turned = in_ref[0].T
        one_ref[0] = turned[:rows]
        two_ref[...] = turned[rows:]

    outs = [out_whole((1, rows, d), F32), out_whole((n - rows, d), F32)]
    return call(body, "across", ins=[whole(array)], outs=outs)


def body(
    dp, tensor, tokens, token_kinds, segment_ids, cotangent, query_weight, query_bias, key_weight, key_bias,
    value_weight, value_bias, output_weight, output_bias, inner_gain, inner_shift, expand_weight, expand_bias,
    contract_weight, contract_bias, outer_gain, outer_shift,
):
    count, length = token_kinds.shape
    d = tokens.shape[1]
    rows = length // tensor
    me = lax.axis_index("tensor")
    width = key_weight.shape[2]
    hidden = expand_weight.shape[2]

    devices = np.arange(tensor)
    piece_at = np.array(
        [[[o * count + k for o in devices ^ r] for k in range(count)] for r in range(tensor)], np.int32
    )
    seq_piece = np.array(
        [[[s * tensor + b for b in devices ^ r] for s in range(count)] for r in range(tensor)], np.int32
    )
    table_of = np.array(
        [[(g % count) * tensor + ((g // count) ^ r) for g in seq_piece[r].reshape(-1)] for r in range(tensor)], np.int32
    )
    pick = lambda values: lax.dynamic_index_in_dim(jnp.asarray(values), me, 0, keepdims=False)
    table = pick(table_of)
    codes = (segment_ids * 2 + token_kinds).reshape(count * tensor, rows)
    lie = piece_at.transpose(0, 2, 1).reshape(tensor, -1)
    codes = codes[pick(np.concatenate([lie, seq_piece.reshape(tensor, -1)], axis=1))]
    lie_codes = codes[: count * tensor].reshape(tensor // 2, 1, -1)
    lie_codes = jnp.pad(lie_codes, ((0, 0), (0, 0), (0, -lie_codes.shape[2] % 128)))
    seq_codes = codes[count * tensor :].reshape(count, 1, length)

    weights = (query_weight[0], key_weight[0], value_weight[0])
    biases = jnp.concatenate([query_bias[0], key_bias, value_bias], axis=0).astype(F32)
    expand, contract = expand_weight[0], contract_weight[0]
    expand_bias32 = expand_bias.astype(F32)
    out_proj = output_weight[0]
    Order.mark, Order.weight = None, 0.2

    rounds = piece_rounds(count, tensor)
    perms = [[(u, v) for u, (v, _) in enumerate(chosen)] for chosen in rounds]
    stays = [all(u == v for u, v in perm) for perm in perms]
    sends = np.array([[chosen[u][1] % count for chosen in rounds] for u in range(tensor)], np.int32)
    spots_of = np.zeros((tensor, count), np.int32)
    for number, chosen in enumerate(rounds):
        for v, g in chosen:
            spots_of[v, g // tensor] = number
    spots = pick(spots_of)
    arrived = [
        block if stay else lax.ppermute(block, "tensor", perm)
        for block, stay, perm in zip(
            take(cotangent.reshape(count, rows, d), pick(sends), [BF16] * count, (lie_codes, seq_codes, biases)),
            stays, perms, strict=True,
        )
    ]
    held = {0: tokens}
    for bit in range(1, tensor.bit_length() - 1):
        for j in sorted(held):
            held[j | 1 << bit] = swap(held[j], "tensor", tensor, 1 << bit)
    near = project_rows([tokens, swap(tokens, "tensor", tensor, 1)], lie_codes, weights, biases, count)
    for j in range(2, tensor, 2):
        held[j] = relay([held[j]])[0]
        held[j | 1] = swap(held[j], "tensor", tensor, 1)
    pieces = project_rows([held[j] for j in range(2, tensor)], lie_codes, weights, biases, count, near)
    qkv, x_pieces = (a.reshape(count * tensor, rows, -1) for a in pieces)

    hold = {"cotangents": collect(arrived)}

    def run_attend(s):
        hold["context", s], hold["lse", s], *partial = attend(qkv, table, s, seq_codes, out_proj, tensor, rows)
        return partial

    def finish_attend(s):
        y, hold["n1", s], hold["rstd1", s] = inner_norm(
            hold["addends", s], x_pieces, table, s, output_bias, inner_gain, inner_shift, tensor
        )
        hold["y", s] = gather_start(y, tensor)

    def run_forward(s):
        out = feed_forward(hold["y", s], expand, expand_bias32, contract, hold.get("kept"), s, count)
        hold["kept"] = out[:3]
        return out[3:]

    def finish_forward(s):
        hold["results"], hold["dz", s], dzb, hold["outer", s] = outer_norm(
            hold["addends", s], hold["n1", s], inner_gain, inner_shift, contract_bias, outer_gain, outer_shift,
            hold["cotangents"], spots, hold.get("results"), s, count,
        )
        hold["dzb", s] = gather_start(dzb, tensor)

    def run_back(s):
        out = feed_back(hold["dzb", s], expand, contract, hold["kept"][2], hold.get("back"), s, count)
        hold["expand_bias", s], hold["back"] = out[0], out[1:3]
        return out[3:]

    def finish_back(s):
        drb, hold["inner", s] = inner_norm_back(
            hold["addends", s], hold["dz", s], hold["n1", s], hold["rstd1", s], inner_gain
        )
        hold["drb", s] = gather_start(drb, tensor)

    shapes = [(4, d, width), (1, d, width), (1, d, width), (1, d, width + 128), (1, d, hidden), (1, hidden, d)]
    grads = {}
    flat = lambda a: a.reshape(-1, a.shape[-1])
    bits = list(range(dp.bit_length() - 1))
    swapped = bits[1::-1] + bits[2:]
    orders = {name: swapped if name in SWAPPED else bits for name in "ceab"}

    def sum_over_dp(name, halves, order, layout):
        sums[name] = DpSum([(halves, order, layout)], dp, grads, shapes, name)

    sums = {}

    stages = [(run_attend, finish_attend, "y"), (run_forward, finish_forward, "dzb"), (run_back, finish_back, "drb")]
    runs = [(*one, s) for one in stages for s in range(count)]
    finished, complete = set(), set()

    def finish(i):
        if i not in finished:
            finished.add(i)
            runs[i][1](runs[i][3])

    def bring(i):
        if i not in complete:
            finish(i)
            complete.add(i)
            key = runs[i][2], runs[i][3]
            hold[key] = gather_end(hold[key], tensor)

    for i, (run, _, _, s) in enumerate(runs):
        if i >= count:
            bring(i - count)
        send, *keeps = run(s)
        received = swap(send, "tensor", tensor, 1)
        if i >= 2:
            bring(i - 2)
        if i >= 1:
            finish(i - 1)
        hold["addends", s] = scatter_rest(keeps, received, tensor)
    y_all, du_all = hold["kept"][0], hold["back"][1]

    def steps(names):
        for name in names:
            one = sums[{"c": "contract", "e": "expand", "a": "first", "b": "second"}[name]]
            if one.at < one.steps:
                one.step()

    returns, lands = np.zeros((tensor, count), np.int32), np.zeros((tensor, count), np.int32)
    for number, chosen in enumerate(rounds):
        for u, (v, g) in enumerate(chosen):
            returns[v, number], lands[u, number] = g // tensor, g % count

    kept, output_sum = None, None
    x_flat = flat(x_pieces)
    runs_back = list(range(count))
    for token in AFTER:
        name, _, weight = token.partition(":")
        Order.weight = float(weight or 0.2)
        if name == "attend":
            s = runs_back.pop(0)
            bring(2 * count + s)
            *kept, output_sum, hold["bias", s] = attend_back(
                qkv, table, s, seq_codes, out_proj, hold["context", s], hold["lse", s], hold["drb", s], kept,
                output_sum, count,
            )
            first, second, dr_pieces = kept
        elif name in ("near1", "near2"):
            bring(2 * count + int(name[-1]))
        elif name == "norm":
            finish(3 * count - 1)
        elif name == "norms":
            norms = norm_sums([hold["outer", s] for s in range(count)], [hold["inner", s] for s in range(count)])
            came = swap(norms, "tensor", tensor, 1)
        elif name == "add":
            for bit in range(1, tensor.bit_length() - 1):
                norms = add(norms, came)
                came = swap(norms, "tensor", tensor, 1 << bit)
        elif name == "Gc":
            halves = weight_grad(flat(hold["kept"][1]), flat(hold["back"][0]), orders["c"][0], "contract_grad")
            sum_over_dp("contract", halves, orders["c"], [(5, (0, 1), 0, d, 0)])
        elif name == "Ge":
            halves = weight_grad(flat(y_all), flat(du_all), orders["e"][0], "expand_grad")
            sum_over_dp("expand", halves, orders["e"], [(4, (0, 1), 0, hidden, 0)])
        elif name == "Ga":
            halves = weight_grad(x_flat, flat(first), orders["a"][0], "first_grad")
            sum_over_dp("first", halves, orders["a"], [(0, (0, 4), 0, width, 0)])
        elif name == "Gb":
            sums_of = lambda key: [hold[key, s] for s in range(count)]
            more = pack(output_sum, norms, came, sums_of("expand_bias"), sums_of("bias"))
            halves = weight_grad(x_flat, flat(second), orders["b"][0], "second_grad", more)
            layout = [(1, (0, 1), 0, width, 0), (2, (0, 1), width, width, 0), (3, (0, 1), 2 * width, width + 128, 0)]
            sum_over_dp("second", halves, orders["b"], layout)
        elif name == "in":
            send, *keeps = input_back(first, second, weights, tensor, count)
        elif name == "send":
            received = swap(again(send), "tensor", tensor, 1)
        elif name == "sum":
            addends = scatter_rest(keeps, received, tensor)
        elif name == "end":
            upstream = final_sum(addends, dr_pieces, tensor, count)
        elif name == "take":
            blocks = take(hold["results"], pick(returns), [F32 if stay else BF16 for stay in stays])
            blocks = [
                block if stay else lax.ppermute(block, "tensor", [(v, u) for u, v in perm])
                for block, stay, perm in zip(blocks, stays, perms, strict=True)
            ]
        elif name == "put":
            hold["result"] = put(blocks, pick(lands))
        else:
            steps(name)
    Order.weight = 0.2
    for one in sums.values():
        while one.at < one.steps:
            one.step()

    output_grad, small = across(grads[3], width)
    return (
        hold["result"],
        upstream,
        grads[0][None],
        small[None, 7:11, :width],
        grads[1],
        small[11:12, :width],
        grads[2],
        small[12:13, :width],
        output_grad,
        small[3:4],
        small[4:5],
        small[5:6],
        grads[4],
        small[6:7, :hidden],
        grads[5],
        small[0:1],
        small[1:2],
        small[2:3],
    )


def solution(mesh):
    rows, both = P("dp", None), P(("dp", "tensor"), None)
    columns = lambda dims: P(*[None] * (dims - 1), "tensor")
    down = P(None, "tensor", None)
    weight_specs = [columns(4), columns(3), columns(3), columns(2), columns(3), columns(2), down]
    ffn_specs = [columns(3), columns(2), down]
    return jax.shard_map(
        functools.partial(body, mesh.shape["dp"], mesh.shape["tensor"]),
        mesh=mesh,
        in_specs=(both, rows, rows, both, *weight_specs, P(), P(), P(), *ffn_specs, P(), P(), P()),
        out_specs=(both, both, *weight_specs, P(), P(), P(), *ffn_specs, P(), P(), P()),
        check_vma=False,
    )
```

```python
import functools

import jax
import jax.numpy as jnp
import numpy as np
from jax import lax
from jax.experimental import pallas as pl
from jax.experimental.pallas import tpu as pltpu
from jax.sharding import PartitionSpec as P

HD = 64
NORM_EPS = 1e-05
MASKED = -1e30
F32 = jnp.float32
BF16 = jnp.bfloat16
SMALL, LARGE = 6, 22
COST = 1.15e9
SWAPPED = "ea"
AFTER = (
    "Ge:2.5", "Gc:0.02", "near1", "attend:1", "norm:5", "norms:1", "attend:1", "c:0.02", "e:0.02", "near2:5", "take:2.5", "add:2.5", "attend:1", "Ga",
    "c:0.02", "e:2.5", "Gb", "in:1", "e:0.02", "c:2.5", "a:2.5", "b", "e:2.5", "a:0.02", "send:0.5", "c:2.5", "b:0.5", "put:0.02", "a:1", "b:1", "e:0.5", "c:0.02", "a:9", "b:0.02", "sum:1", "a:0.5", "e:1", "c:0.5", "b:0.5", "a:1", "end:0.5", "b:9",
)


def nn(a, b):
    return lax.dot_general(a, b, (((1,), (0,)), ((), ())), preferred_element_type=F32)


def nt(a, b):
    return lax.dot_general(a, b, (((1,), (1,)), ((), ())), preferred_element_type=F32)


def tn(a, b):
    return lax.dot_general(a, b, (((0,), (0,)), ((), ())), preferred_element_type=F32)


class Order:
    mark = None
    weight = 0.2


def call(body, name, *, grid=(1,), prefetch=(), ins, outs, aliases=None, scratch=(), weight=None, vmem=SMALL):
    def spec(block, index_map):
        if block is None:
            return pl.BlockSpec(memory_space=pl.ANY)
        return pl.BlockSpec(block, index_map, pipeline_mode=pl.Buffered(1) if grid == (1,) else None)

    shift = len(prefetch)
    marks = [] if Order.mark is None else [Order.mark]
    n_in, n_out = shift + len(ins), len(outs)

    def inner(*refs):
        given, rest = refs[:n_in], refs[n_in + len(marks) :]
        body(*given, *rest[:n_out], *rest[n_out + 1 :])

    in_specs = [spec(block, index_map) for _, block, index_map in ins]
    in_specs += [pl.BlockSpec(memory_space=pl.ANY) for _ in marks]
    out_specs = [spec(block, index_map) for _, _, block, index_map in outs]
    out_specs.append(pl.BlockSpec(memory_space=pl.ANY))
    shapes = [jax.ShapeDtypeStruct(shape, dtype) for shape, dtype, _, _ in outs]
    *results, Order.mark = pl.pallas_call(
        inner,
        grid_spec=pltpu.PrefetchScalarGridSpec(
            num_scalar_prefetch=shift,
            grid=grid,
            in_specs=in_specs,
            out_specs=out_specs,
            scratch_shapes=list(scratch),
        ),
        out_shape=[*shapes, jax.ShapeDtypeStruct((8, 128), F32)],
        input_output_aliases={shift + k: v for k, v in (aliases or {}).items()},
        compiler_params=pltpu.CompilerParams(vmem_limit_bytes=vmem * 1024 * 1024),
        cost_estimate=pl.CostEstimate(flops=int((Order.weight if weight is None else weight) * COST), bytes_accessed=1, transcendentals=0),
        name=name,
    )(*prefetch, *[array for array, _, _ in ins], *marks)
    return results


def whole(array):
    zeros = (0,) * array.ndim
    return (array, array.shape, lambda *_: zeros)


def out_whole(shape, dtype):
    zeros = (0,) * len(shape)
    return (shape, dtype, shape, lambda *_: zeros)


def swap(array, axis, size, bit):
    return lax.ppermute(array, axis, [(r, r ^ bit) for r in range(size)])


def gather_start(own, size):
    blocks = {0: own}
    bit = 2
    while bit < size:
        for j in sorted(blocks):
            blocks[j | bit] = swap(blocks[j], "tensor", size, bit)
        bit *= 2
    return blocks


def gather_end(blocks, size):
    even = relay([blocks[j] for j in range(0, size, 2)])
    odd = swap(even, "tensor", size, 1)
    return [((odd if j & 1 else even), j // 2) for j in range(size)]


def block_specs(blocks):
    return [
        (a, (1, *a.shape[1:]), functools.partial(lambda at, *_: (at, 0, 0), at)) for a, at in blocks
    ]


def combine(keep, received, m):
    rows, d = keep.shape

    def body(k_ref, r_ref, o_ref):
        o_ref[...] = (k_ref[...].astype(F32) + r_ref[0].astype(F32)).astype(BF16)

    ins = [whole(keep), (received, (1, rows, d), lambda *_: (m, 0, 0))]
    return call(body, "combine", ins=ins, outs=[out_whole((rows, d), BF16)])[0]


def scatter_rest(keeps, received, size):
    addends = [keeps[0][None], received]
    held = {2 * m: combine(keeps[m], received, m) for m in range(1, len(keeps))}
    bit = size // 2
    while bit >= 2:
        leaving = sorted(j for j in held if j & bit)
        arrived = [swap(held.pop(j), "tensor", size, bit) for j in leaving]
        addends.append(arrived[0][None])
        for j, block in zip(leaving[1:], arrived[1:], strict=True):
            held[j ^ bit] = combine(held[j ^ bit], block[None], 0)
        bit //= 2
    return addends


def addend_specs(addends):
    return [(a, (1,) + a.shape[1:], lambda *_: (0, 0, 0)) for a in addends]


def place_outs(state, shapes, layout, rows, spot_of, ins):
    outs, aliases = [], {}
    for number, (out, (lead, leads), _, wide, block) in enumerate(layout):
        index_map = functools.partial(lambda lead, block, m, spots: (lead, spot_of(m, spots), block), lead, block)
        outs.append((shapes[out], F32, (leads, rows, wide), index_map))
        if out in state:
            aliases[len(ins)] = number
            ins.append((state[out], None, None))
    return outs, aliases


def place_values(values, layout, out_refs):
    for (_, (_, leads), start, wide, _), out_ref in zip(layout, out_refs, strict=True):
        for lead in range(leads):
            at = start + lead * wide
            out_ref[lead] = values[:, at : at + wide].astype(F32)


class DpSum:
    def __init__(self, entries, size, state, shapes, name):
        self.size, self.name, self.state, self.shapes = size, name, state, shapes
        self.at = 0
        self.orders = [order for _, order, _ in entries]
        self.layouts = [layout for _, _, layout in entries]
        self.bits = len(entries[0][1])
        self.steps = 2 * self.bits
        here = lax.axis_index("dp")
        self.mine = [[(here >> bit) & 1 for bit in order] for order in self.orders]
        self.held = [0]
        self.staying = [halves[0] for halves, _, _ in entries]
        self.send([halves[1] for halves, _, _ in entries], 0)

    def scalars(self, values):
        return jnp.stack([jnp.asarray(v, jnp.int32) for v in values])

    def send(self, blocks, level):
        self.arrived = [
            swap(block, "dp", self.size, 1 << order[level]) for block, order in zip(blocks, self.orders, strict=True)
        ]

    def where(self, m, differs):
        spot = 0
        for level, mine in enumerate(self.mine[m]):
            spot = spot * 2 + (mine ^ ((differs >> level) & 1))
        return spot

    def step(self):
        if self.at < self.bits:
            self.halve()
        else:
            self.join()
        self.at += 1

    def placing(self, ins, rows, spot_of):
        outs, aliases = [], {}
        for m, layout in enumerate(self.layouts):
            index_of = functools.partial(spot_of, m)
            more, taken = place_outs(self.state, self.shapes, layout, rows[m], index_of, ins)
            aliases.update({k: v + len(outs) for k, v in taken.items()})
            outs += more
        return outs, aliases

    def keep_placed(self, got):
        names = [entry[0] for layout in self.layouts for entry in layout]
        self.state.update(dict(zip(names, got, strict=True)))

    def halve(self):
        level = self.at
        last = level == self.bits - 1
        n = len(self.staying)
        shapes = [a.shape for a in self.arrived]
        ends = np.cumsum([0] + [len(layout) for layout in self.layouts])

        def body(scalars_ref, *refs):
            outs = refs[2 * n :]
            for m in range(n):
                stay_ref, came_ref = refs[2 * m : 2 * m + 2]
                if last:
                    total = (stay_ref[...].astype(F32) + came_ref[...].astype(F32)).astype(BF16)
                    outs[len(outs) - n + m][...] = total
                    place_values(total, self.layouts[m], outs[len(outs) - n - ends[-1] :][ends[m] : ends[m + 1]])
                    continue
                half = shapes[m][0] // 2
                for out_ref, part in ((outs[2 * m], 1 - scalars_ref[m]), (outs[2 * m + 1], scalars_ref[m])):
                    at = pl.ds(pl.multiple_of(part * half, 16), half)
                    out_ref[...] = (stay_ref[at, :].astype(F32) + came_ref[at, :].astype(F32)).astype(BF16)

        ins = [whole(a) for pair in zip(self.staying, self.arrived, strict=True) for a in pair]
        if last:
            prefetch = self.scalars([self.where(m, 0) for m in range(n)])
            outs, aliases = self.placing(ins, [shape[0] for shape in shapes], lambda m, i, spots: spots[m])
            outs += [out_whole(shape, BF16) for shape in shapes]
        else:
            prefetch = self.scalars([mine[level + 1] for mine in self.mine])
            outs, aliases = [], {}
            for rows, columns in shapes:
                outs += [out_whole((rows // 2, columns), BF16)] * 2
        got = call(
            body, self.name + "_halve", prefetch=(prefetch,), ins=ins, outs=outs, aliases=aliases
        )
        if last:
            self.staying = got[len(got) - n :]
            self.keep_placed(got[: len(got) - n])
            self.send(self.staying, level)
        else:
            self.staying = got[1::2]
            self.send(got[0::2], level + 1)

    def join(self):
        level = self.steps - 1 - self.at
        count = len(self.held)
        came = [differs | (1 << level) for differs in self.held]
        self.held = self.held + came
        n = len(self.arrived)
        spots = self.scalars([self.where(m, differs) for m in range(n) for differs in came])
        rows = [a.shape[0] // count for a in self.arrived]
        ends = np.cumsum([0] + [len(layout) for layout in self.layouts])
        block = lambda i, spots: (i, 0)
        ins = [(a, (r, a.shape[1]), block) for a, r in zip(self.arrived, rows, strict=True)]
        if level:
            ins += [(a, (r, a.shape[1]), block) for a, r in zip(self.staying, rows, strict=True)]

        def body(spots_ref, *refs):
            joined = refs[len(refs) - n :] if level else ()
            placed = refs[len(refs) - len(joined) - ends[-1] : len(refs) - len(joined)]
            for m in range(n):
                values = refs[m][...]
                if level:
                    joined[m][0] = refs[n + m][...]
                    joined[m][1] = values
                place_values(values, self.layouts[m], placed[ends[m] : ends[m + 1]])

        outs, aliases = self.placing(ins, rows, lambda m, i, spots: spots[m * count + i])
        if level:
            for a, r in zip(self.arrived, rows, strict=True):
                outs.append(((2, *a.shape), BF16, (2, r, a.shape[1]), lambda i, spots: (0, i, 0)))
        got = call(
            body, self.name + "_join", grid=(count,), prefetch=(spots,), ins=ins, outs=outs, aliases=aliases
        )
        if level:
            self.staying = [a.reshape(-1, a.shape[2]) for a in got[len(got) - n :]]
            got = got[: len(got) - n]
            self.send(self.staying, level - 1)
        self.keep_placed(got)


def weight_grad(left_side, right_side, bit, name, more=None):
    tokens, total = left_side.shape
    columns = right_side.shape[1]
    half = total // 2

    def body(mine_ref, a_ref, b_ref, *refs):
        stay_ref, leave_ref = refs[-2:]
        product = tn(a_ref[...], b_ref[...]).astype(BF16)
        if more is not None:
            product = jnp.concatenate([product, refs[0][...]], axis=1)
        mine = pl.program_id(0) == mine_ref[0]

        @pl.when(mine)
        def _():
            stay_ref[...] = product

        @pl.when(jnp.logical_not(mine))
        def _():
            leave_ref[...] = product

    ins = [(left_side, (tokens, half), lambda i, mine: (0, i)), whole(right_side)]
    if more is not None:
        ins.append((more, (half, more.shape[1]), lambda i, mine: (i, 0)))
        columns += more.shape[1]
    outs = [out_whole((half, columns), BF16)] * 2
    mine = ((lax.axis_index("dp") >> bit) & 1).reshape(1).astype(jnp.int32)
    return call(body, name, vmem=LARGE, grid=(2,), prefetch=(mine,), ins=ins, outs=outs)


def add(one, two):
    def body(one_ref, two_ref, out_ref):
        out_ref[...] = one_ref[...] + two_ref[...]

    return call(body, "add", ins=[whole(one), whole(two)], outs=[out_whole(one.shape, F32)])[0]


def norm_sums(outer, inner):
    n, shape = len(outer), outer[0].shape

    def body(*refs):
        for at, group in ((0, refs[:n]), (3, refs[n : 2 * n])):
            total = group[0][0:3]
            for r in group[1:]:
                total = total + r[0:3]
            refs[-1][at : at + 3] = total
        refs[-1][6:8] = jnp.zeros((2, shape[1]), F32)

    ins = [whole(a) for a in (*outer, *inner)]
    return call(body, "norm_sums", ins=ins, outs=[out_whole(shape, F32)])[0]


def pack(output_sum, norms, came, expand_bias, bias):
    width, d = output_sum.shape
    hidden = expand_bias[0].shape[1]
    n = len(bias)

    def body(o_ref, norm_ref, came_ref, *refs):
        out_ref, rows_ref = refs[-2:]
        rows_ref[...] = jnp.zeros((128, d), F32)
        rows_ref[0:6] = norm_ref[0:6] + came_ref[0:6]
        total = refs[0][...]
        for r in refs[1:n]:
            total = total + r[...]
        rows_ref[6:7, :hidden] = total
        total = refs[n][0:6]
        for r in refs[n + 1 : 2 * n]:
            total = total + r[0:6]
        rows_ref[7:13, :width] = total
        out_ref[:, :width] = o_ref[...].T.astype(BF16)
        out_ref[:, width:] = rows_ref[...].T.astype(BF16)

    ins = [whole(a) for a in (output_sum, norms, came, *expand_bias, *bias)]
    outs = [out_whole((d, width + 128), BF16)]
    return call(body, "pack", ins=ins, outs=outs, scratch=[pltpu.VMEM((128, d), F32)])[0]


def piece_rounds(count, size):
    left = {}
    for g in range(count * size):
        left.setdefault((g // count, g % size), []).append(g)
    rounds = []
    for _ in range(count):
        match = {}

        def augment(u, seen):
            for v in range(size):
                if left.get((u, v)) and v not in seen:
                    seen.add(v)
                    if v not in match or augment(match[v], seen):
                        match[v] = u
                        return True
            return False

        for bit in range(size):
            if all(left.get((u, u ^ bit)) for u in range(size)):
                match.update({u ^ bit: u for u in range(size)})
                break
        else:
            for u in range(size):
                augment(u, set())
        chosen = {u: (v, left[(u, v)].pop(0)) for v, u in match.items()}
        rounds.append([chosen[u] for u in range(size)])
    return rounds


def erf_parts(u):
    size = jnp.abs(u) * np.float32(0.7071067811865476)
    bell = jnp.exp(-(size * size))
    t = pl.reciprocal(1.0 + np.float32(0.3275911) * size)
    poly = np.float32(1.061405429 * 0.5)
    for c in (-1.453152027, 1.421413741, -0.284496736, 0.254829592):
        poly = poly * t + np.float32(c * 0.5)
    tail = poly * t * bell
    return jnp.where(u < 0, tail, 1.0 - tail), bell * np.float32(0.3989422804014327)


def write_rows(values, out_refs, size, rows):
    for j in range(size):
        block = values[j * rows : (j + 1) * rows].astype(BF16)
        if j & 1:
            out_refs[0][j // 2] = block
        else:
            out_refs[1 + j // 2][...] = block


def partial_outs(size, rows, width):
    return [out_whole((size // 2, rows, width), BF16)] + [out_whole((rows, width), BF16)] * (size // 2)


def column(row, wide):
    one = jnp.broadcast_to(row.astype(F32), (128, row.shape[1])).T
    return one if wide == 128 else jnp.concatenate([one] * (wide // 128), axis=1)


def project_rows(blocks, codes, weights, biases, count, near=()):
    size = len(blocks)
    skip = near[0].shape[1] if near else 0
    rows = blocks[0].shape[0] // count
    d = blocks[0].shape[1]
    width = weights[1].shape[1]
    total = 2 * count * rows

    def body(*refs):
        code_ref, qw_ref, kw_ref, vw_ref, b_ref, *near_refs, out_ref, x_out = refs[size:]
        for near_ref, to in zip(near_refs, (out_ref, x_out)):
            to[:, :skip] = near_ref[...]
        bias = [b_ref[m : m + 1, :] for m in range(6)]
        for at in range(0, size, 2):
            x = jnp.concatenate([refs[at][...], refs[at + 1][...]], axis=0)
            spots = [(m, skip + at + i) for i in range(2) for m in range(count)]
            for number, (m, i) in enumerate(spots):
                x_out[m, i] = x[number * rows : (number + 1) * rows]
            word = column(code_ref[(skip + at) // 2] & 1, width)[:total] == 0.0

            def write(part, values):
                for number, (m, i) in enumerate(spots):
                    out_ref[m, i, :, part * width : (part + 1) * width] = values[number * rows : (number + 1) * rows]

            for part, (first, second) in enumerate(((0, 2), (1, 3))):
                one = nn(x, qw_ref[first]) + bias[first]
                two = nn(x, qw_ref[second]) + bias[second]
                write(part, jnp.where(word, one, two).astype(BF16))
            for part, ref, m in ((2, kw_ref, 4), (3, vw_ref, 5)):
                write(part, (nn(x, ref[...]) + bias[m]).astype(BF16))

    ins = [whole(b) for b in blocks] + [whole(codes)]
    ins += [whole(w) for w in weights] + [whole(biases)] + [whole(a) for a in near]
    outs = [out_whole((count, skip + size, rows, wide), BF16) for wide in (4 * width, d)]
    return call(body, "project_rows", vmem=LARGE, weight=5, ins=ins, outs=outs)


def relay(blocks):
    rows, d = blocks[0].shape
    n = len(blocks)

    def body(*refs):
        for m in range(n):
            refs[-1][m] = refs[m][...]

    return call(body, "relay", ins=[whole(b) for b in blocks], outs=[out_whole((n, rows, d), BF16)])[0]


def again(array):
    def body(in_ref, out_ref):
        out_ref[...] = in_ref[...]

    return call(body, "again", ins=[whole(array)], outs=[out_whole(array.shape, array.dtype)])[0]


def head_views(piece_refs, part, pair, width):
    start = part * width + pair * 128
    return jnp.concatenate([r[0, :, start : start + 128] for r in piece_refs], axis=0)


def swap_lanes(values):
    return pltpu.roll(values.astype(F32), 64, 1)


def extended(piece_refs, pair, width, takes, left):
    qw = head_views(piece_refs, 0, pair, width)
    qe = head_views(piece_refs, 1, pair, width)
    k = head_views(piece_refs, 2, pair, width)
    v = head_views(piece_refs, 3, pair, width)
    qw32, qe32, k32 = qw.astype(F32), qe.astype(F32), k.astype(F32) * 0.125
    qw_s, qe_s, k_s = swap_lanes(qw32), swap_lanes(qe32), swap_lanes(k32)
    q_ext = (
        jnp.where(left, qw32, qe_s).astype(BF16),
        jnp.where(left, qw_s, qe32).astype(BF16),
    )
    k_ext = (
        jnp.where(takes, jnp.where(left, k32, k_s), 0.0).astype(BF16),
        jnp.where(takes, jnp.where(left, k_s, k32), 0.0).astype(BF16),
    )
    return q_ext, k_ext, v


def query_blocks(length):
    spans, at = [], 0
    while at < length:
        step = length
        spans.append((at, step))
        at += step
    return spans


def attend(pieces, table, s, codes, out_proj, size, rows):
    length = size * rows
    width, d = out_proj.shape
    pairs = width // 128

    def body(table_ref, *refs):
        piece_refs = refs[:size]
        code_ref, wo_ref, c_ref, lse_ref = refs[size : size + 4]
        left = lax.broadcasted_iota(jnp.int32, (length, 128), 1) < 64
        code = code_ref[0]
        word = column(code & 1, 128) == 0.0
        takes = word == left
        segr = (code >> 1).astype(F32)
        segc = column(code >> 1, length)
        for pair in range(pairs):
            q_ext, k_ext, v = extended(piece_refs, pair, width, takes, left)
            v_t = v.astype(F32).T.astype(BF16)
            for at, step in query_blocks(length):
                same = segc[:, :step] == segr[:, at : at + step]
                tops = []
                for h in range(2):
                    s_t = nt(k_ext[h], q_ext[h][at : at + step])
                    s_t = jnp.where(same, s_t, MASKED)
                    top = jnp.max(s_t, axis=0, keepdims=True)
                    e = jnp.exp(s_t - top)
                    total = jnp.sum(e, axis=0, keepdims=True)
                    o_t = nn(v_t[h * 64 : h * 64 + 64], e.astype(BF16))
                    tops.append(o_t * (1.0 / total))
                    lse_ref[2 * pair + h : 2 * pair + h + 1, at : at + step] = top + jnp.log(total)
                c = jnp.concatenate(tops, axis=0).T.astype(BF16)
                c_ref[at : at + step, pair * 128 : pair * 128 + 128] = c
        write_rows(nn(c_ref[...], wo_ref[...]), refs[-1 - size // 2 :], size, rows)

    ins = [
        (pieces, (1, rows, 4 * width), functools.partial(lambda j, _, t: (t[s * size + j], 0, 0), j))
        for j in range(size)
    ]
    ins += [
        (codes, (1, 1, length), lambda *_: (s, 0, 0)),
        whole(out_proj),
    ]
    outs = [out_whole((length, width), BF16), out_whole((8, length), F32)]
    outs += partial_outs(size, rows, d)
    return call(
        body, "attend", vmem=LARGE, weight=7, prefetch=(table,), ins=ins, outs=outs,
    )


def attend_back(pieces, table, s, codes, out_proj, context, lse, delta_blocks, buffers, sums, count):
    size = len(delta_blocks)
    rows, d = delta_blocks[0][0].shape[1:]
    length = size * rows
    width = out_proj.shape[0]
    pairs = width // 128

    def body(table_ref, *refs):
        piece_refs = refs[:size]
        delta_refs = refs[size : 2 * size]
        code_ref, wo_ref, c_ref, lse_ref = refs[2 * size : 2 * size + 4]
        n_out = 5
        tail = refs[2 * size + 4 :]
        sum_in = tail[0] if sums is not None else None
        first_out, second_out, delta_out, wo_grad, bias_out, first_all, second_all = tail[-(n_out + 2) :]
        step_at = pl.program_id(0)

        @pl.when(step_at == 0)
        def _():
            left = lax.broadcasted_iota(jnp.int32, (length, 128), 1) < 64
            code = code_ref[0]
            word = column(code & 1, 128) == 0.0
            takes = word == left
            segr = (code >> 1).astype(F32)
            segc = column(code >> 1, length)
            delta = jnp.concatenate([r[0] for r in delta_refs], axis=0)
            c_all = c_ref[...]
            grad = nn(c_all.astype(F32).T.astype(BF16), delta)
            wo_grad[...] = grad if sum_in is None else grad + sum_in[...]
            for pair in range(pairs):
                dc = nt(delta, wo_ref[pair * 128 : pair * 128 + 128, :]).astype(BF16)
                q_ext, k_ext, v = extended(piece_refs, pair, width, takes, left)
                k_ext_t = [k.astype(F32).T.astype(BF16) for k in k_ext]
                dc32 = dc.astype(F32)
                dc_h = (jnp.where(left, dc32, 0.0).astype(BF16), jnp.where(left, 0.0, dc32).astype(BF16))
                dv = jnp.zeros((length, 128), F32)
                dk = [jnp.zeros((length, 128), F32)] * 2
                dq = [[], []]
                for at, step in query_blocks(length):
                    same = segc[:, :step] == segr[:, at : at + step]
                    for h in range(2):
                        q_b, dc_b = q_ext[h][at : at + step], dc_h[h][at : at + step]
                        row = 2 * pair + h
                        s_t = nt(k_ext[h], q_b)
                        p = jnp.where(same, jnp.exp(s_t - lse_ref[row : row + 1, at : at + step]), 0.0)
                        dp = nt(v, dc_b)
                        row_inner = jnp.sum(p * dp, axis=0, keepdims=True)
                        ds = (p * (dp - row_inner)).astype(BF16)
                        dv = dv + nn(p.astype(BF16), dc_b)
                        dk[h] = dk[h] + nn(ds, q_b)
                        dq[h].append(nn(k_ext_t[h], ds).T)
                dq0, dq1 = (jnp.concatenate(parts, axis=0) for parts in dq)
                dqw = jnp.where(left, dq0, swap_lanes(dq1))
                dqe = jnp.where(left, swap_lanes(dq0), dq1)
                dk0, dk1 = dk[0] * 0.125, dk[1] * 0.125
                dk_pair = jnp.where(takes, jnp.where(left, dk0, dk1), jnp.where(left, swap_lanes(dk0), swap_lanes(dk1)))
                outs = (
                    jnp.where(word, dqw, 0.0), jnp.where(word, dqe, 0.0), jnp.where(word, 0.0, dqw),
                    jnp.where(word, 0.0, dqe), dk_pair, dv,
                )
                for number, values in enumerate(outs):
                    rounded = values.astype(BF16)
                    target = (first_all, second_all)[number // 4]
                    start = (number % 4) * width + pair * 128
                    target[:, start : start + 128] = rounded
                    bias_out[number : number + 1, pair * 128 : pair * 128 + 128] = jnp.sum(
                        rounded.astype(F32), axis=0, keepdims=True
                    )

        at_rows = pl.ds(pl.multiple_of(step_at * rows, 16), rows)
        first_out[0] = first_all[at_rows, :]
        second_out[0] = second_all[at_rows, :]
        for j in range(size):

            @pl.when(step_at == j)
            def _():
                delta_out[0] = delta_refs[j][0]

    ins = [
        (pieces, (1, rows, 4 * width), functools.partial(lambda j, _, t: (t[s * size + j], 0, 0), j))
        for j in range(size)
    ]
    ins += block_specs(delta_blocks)
    ins += [
        (codes, (1, 1, length), lambda *_: (s, 0, 0)),
        whole(out_proj),
        whole(context),
        whole(lse),
    ]
    if sums is not None:
        ins.append(whole(sums))
    aliases = {}
    if buffers is not None:
        for number, b in enumerate(buffers):
            aliases[len(ins)] = number
            ins.append((b, None, None))
    spot = lambda m, t: (t[s * size + m], 0, 0)
    outs = [
        ((count * size, rows, 4 * width), BF16, (1, rows, 4 * width), spot),
        ((count * size, rows, 2 * width), BF16, (1, rows, 2 * width), spot),
        ((count * size, rows, d), BF16, (1, rows, d), spot),
        out_whole((width, d), F32),
        out_whole((8, width), F32),
    ]
    return call(
        body, "attend_back", vmem=LARGE, grid=(size,), prefetch=(table,), ins=ins, outs=outs, aliases=aliases,
        scratch=[pltpu.VMEM((length, 4 * width), BF16), pltpu.VMEM((length, 2 * width), BF16)],
    )


def add_up(refs):
    total = refs[0][0].astype(F32)
    for r in refs[1:]:
        total = total + r[0].astype(F32)
    return total


def normed(values):
    centre = jnp.mean(values, axis=-1, keepdims=True)
    offset = values - centre
    spread = jnp.mean(offset * offset, axis=-1, keepdims=True)
    rstd = lax.rsqrt(spread + NORM_EPS)
    return offset * rstd, rstd


def norm_pull(upstream, n, rstd, gain):
    scaled = upstream * gain
    inner = jnp.mean(scaled, axis=-1, keepdims=True)
    cross = jnp.mean(scaled * n, axis=-1, keepdims=True)
    return rstd * (scaled - inner - n * cross)


def column_sum(values):
    return jnp.sum(values, axis=0, keepdims=True)


def inner_norm(addends, x_pieces, table, s, bias, gain, shift, size):
    rows, d = addends[0].shape[1:]
    n_add = len(addends)

    def body(table_ref, *refs):
        x_ref, b_ref, g_ref, h_ref, y_ref, n_ref, rstd_ref = refs[n_add:]
        r = add_up(refs[:n_add]) + b_ref[...] + x_ref[0].astype(F32)
        n, rstd = normed(r)
        n_ref[...] = n
        rstd_ref[...] = jnp.broadcast_to(rstd, (rows, 128))
        y_ref[...] = (n * g_ref[...] + h_ref[...]).astype(BF16)

    ins = addend_specs(addends)
    ins.append((x_pieces, (1, rows, d), lambda _, t: (t[s * size], 0, 0)))
    ins += [whole(bias), whole(gain), whole(shift)]
    outs = [out_whole((rows, d), BF16), out_whole((rows, d), F32), out_whole((rows, 128), F32)]
    return call(body, "inner_norm", weight=5, prefetch=(table,), ins=ins, outs=outs)


def outer_norm(addends, n1, inner_gain, inner_shift, bias, gain, shift, cotangents, spots, buffer, s, count):
    rows, d = addends[0].shape[1:]
    n_add = len(addends)

    def body(spots_ref, *refs):
        n1_ref, g1_ref, h1_ref, b_ref, g_ref, h_ref, e_ref = refs[n_add : n_add + 7]
        res_ref, dz_ref, dzb_ref, sums_ref = refs[-4:]
        z = add_up(refs[:n_add]) + b_ref[...] + (n1_ref[...] * g1_ref[...] + h1_ref[...])
        n, rstd = normed(z)
        res_ref[0] = n * g_ref[...] + h_ref[...]
        e = e_ref[0].astype(F32)
        dz = norm_pull(e, n, rstd, g_ref[...])
        dz_ref[...] = dz
        dzb_ref[...] = dz.astype(BF16)
        sums_ref[0:1] = column_sum(dz)
        sums_ref[1:2] = column_sum(e * n)
        sums_ref[2:3] = column_sum(e)

    ins = addend_specs(addends)
    ins += [whole(a) for a in (n1, inner_gain, inner_shift, bias, gain, shift)]
    ins.append((cotangents, (1, rows, d), lambda _, t: (t[s], 0, 0)))
    aliases = {}
    if buffer is not None:
        aliases[len(ins)] = 0
        ins.append((buffer, None, None))
    outs = [
        ((count, rows, d), F32, (1, rows, d), lambda *_: (s, 0, 0)),
        out_whole((rows, d), F32),
        out_whole((rows, d), BF16),
        out_whole((8, d), F32),
    ]
    return call(
        body, "outer_norm", weight=5, prefetch=(spots,), ins=ins, outs=outs, aliases=aliases,
    )


def inner_norm_back(addends, dz, n1, rstd1, gain):
    rows, d = addends[0].shape[1:]
    n_add = len(addends)

    def body(*refs):
        dz_ref, n_ref, rstd_ref, g_ref, dr_ref, sums_ref = refs[n_add:]
        da = add_up(refs[:n_add]) + dz_ref[...]
        n = n_ref[...]
        dr = norm_pull(da, n, rstd_ref[:, 0:1], g_ref[...])
        dr_ref[...] = dr.astype(BF16)
        sums_ref[0:1] = column_sum(dr)
        sums_ref[1:2] = column_sum(da * n)
        sums_ref[2:3] = column_sum(da)

    ins = addend_specs(addends) + [whole(a) for a in (dz, n1, rstd1, gain)]
    outs = [out_whole((rows, d), BF16), out_whole((8, d), F32)]
    return call(body, "inner_norm_back", weight=5, ins=ins, outs=outs)


def feed_forward(blocks, expand, expand_bias, contract, buffers, s, count):
    size = len(blocks)
    rows, d = blocks[0][0].shape[1:]
    hidden = expand.shape[1]
    length = size * rows
    tile = min(256, hidden)

    def body(*refs):
        y_refs = refs[:size]
        we_ref, be_ref, wc_ref = refs[size : size + 3]
        n_partial = 1 + size // 2
        y_out, g_out, slope_out = refs[-3 - n_partial : -n_partial]
        y = jnp.concatenate([r[0] for r in y_refs], axis=0)
        y_out[0] = y
        for at in range(0, hidden, tile):
            cols = slice(at, at + tile)
            u = nn(y, we_ref[:, cols]) + be_ref[:, cols]
            phi_sum, phi = erf_parts(u)
            g_out[0, :, cols] = (u * phi_sum).astype(BF16)
            slope_out[0, :, cols] = (phi_sum + u * phi).astype(BF16)
        write_rows(nn(g_out[0], wc_ref[...]), refs[-n_partial:], size, rows)

    ins = block_specs(blocks) + [whole(a) for a in (expand, expand_bias, contract)]
    aliases = {}
    if buffers is not None:
        for number, b in enumerate(buffers):
            aliases[len(ins)] = number
            ins.append((b, None, None))
    outs = [
        ((count, length, w), BF16, (1, length, w), lambda *_: (s, 0, 0)) for w in (d, hidden, hidden)
    ] + partial_outs(size, rows, d)
    return call(
        body, "feed_forward", vmem=LARGE, weight=7, ins=ins, outs=outs, aliases=aliases,
    )


def feed_back(blocks, expand, contract, slopes, buffers, s, count):
    size = len(blocks)
    rows, d = blocks[0][0].shape[1:]
    hidden = expand.shape[1]
    length = size * rows
    tile = min(256, hidden)

    def body(*refs):
        dz_refs = refs[:size]
        we_ref, wc_ref, slope_ref = refs[size : size + 3]
        n_partial = 1 + size // 2
        sums_ref, dz_out, du_out = refs[-3 - n_partial : -n_partial]
        dz = jnp.concatenate([r[0] for r in dz_refs], axis=0)
        dz_out[0] = dz
        for at in range(0, hidden, tile):
            cols = slice(at, at + tile)
            du = (nt(dz, wc_ref[cols, :]) * slope_ref[0, :, cols].astype(F32)).astype(BF16)
            du_out[0, :, cols] = du
            sums_ref[:, cols] = column_sum(du.astype(F32))
        write_rows(nt(du_out[0], we_ref[...]), refs[-n_partial:], size, rows)

    ins = block_specs(blocks) + [whole(expand), whole(contract)]
    ins.append((slopes, (1, length, hidden), lambda *_: (s, 0, 0)))
    aliases = {}
    if buffers is not None:
        for number, b in enumerate(buffers):
            aliases[len(ins)] = 1 + number
            ins.append((b, None, None))
    outs = [out_whole((1, hidden), F32)]
    outs += [((count, length, w), BF16, (1, length, w), lambda *_: (s, 0, 0)) for w in (d, hidden)]
    outs += partial_outs(size, rows, d)
    return call(
        body, "feed_back", vmem=LARGE, weight=6, ins=ins, outs=outs, aliases=aliases,
    )


def input_back(first, second, weights, size, count):
    rows = first.shape[1]
    d = weights[1].shape[0]
    width = weights[1].shape[1]

    def body(*refs):
        a_ref, b_ref, qw_ref, kw_ref, vw_ref = refs[:5]
        a = jnp.concatenate([a_ref[j] for j in range(size)], axis=0)
        b = jnp.concatenate([b_ref[j] for j in range(size)], axis=0)
        total = nt(a[:, :width], qw_ref[0])
        for m in (1, 2, 3):
            total = total + nt(a[:, m * width : (m + 1) * width], qw_ref[m])
        total = total + nt(b[:, :width], kw_ref[...])
        total = total + nt(b[:, width:], vw_ref[...])
        write_rows(total, refs[5:], size, rows)

    ins = [(a, (size, rows, a.shape[2]), lambda k: (k, 0, 0)) for a in (first, second)]
    ins += [whole(w) for w in weights]
    outs = [((size // 2, count * rows, d), BF16, (size // 2, rows, d), lambda k: (0, k, 0))]
    outs += [((count * rows, d), BF16, (rows, d), lambda k: (k, 0)) for _ in range(size // 2)]
    return call(body, "input_back", vmem=LARGE, grid=(count,), ins=ins, outs=outs)


def take(array, spots, dtypes, ready=()):
    rows, d = array.shape[1:]

    def body(spots_ref, in_ref, *out_refs):
        for m, out_ref in enumerate(out_refs[len(ready) :]):
            out_ref[...] = in_ref[spots_ref[m]].astype(out_ref.dtype)

    ins = [whole(array)] + [(a, None, None) for a in ready]
    outs = [out_whole((rows, d), dtype) for dtype in dtypes]
    return call(body, "take", prefetch=(spots,), ins=ins, outs=outs)


def put(blocks, spots):
    rows, d = blocks[0].shape
    n = len(blocks)

    def body(spots_ref, *refs):
        for m in range(n):
            refs[-1][pl.ds(pl.multiple_of(spots_ref[m] * rows, 16), rows), :] = refs[m][...].astype(F32)

    ins = [whole(b) for b in blocks]
    return call(body, "put", prefetch=(spots,), ins=ins, outs=[out_whole((n * rows, d), F32)])[0]


def collect(blocks):
    rows, d = blocks[0].shape

    def body(*refs):
        for m in range(len(blocks)):
            refs[-1][m] = refs[m][...]

    outs = [out_whole((len(blocks), rows, d), BF16)]
    return call(body, "collect", ins=[whole(b) for b in blocks], outs=outs)[0]


def final_sum(addends, dr_pieces, size, count):
    rows, d = dr_pieces.shape[1:]

    def body(*refs):
        refs[-1][...] = add_up(refs[:-1])

    ins = [(a, (1, rows, d), lambda k: (0, k, 0)) for a in addends]
    ins.append((dr_pieces, (1, rows, d), lambda k: (k * size, 0, 0)))
    outs = [((count * rows, d), F32, (rows, d), lambda k: (k, 0))]
    return call(body, "final_sum", grid=(count,), ins=ins, outs=outs)[0]


def across(array, rows):
    d, n = array.shape[1:]

    def body(in_ref, one_ref, two_ref):
        turned = in_ref[0].T
        one_ref[0] = turned[:rows]
        two_ref[...] = turned[rows:]

    outs = [out_whole((1, rows, d), F32), out_whole((n - rows, d), F32)]
    return call(body, "across", ins=[whole(array)], outs=outs)


def body(
    dp, tensor, tokens, token_kinds, segment_ids, cotangent, query_weight, query_bias, key_weight, key_bias,
    value_weight, value_bias, output_weight, output_bias, inner_gain, inner_shift, expand_weight, expand_bias,
    contract_weight, contract_bias, outer_gain, outer_shift,
):
    count, length = token_kinds.shape
    d = tokens.shape[1]
    rows = length // tensor
    me = lax.axis_index("tensor")
    width = key_weight.shape[2]
    hidden = expand_weight.shape[2]

    devices = np.arange(tensor)
    piece_at = np.array(
        [[[o * count + k for o in devices ^ r] for k in range(count)] for r in range(tensor)], np.int32
    )
    seq_piece = np.array(
        [[[s * tensor + b for b in devices ^ r] for s in range(count)] for r in range(tensor)], np.int32
    )
    table_of = np.array(
        [[(g % count) * tensor + ((g // count) ^ r) for g in seq_piece[r].reshape(-1)] for r in range(tensor)], np.int32
    )
    pick = lambda values: lax.dynamic_index_in_dim(jnp.asarray(values), me, 0, keepdims=False)
    table = pick(table_of)
    codes = (segment_ids * 2 + token_kinds).reshape(count * tensor, rows)
    lie = piece_at.transpose(0, 2, 1).reshape(tensor, -1)
    codes = codes[pick(np.concatenate([lie, seq_piece.reshape(tensor, -1)], axis=1))]
    lie_codes = codes[: count * tensor].reshape(tensor // 2, 1, -1)
    lie_codes = jnp.pad(lie_codes, ((0, 0), (0, 0), (0, -lie_codes.shape[2] % 128)))
    seq_codes = codes[count * tensor :].reshape(count, 1, length)

    weights = (query_weight[0], key_weight[0], value_weight[0])
    biases = jnp.concatenate([query_bias[0], key_bias, value_bias], axis=0).astype(F32)
    expand, contract = expand_weight[0], contract_weight[0]
    expand_bias32 = expand_bias.astype(F32)
    out_proj = output_weight[0]
    Order.mark, Order.weight = None, 0.2

    rounds = piece_rounds(count, tensor)
    perms = [[(u, v) for u, (v, _) in enumerate(chosen)] for chosen in rounds]
    stays = [all(u == v for u, v in perm) for perm in perms]
    sends = np.array([[chosen[u][1] % count for chosen in rounds] for u in range(tensor)], np.int32)
    spots_of = np.zeros((tensor, count), np.int32)
    for number, chosen in enumerate(rounds):
        for v, g in chosen:
            spots_of[v, g // tensor] = number
    spots = pick(spots_of)
    arrived = [
        block if stay else lax.ppermute(block, "tensor", perm)
        for block, stay, perm in zip(
            take(cotangent.reshape(count, rows, d), pick(sends), [BF16] * count, (lie_codes, seq_codes, biases)),
            stays, perms, strict=True,
        )
    ]
    held = {0: tokens}
    for bit in range(1, tensor.bit_length() - 1):
        for j in sorted(held):
            held[j | 1 << bit] = swap(held[j], "tensor", tensor, 1 << bit)
    near = project_rows([tokens, swap(tokens, "tensor", tensor, 1)], lie_codes, weights, biases, count)
    for j in range(2, tensor, 2):
        held[j] = relay([held[j]])[0]
        held[j | 1] = swap(held[j], "tensor", tensor, 1)
    pieces = project_rows([held[j] for j in range(2, tensor)], lie_codes, weights, biases, count, near)
    qkv, x_pieces = (a.reshape(count * tensor, rows, -1) for a in pieces)

    hold = {"cotangents": collect(arrived)}

    def run_attend(s):
        hold["context", s], hold["lse", s], *partial = attend(qkv, table, s, seq_codes, out_proj, tensor, rows)
        return partial

    def finish_attend(s):
        y, hold["n1", s], hold["rstd1", s] = inner_norm(
            hold["addends", s], x_pieces, table, s, output_bias, inner_gain, inner_shift, tensor
        )
        hold["y", s] = gather_start(y, tensor)

    def run_forward(s):
        out = feed_forward(hold["y", s], expand, expand_bias32, contract, hold.get("kept"), s, count)
        hold["kept"] = out[:3]
        return out[3:]

    def finish_forward(s):
        hold["results"], hold["dz", s], dzb, hold["outer", s] = outer_norm(
            hold["addends", s], hold["n1", s], inner_gain, inner_shift, contract_bias, outer_gain, outer_shift,
            hold["cotangents"], spots, hold.get("results"), s, count,
        )
        hold["dzb", s] = gather_start(dzb, tensor)

    def run_back(s):
        out = feed_back(hold["dzb", s], expand, contract, hold["kept"][2], hold.get("back"), s, count)
        hold["expand_bias", s], hold["back"] = out[0], out[1:3]
        return out[3:]

    def finish_back(s):
        drb, hold["inner", s] = inner_norm_back(
            hold["addends", s], hold["dz", s], hold["n1", s], hold["rstd1", s], inner_gain
        )
        hold["drb", s] = gather_start(drb, tensor)

    shapes = [(4, d, width), (1, d, width), (1, d, width), (1, d, width + 128), (1, d, hidden), (1, hidden, d)]
    grads = {}
    flat = lambda a: a.reshape(-1, a.shape[-1])
    bits = list(range(dp.bit_length() - 1))
    swapped = bits[1::-1] + bits[2:]
    orders = {name: swapped if name in SWAPPED else bits for name in "ceab"}

    def sum_over_dp(name, halves, order, layout):
        sums[name] = DpSum([(halves, order, layout)], dp, grads, shapes, name)

    sums = {}

    stages = [(run_attend, finish_attend, "y"), (run_forward, finish_forward, "dzb"), (run_back, finish_back, "drb")]
    runs = [(*one, s) for one in stages for s in range(count)]
    finished, complete = set(), set()

    def finish(i):
        if i not in finished:
            finished.add(i)
            runs[i][1](runs[i][3])

    def bring(i):
        if i not in complete:
            finish(i)
            complete.add(i)
            key = runs[i][2], runs[i][3]
            hold[key] = gather_end(hold[key], tensor)

    for i, (run, _, _, s) in enumerate(runs):
        if i >= count:
            bring(i - count)
        send, *keeps = run(s)
        received = swap(send, "tensor", tensor, 1)
        if i >= 2:
            bring(i - 2)
        if i >= 1:
            finish(i - 1)
        hold["addends", s] = scatter_rest(keeps, received, tensor)
    y_all, du_all = hold["kept"][0], hold["back"][1]

    def steps(names):
        for name in names:
            one = sums[{"c": "contract", "e": "expand", "a": "first", "b": "second"}[name]]
            if one.at < one.steps:
                one.step()

    returns, lands = np.zeros((tensor, count), np.int32), np.zeros((tensor, count), np.int32)
    for number, chosen in enumerate(rounds):
        for u, (v, g) in enumerate(chosen):
            returns[v, number], lands[u, number] = g // tensor, g % count

    kept, output_sum = None, None
    x_flat = flat(x_pieces)
    runs_back = list(range(count))
    for token in AFTER:
        name, _, weight = token.partition(":")
        Order.weight = float(weight or 0.2)
        if name == "attend":
            s = runs_back.pop(0)
            bring(2 * count + s)
            *kept, output_sum, hold["bias", s] = attend_back(
                qkv, table, s, seq_codes, out_proj, hold["context", s], hold["lse", s], hold["drb", s], kept,
                output_sum, count,
            )
            first, second, dr_pieces = kept
        elif name in ("near1", "near2"):
            bring(2 * count + int(name[-1]))
        elif name == "norm":
            finish(3 * count - 1)
        elif name == "norms":
            norms = norm_sums([hold["outer", s] for s in range(count)], [hold["inner", s] for s in range(count)])
            came = swap(norms, "tensor", tensor, 1)
        elif name == "add":
            for bit in range(1, tensor.bit_length() - 1):
                norms = add(norms, came)
                came = swap(norms, "tensor", tensor, 1 << bit)
        elif name == "Gc":
            halves = weight_grad(flat(hold["kept"][1]), flat(hold["back"][0]), orders["c"][0], "contract_grad")
            sum_over_dp("contract", halves, orders["c"], [(5, (0, 1), 0, d, 0)])
        elif name == "Ge":
            halves = weight_grad(flat(y_all), flat(du_all), orders["e"][0], "expand_grad")
            sum_over_dp("expand", halves, orders["e"], [(4, (0, 1), 0, hidden, 0)])
        elif name == "Ga":
            halves = weight_grad(x_flat, flat(first), orders["a"][0], "first_grad")
            sum_over_dp("first", halves, orders["a"], [(0, (0, 4), 0, width, 0)])
        elif name == "Gb":
            sums_of = lambda key: [hold[key, s] for s in range(count)]
            more = pack(output_sum, norms, came, sums_of("expand_bias"), sums_of("bias"))
            halves = weight_grad(x_flat, flat(second), orders["b"][0], "second_grad", more)
            layout = [(1, (0, 1), 0, width, 0), (2, (0, 1), width, width, 0), (3, (0, 1), 2 * width, width + 128, 0)]
            sum_over_dp("second", halves, orders["b"], layout)
        elif name == "in":
            send, *keeps = input_back(first, second, weights, tensor, count)
        elif name == "send":
            received = swap(again(send), "tensor", tensor, 1)
        elif name == "sum":
            addends = scatter_rest(keeps, received, tensor)
        elif name == "end":
            upstream = final_sum(addends, dr_pieces, tensor, count)
        elif name == "take":
            blocks = take(hold["results"], pick(returns), [F32 if stay else BF16 for stay in stays])
            blocks = [
                block if stay else lax.ppermute(block, "tensor", [(v, u) for u, v in perm])
                for block, stay, perm in zip(blocks, stays, perms, strict=True)
            ]
        elif name == "put":
            hold["result"] = put(blocks, pick(lands))
        else:
            steps(name)
    Order.weight = 0.2
    for one in sums.values():
        while one.at < one.steps:
            one.step()

    output_grad, small = across(grads[3], width)
    return (
        hold["result"],
        upstream,
        grads[0][None],
        small[None, 7:11, :width],
        grads[1],
        small[11:12, :width],
        grads[2],
        small[12:13, :width],
        output_grad,
        small[3:4],
        small[4:5],
        small[5:6],
        grads[4],
        small[6:7, :hidden],
        grads[5],
        small[0:1],
        small[1:2],
        small[2:3],
    )


def solution(mesh):
    rows, both = P("dp", None), P(("dp", "tensor"), None)
    columns = lambda dims: P(*[None] * (dims - 1), "tensor")
    down = P(None, "tensor", None)
    weight_specs = [columns(4), columns(3), columns(3), columns(2), columns(3), columns(2), down]
    ffn_specs = [columns(3), columns(2), down]
    return jax.shard_map(
        functools.partial(body, mesh.shape["dp"], mesh.shape["tensor"]),
        mesh=mesh,
        in_specs=(both, rows, rows, both, *weight_specs, P(), P(), P(), *ffn_specs, P(), P(), P()),
        out_specs=(both, both, *weight_specs, P(), P(), P(), *ffn_specs, P(), P(), P()),
        check_vma=False,
    )
```
